512 devices in a mesh: rows: 128 (over y, z, core), tilt: 4 (over x).
Axes of the slice: x: 4, y: 8, z: 8, core: 2. Of those that a mesh axis runs over, the one named last changes fastest.
Arguments:
- start: float32 [32, 2621440], P('tilt', 'rows'), may hold values from -6 to 6
- reward: float32 [2621440], P('rows'), may hold values from -1 to 1
- theta: float32 [32], P('tilt'), may hold values from -1 to 1
- kernels: bfloat16 [4, 512, 512], replicated, may hold values from -0.25 to 0.25
- rates: bfloat16 [5120, 12, 512], P('rows'), may hold values from 0.1 to 12, as said below
- pattern: int32 [5120, 12], P('rows'), may hold values from 0 to 5119, as said below
Outputs:
- iterate: float32 [32, 2621440], P('tilt', 'rows')
- growth: float32 [2, 32], P(None, 'tilt')
The draws below stay inside these ranges and needn't reach their ends.
Inputs may be any that keep to these rules, and one draw needn't show every extreme that they name: `pattern`: entries 0 to 7 of block row i lie within 20 blocks of i, counted cyclically modulo 5120. Among the far entries (8 onward) of the 40 block rows of one index of rows, the blocks of any one index of rows are named exactly 2 times or not at all. Positive rates.
All inputs are finite; a program needn't handle non-finite values.
Results may differ from the reference program's by a relative error of at most 0.0033.
Values may be sent and summed in bfloat16 or wider, within the bound.
No kernel may reach another device: no remote copies, remote signals or barrier semaphores. Data moves between devices by JAX's collectives and lax.ppermute only.
A program may use at most 64 MiB of HBM per device.

```python
import math
import jax
import jax.numpy as jnp
from jax import lax

BS = 512
SLOTS = 12
NEAR = 8
KINDS = 4
TILTS = 32
ITERS = 2
NB_DEV = 40
FAR = 4
CAP = 2
BLOCKS = 5120
STATES = 2621440
N_ROWS = 128


def draw_start(key, part):
    key = jax.random.fold_in(key, 37)
    noise_key, common_key = jax.random.split(key, 2)
    noise = jax.random.normal(noise_key, (TILTS, N_ROWS, NB_DEV, BS), jnp.float32)
    common = jnp.clip(jax.random.normal(common_key, (TILTS, 1, 1, BS), jnp.float32), -2.2, 2.2)
    parity = (jnp.arange(N_ROWS, dtype=jnp.int32) % 2 == 0)[None, :, None, None]
    drawn = jnp.where(parity, noise + 2.0 * common, noise * math.sqrt(5.0))
    return jnp.clip(drawn, -6.0, 6.0).reshape(TILTS, STATES)


def draw_pattern(key, part):
    key = jax.random.fold_in(key, 11)
    near_key, perm_key, local_key = jax.random.split(key, 3)
    half_span = NB_DEV // 2
    row_ids = jnp.arange(BLOCKS, dtype=jnp.int32)
    shifts = jax.random.randint(near_key, (BLOCKS, NEAR), -half_span, half_span + 1)
    near_cols = (row_ids[:, None] + shifts) % BLOCKS

    def draw_order(device_id):
        return jax.random.permutation(jax.random.fold_in(perm_key, device_id), N_ROWS)
    orders = jax.vmap(draw_order)(jnp.arange(N_ROWS, dtype=jnp.int32))
    sources_used = NB_DEV * FAR // CAP
    request_ids = jnp.arange(NB_DEV * FAR, dtype=jnp.int32) % sources_used
    owners = orders[:, request_ids].reshape(BLOCKS, FAR)
    within = jax.random.randint(local_key, (BLOCKS, FAR), 0, NB_DEV)
    far_cols = owners * NB_DEV + within
    return jnp.concatenate([near_cols, far_cols], axis=1).astype(jnp.int32)


def draw_rates(key, part):
    key = jax.random.fold_in(key, 23)
    level_key = jax.random.fold_in(key, 0)
    position = jnp.arange(BLOCKS, dtype=jnp.float32) / max(BLOCKS - 1, 1)
    rising = jnp.exp(math.log(3.0) * position)[:, None, None]
    levels = jax.random.uniform(level_key, (BLOCKS, SLOTS, BS), jnp.float32, math.log(0.1), 0.0)
    drawn = jnp.exp(levels) * rising
    return drawn.astype(jnp.bfloat16)


def level_of(rng, extent, cuts, least, largest):
    def one(dim, shards_of):
        steps = jax.random.uniform(jax.random.fold_in(jax.random.fold_in(rng, 6), dim), (shards_of,), jnp.float32, least / len(cuts), largest / len(cuts))
        return jnp.repeat(jnp.exp(steps), extent[dim] // shards_of).reshape((-1,) + (1,) * (len(extent) - dim - 1))

    factor_of = one(*cuts[0])
    for cut in cuts[1:]:
        factor_of = factor_of * one(*cut)
    return factor_of


def bell_draw(rng, extent, deviation, reach, kind=jnp.bfloat16):
    result = deviation * jax.random.normal(rng, extent, jnp.float32)
    return jnp.clip(result, min=-reach, max=reach).astype(kind)


def setup_inputs(seed: int = 0) -> dict:
    key_list = jax.random.split(jax.random.key(seed), 7)
    start = draw_start(jax.random.fold_in(key_list[6], 71), 0)
    reward = jnp.clip(jax.random.uniform(key_list[1], (STATES,), jnp.float32, -1.0, 1.0) * level_of(key_list[1], (STATES,), ((0, 128),), -0.4, 0.0), -1.0, 1.0)
    theta = jnp.clip(jax.random.uniform(key_list[2], (TILTS,), jnp.float32, -1.0, 1.0) * level_of(key_list[2], (TILTS,), ((0, 4),), -0.4, 0.0), -1.0, 1.0)
    kernels = bell_draw(key_list[3], (KINDS, BS, BS), BS ** -0.5, 0.25)
    rates = draw_rates(jax.random.fold_in(key_list[6], 71), 0)
    pattern = draw_pattern(jax.random.fold_in(key_list[6], 71), 0)
    return {"start": start, "reward": reward, "theta": theta, "kernels": kernels, "rates": rates, "pattern": pattern}


group_rows = 64

def apply_blocks(tilted, kernels, rates, pattern):
    group_count = pattern.shape[0] // group_rows
    pattern_groups = pattern.reshape(group_count, group_rows, SLOTS)
    rate_groups = rates.reshape(group_count, group_rows, SLOTS // KINDS, KINDS, BS)
    kernel_full = kernels.astype(jnp.float32)

    def one_group(pieces):
        pattern_part, rate_part = pieces
        columns = jnp.take(tilted, pattern_part.reshape(-1), axis=0).astype(jnp.float32)
        columns = columns.reshape(group_rows, SLOTS // KINDS, KINDS, TILTS, BS)
        summed = jnp.zeros((group_rows, TILTS, BS), jnp.float32)
        for kind_index in range(KINDS):
            kernel_out = jnp.einsum('gmtb,ba->gmta', columns[:, :, kind_index], kernel_full[kind_index])
            weights = rate_part[:, :, kind_index, None, :].astype(jnp.float32)
            summed = summed + lax.optimization_barrier(jnp.sum(kernel_out * weights, axis=1))
        return summed
    mapped_all = lax.map(one_group, (pattern_groups, rate_groups))
    return mapped_all.reshape(-1, TILTS, BS)

def reference(start, reward, theta, kernels, rates, pattern):
    factor = jnp.exp(theta[:, None] * reward[None, :])
    iterate = start
    growth = []
    for iteration in range(ITERS):
        tilted = (factor * iterate).astype(jnp.bfloat16)
        tilted = tilted.reshape(TILTS, BLOCKS, BS).transpose(1, 0, 2)
        mapped = apply_blocks(tilted, kernels, rates, pattern)
        mapped = mapped.transpose(1, 0, 2).reshape(TILTS, STATES)
        norm_scale = jnp.sqrt(lax.optimization_barrier(jnp.mean(mapped * mapped, axis=1)) + 1e-06)
        iterate = mapped / norm_scale[:, None]
        growth.append(jnp.log(norm_scale))
    return (iterate, jnp.stack(growth))
```

```python
import jax
import jax.numpy as jnp
from jax import lax
from jax.sharding import PartitionSpec as P

NEAR = 8
ITERS = 2


def on_device(start, reward, theta, kernels, rates, pattern):
    tilt_count = start.shape[0]
    blocks_here, slot_count = pattern.shape
    kind_count, block_size = kernels.shape[0], kernels.shape[1]
    peer_count = lax.axis_size("rows")
    position = lax.axis_index("rows")
    total_blocks = blocks_here * peer_count
    far_count = slot_count - NEAR
    half_span = blocks_here // 2
    capacity = max(2, blocks_here * far_count // peer_count)
    local_rows = jnp.arange(blocks_here, dtype=jnp.int32)
    global_rows = position * blocks_here + local_rows
    shifts = (pattern[:, :NEAR] - global_rows[:, None] + half_span) % total_blocks - half_span
    near_index = local_rows[:, None] + shifts + half_span

    far_cols = pattern[:, NEAR:].reshape(-1)
    owners = far_cols // blocks_here
    within = far_cols % blocks_here
    order_ids = jnp.arange(far_cols.shape[0], dtype=jnp.int32)
    earlier = order_ids[None, :] < order_ids[:, None]
    slot_rank = jnp.sum((owners[:, None] == owners[None, :]) & earlier, axis=1)
    peers = jnp.arange(peer_count, dtype=jnp.int32)
    places = jnp.arange(capacity, dtype=jnp.int32)
    asks = (owners[:, None, None] == peers[None, :, None]) & (
        slot_rank[:, None, None] == places[None, None, :]
    )
    requests = jnp.sum(jnp.where(asks, within[:, None, None], 0), axis=0)
    asked_blocks = lax.all_to_all(requests, "rows", split_axis=0, concat_axis=0, tiled=True)
    far_index = (owners * capacity + slot_rank).reshape(blocks_here, far_count)

    up = [(i, (i + 1) % peer_count) for i in range(peer_count)]
    down = [(j, i) for i, j in up]
    rate_split = rates.astype(jnp.float32)
    factor = jnp.exp(theta[None, :, None] * reward.reshape(blocks_here, 1, block_size))

    def apply(columns, rate_part):
        groups = columns.shape[1] // kind_count
        columns = columns.reshape(blocks_here, groups, kind_count, tilt_count, block_size)
        rate_part = rate_part.reshape(blocks_here, groups, kind_count, 1, block_size)
        summed = 0.0
        for kind in range(kind_count):
            out = jnp.einsum(
                "lmtb,ba->lmta",
                columns[:, :, kind],
                kernels[kind],
                preferred_element_type=jnp.float32,
            )
            summed = summed + jnp.sum(out * rate_part[:, :, kind], axis=1)
        return summed

    mapped = start.reshape(tilt_count, blocks_here, block_size).transpose(1, 0, 2)
    squares = []
    for _ in range(ITERS):
        tilted = (factor * mapped).astype(jnp.bfloat16)
        before = lax.ppermute(tilted[blocks_here - half_span :], "rows", up)
        after = lax.ppermute(tilted[:half_span], "rows", down)
        outgoing = tilted[asked_blocks.reshape(-1)]
        arrived = lax.all_to_all(outgoing, "rows", split_axis=0, concat_axis=0, tiled=True)
        extended = jnp.concatenate([before, tilted, after], axis=0)
        near_sum = apply(extended[near_index], rate_split[:, :NEAR])
        far_sum = apply(arrived[far_index], rate_split[:, NEAR:])
        mapped = near_sum + far_sum
        squares.append(jnp.sum(mapped * mapped, axis=(0, 2)))

    partial = jnp.concatenate(squares)
    spread = jnp.broadcast_to(partial, (peer_count, partial.shape[0]))
    gathered = lax.all_to_all(spread, "rows", split_axis=0, concat_axis=0, tiled=True)
    totals = jnp.sum(gathered, axis=0).reshape(ITERS, tilt_count)
    states = total_blocks * block_size
    product = jnp.ones((tilt_count,), jnp.float32)
    growth = []
    for j in range(ITERS):
        scale = jnp.sqrt(totals[j] / product / product / states + 1e-06)
        product = product * scale
        growth.append(jnp.log(scale))
    iterate = mapped / product[None, :, None]
    return (iterate.transpose(1, 0, 2).reshape(tilt_count, -1), jnp.stack(growth))


def solution(mesh):
    placed = (P("tilt", "rows"), P("rows"), P("tilt"), P(), P("rows", None, None), P("rows", None))
    return jax.shard_map(
        on_device,
        mesh=mesh,
        in_specs=placed,
        out_specs=(P("tilt", "rows"), P(None, "tilt")),
        check_vma=False,
    )
```

```python
import functools

import jax
import jax.numpy as jnp
from jax import lax
from jax.experimental import pallas as pl
from jax.experimental.pallas import tpu as pltpu
from jax.sharding import PartitionSpec as P

NEAR = 8
ITERS = 2
VMEM_LIMIT = 48 * 1024 * 1024


def pack_blocks(asked, tilted, out):
    def body(j, carry):
        out[j] = tilted[asked[j]]
        return carry

    lax.fori_loop(0, out.shape[0], body, 0, unroll=8)


def mapped_sum(index, source, kernels, rates, gathered, slots, first):
    kinds, size = kernels.shape[0], kernels.shape[1]
    rows = rates.shape[1]
    tilts = source.shape[1]
    total = None
    for slot in range(slots):

        def gather(pair, carry, slot=slot):
            low = source[index[2 * pair * slots + slot]]
            high = source[index[(2 * pair + 1) * slots + slot]]
            both = jnp.concatenate([low, high], axis=0)
            gathered[pl.ds(pl.multiple_of(pair * 2 * tilts, 2 * tilts), 2 * tilts), :] = both
            return carry

        lax.fori_loop(0, rows // 2, gather, 0, unroll=True)
        product = jnp.dot(
            gathered[...], kernels[slot % kinds], preferred_element_type=jnp.float32
        ).reshape(rows, tilts, size)
        term = product * rates[first + slot][:, None, :]
        total = term if total is None else total + term
    return total


def near_kernel(index, extended, kernels, rates, out, gathered):
    out[...] = mapped_sum(index, extended, kernels, rates, gathered, NEAR, 0)


def far_kernel(index, asked, arrived, kernels, rates, near, factor, tilted, outgoing, squares, gathered):
    slots = rates.shape[0] - NEAR
    total = mapped_sum(index, arrived, kernels, rates, gathered, slots, NEAR) + near[...]
    squares[...] = jnp.sum(total * total, axis=0)
    tilted[...] = (factor[...] * total).astype(jnp.bfloat16)
    pack_blocks(asked, tilted, outgoing)


def last_kernel(index, arrived, kernels, rates, near, mapped, squares, gathered):
    slots = rates.shape[0] - NEAR
    total = mapped_sum(index, arrived, kernels, rates, gathered, slots, NEAR) + near[...]
    squares[...] = jnp.sum(total * total, axis=0)
    for row in range(total.shape[0]):
        mapped[:, row * total.shape[2] : (row + 1) * total.shape[2]] = total[row]


def call(kernel, out_shape, scalars, arrays, scratch, flops):
    moved = sum(a.size * a.dtype.itemsize for a in (*arrays, *jax.tree.leaves(out_shape)))
    return pl.pallas_call(
        kernel,
        out_shape=out_shape,
        in_specs=[pl.BlockSpec(memory_space=pltpu.SMEM)] * len(scalars)
        + [pl.BlockSpec(memory_space=pltpu.VMEM)] * len(arrays),
        out_specs=jax.tree.map(lambda _: pl.BlockSpec(memory_space=pltpu.VMEM), out_shape),
        scratch_shapes=scratch,
        compiler_params=pltpu.CompilerParams(vmem_limit_bytes=VMEM_LIMIT),
        cost_estimate=pl.CostEstimate(flops=flops, bytes_accessed=moved, transcendentals=0),
    )(*scalars, *arrays)


def on_device(start, reward, theta, kernels, rates, pattern):
    tilt_count = start.shape[0]
    blocks_here, slot_count = pattern.shape
    block_size = kernels.shape[1]
    peer_count = lax.axis_size("rows")
    position = lax.axis_index("rows")
    total_blocks = blocks_here * peer_count
    far_count = slot_count - NEAR
    half_span = blocks_here // 2
    capacity = max(2, blocks_here * far_count // peer_count)

    far_cols = pattern[:, NEAR:].reshape(-1)
    owners = far_cols // blocks_here
    within = far_cols % blocks_here
    order_ids = jnp.arange(far_cols.shape[0], dtype=jnp.int32)
    earlier = order_ids[None, :] < order_ids[:, None]
    slot_rank = jnp.sum((owners[:, None] == owners[None, :]) & earlier, axis=1)
    peers = jnp.arange(peer_count, dtype=jnp.int32)
    places = jnp.arange(capacity, dtype=jnp.int32)
    asks = (owners[:, None, None] == peers[None, :, None]) & (
        slot_rank[:, None, None] == places[None, None, :]
    )
    requests = jnp.sum(jnp.where(asks, within[:, None, None], 0), axis=0)
    asked = lax.all_to_all(requests, "rows", split_axis=0, concat_axis=0, tiled=True).reshape(-1)
    far_index = owners * capacity + slot_rank

    local_rows = jnp.arange(blocks_here, dtype=jnp.int32)
    global_rows = position * blocks_here + local_rows
    shifts = (pattern[:, :NEAR] - global_rows[:, None] + half_span) % total_blocks - half_span
    near_index = (local_rows[:, None] + shifts + half_span).reshape(-1)

    up = [(i, (i + 1) % peer_count) for i in range(peer_count)]
    down = [(j, i) for i, j in up]
    rate_full = rates.transpose(1, 0, 2).astype(jnp.float32)
    factor = jnp.exp(theta[None, :, None] * reward.reshape(blocks_here, 1, block_size))

    block = (tilt_count, block_size)
    arrived_blocks = peer_count * capacity
    scratch = [pltpu.VMEM((blocks_here * tilt_count, block_size), jnp.bfloat16)]
    product_flops = 2 * blocks_here * tilt_count * block_size * block_size
    own_shape = jax.ShapeDtypeStruct((blocks_here, *block), jnp.float32)
    tilted_shape = jax.ShapeDtypeStruct((blocks_here, *block), jnp.bfloat16)
    outgoing_shape = jax.ShapeDtypeStruct((arrived_blocks, *block), jnp.bfloat16)
    squares_shape = jax.ShapeDtypeStruct(block, jnp.float32)
    mapped_shape = jax.ShapeDtypeStruct(start.shape, jnp.float32)

    tilted = factor * start.reshape(tilt_count, blocks_here, block_size).transpose(1, 0, 2)
    tilted = tilted.astype(jnp.bfloat16)
    squares = []
    for iteration in range(ITERS):
        before = lax.ppermute(tilted[blocks_here - half_span :], "rows", up)
        after = lax.ppermute(tilted[:half_span], "rows", down)
        if iteration == 0:
            before, after, asked = lax.optimization_barrier((before, after, asked))
            outgoing = call(pack_blocks, outgoing_shape, [asked], [tilted], [], 0)
        else:
            before, after, outgoing = lax.optimization_barrier((before, after, outgoing))
        arrived = lax.all_to_all(outgoing, "rows", split_axis=0, concat_axis=0, tiled=True)
        extended = jnp.concatenate([before, tilted, after], axis=0)
        near = call(
            near_kernel, own_shape, [near_index], [extended, kernels, rate_full], scratch, NEAR * product_flops
        )
        if iteration < ITERS - 1:
            tilted, outgoing, square = call(
                far_kernel,
                (tilted_shape, outgoing_shape, squares_shape),
                [far_index, asked],
                [arrived, kernels, rate_full, near, factor],
                scratch,
                far_count * product_flops,
            )
        else:
            mapped, square = call(
                last_kernel,
                (mapped_shape, squares_shape),
                [far_index],
                [arrived, kernels, rate_full, near],
                scratch,
                far_count * product_flops,
            )
        squares.append(jnp.sum(square, axis=1))

    partial = jnp.concatenate(squares)
    spread = jnp.broadcast_to(partial, (peer_count, partial.shape[0]))
    gathered = lax.all_to_all(spread, "rows", split_axis=0, concat_axis=0, tiled=True)
    totals = jnp.sum(gathered, axis=0).reshape(ITERS, tilt_count)
    states = total_blocks * block_size
    product = jnp.ones((tilt_count,), jnp.float32)
    growth = []
    for j in range(ITERS):
        scale = jnp.sqrt(totals[j] / product / product / states + 1e-06)
        product = product * scale
        growth.append(jnp.log(scale))
    return (mapped / product[:, None], jnp.stack(growth))


def solution(mesh):
    placed = (P("tilt", "rows"), P("rows"), P("tilt"), P(), P("rows", None, None), P("rows", None))
    return jax.shard_map(
        on_device,
        mesh=mesh,
        in_specs=placed,
        out_specs=(P("tilt", "rows"), P(None, "tilt")),
        check_vma=False,
    )
```

```python
import jax
import jax.numpy as jnp
from jax import lax
from jax.experimental import pallas as pl
from jax.experimental.pallas import tpu as pltpu
from jax.sharding import PartitionSpec as P

NEAR = 8
ITERS = 2
PACK_CHUNKS = 8
VMEM_LIMIT = 40 * 1024 * 1024


def pack_blocks(asked, tilted, staged, outgoing, sems):
    chunk = outgoing.shape[0] // PACK_CHUNKS
    copies = []
    for part in range(PACK_CHUNKS):

        def body(j, carry, part=part):
            staged[part * chunk + j] = tilted[asked[part * chunk + j]]
            return carry

        lax.fori_loop(0, chunk, body, 0, unroll=8)
        span = pl.ds(part * chunk, chunk)
        copies.append(pltpu.make_async_copy(staged.at[span], outgoing.at[span], sems.at[part]))
        copies[-1].start()
    for copy in copies:
        copy.wait()


def pack_kernel(asked, tilted, outgoing, staged, sems):
    pack_blocks(asked, tilted, staged, outgoing, sems)


def weighted(index, stride, slots, source, weights, rates, gathered):
    rows, size = rates.shape[1], rates.shape[2]
    tilts = source.shape[1]
    span = rows * tilts
    for n, slot in enumerate(slots):

        def gather(pair, carry, slot=slot, n=n):
            low = source[index[2 * pair * stride + slot]]
            high = source[index[(2 * pair + 1) * stride + slot]]
            at = pl.multiple_of(n * span + pair * 2 * tilts, 2 * tilts)
            gathered[pl.ds(at, 2 * tilts), :] = jnp.concatenate([low, high], axis=0)
            return carry

        lax.fori_loop(0, rows // 2, gather, 0, unroll=True)
    taken = gathered[: len(slots) * span, :]
    product = jnp.dot(taken, weights, preferred_element_type=jnp.float32)
    return product.reshape(len(slots), rows, tilts, size)


def map_blocks(near_index, far_index, before, own, after, arrived, kernels, rates, scratch):
    extended, far_blocks, weights, rate_buf, gathered, sems = scratch
    kinds = kernels.shape[0]
    rows, half = own.shape[0], before.shape[0]
    slot_count = rates.shape[0]
    far_count = slot_count - NEAR

    def fetch(src, dst, sem):
        copy = pltpu.make_async_copy(src, dst, sems.at[sem])
        copy.start()
        return copy

    pieces = [
        fetch(before, extended.at[pl.ds(0, half)], 0),
        fetch(own, extended.at[pl.ds(half, rows)], 1),
        fetch(after, extended.at[pl.ds(half + rows, half)], 2),
    ]
    kernel_copies = [fetch(kernels.at[0], weights.at[0], 3)]
    rate_copy = fetch(rates, rate_buf, 3 + kinds)
    kernel_copies += [fetch(kernels.at[k], weights.at[k], 3 + k) for k in range(1, kinds)]
    far_copy = fetch(arrived, far_blocks, 4 + kinds)
    for piece in pieces:
        piece.wait()

    total = None
    for kind in range(kinds):
        slots = range(kind, NEAR, kinds)
        kernel_copies[kind].wait()
        if kind == 0:
            rate_copy.wait()
        product = weighted(near_index, NEAR, slots, extended, weights[kind], rate_buf, gathered.at[kind % 2])
        for n, slot in enumerate(slots):
            term = product[n] * rate_buf[slot].astype(jnp.float32)[:, None, :]
            total = term if total is None else total + term
    far_copy.wait()
    for kind in range(kinds):
        slots = range(kind, far_count, kinds)
        product = weighted(far_index, far_count, slots, far_blocks, weights[kind], rate_buf, gathered.at[kind % 2])
        for n, slot in enumerate(slots):
            total = total + product[n] * rate_buf[NEAR + slot].astype(jnp.float32)[:, None, :]
    return total


def step_kernel(
    near_index, far_index, asked, before, own, after, arrived, kernels, rates, factor,
    tilted, outgoing, squares, staged, pack_sems, *scratch,
):
    total = map_blocks(near_index, far_index, before, own, after, arrived, kernels, rates, scratch)
    squares[...] = jnp.sum(total * total, axis=0)
    tilted[...] = (factor[...] * total).astype(jnp.bfloat16)
    pack_blocks(asked, tilted, staged, outgoing, pack_sems)


def last_kernel(
    near_index, far_index, before, own, after, arrived, kernels, rates, mapped, squares, *scratch
):
    total = map_blocks(near_index, far_index, before, own, after, arrived, kernels, rates, scratch)
    squares[...] = jnp.sum(total * total, axis=0)
    for row in range(total.shape[0]):
        mapped[:, row * total.shape[2] : (row + 1) * total.shape[2]] = total[row]


def call(kernel, outs, scalars, arrays, scratch, flops):
    place = {True: pl.BlockSpec(memory_space=pl.ANY), False: pl.BlockSpec(memory_space=pltpu.VMEM)}
    moved = sum(a.size * a.dtype.itemsize for a, _ in (*arrays, *outs))
    return pl.pallas_call(
        kernel,
        out_shape=[shape for shape, _ in outs],
        in_specs=[pl.BlockSpec(memory_space=pltpu.SMEM)] * len(scalars) + [place[far] for _, far in arrays],
        out_specs=[place[far] for _, far in outs],
        scratch_shapes=scratch,
        compiler_params=pltpu.CompilerParams(vmem_limit_bytes=VMEM_LIMIT),
        cost_estimate=pl.CostEstimate(flops=flops, bytes_accessed=moved, transcendentals=0),
    )(*scalars, *[array for array, _ in arrays])


def on_device(start, reward, theta, kernels, rates, pattern):
    tilt_count = start.shape[0]
    blocks_here, slot_count = pattern.shape
    block_size = kernels.shape[1]
    peer_count = lax.axis_size("rows")
    position = lax.axis_index("rows")
    total_blocks = blocks_here * peer_count
    far_count = slot_count - NEAR
    half_span = blocks_here // 2
    capacity = max(2, blocks_here * far_count // peer_count)

    far_cols = pattern[:, NEAR:].reshape(-1)
    owners = far_cols // blocks_here
    within = far_cols % blocks_here
    order_ids = jnp.arange(far_cols.shape[0], dtype=jnp.int32)
    earlier = order_ids[None, :] < order_ids[:, None]
    slot_rank = jnp.sum((owners[:, None] == owners[None, :]) & earlier, axis=1)
    peers = jnp.arange(peer_count, dtype=jnp.int32)
    places = jnp.arange(capacity, dtype=jnp.int32)
    asks = (owners[:, None, None] == peers[None, :, None]) & (
        slot_rank[:, None, None] == places[None, None, :]
    )
    requests = jnp.sum(jnp.where(asks, within[:, None, None], 0), axis=0)
    asked = lax.all_to_all(requests, "rows", split_axis=0, concat_axis=0, tiled=True).reshape(-1)
    far_index = owners * capacity + slot_rank

    local_rows = jnp.arange(blocks_here, dtype=jnp.int32)
    global_rows = position * blocks_here + local_rows
    shifts = (pattern[:, :NEAR] - global_rows[:, None] + half_span) % total_blocks - half_span
    near_index = (local_rows[:, None] + shifts + half_span).reshape(-1)

    up = [(i, (i + 1) % peer_count) for i in range(peer_count)]
    down = [(j, i) for i, j in up]
    rates_by_slot = rates.transpose(1, 0, 2)
    factor = jnp.exp(theta[None, :, None] * reward.reshape(blocks_here, 1, block_size))

    block = (tilt_count, block_size)
    arrived_blocks = peer_count * capacity
    tilted_shape = jax.ShapeDtypeStruct((blocks_here, *block), jnp.bfloat16)
    outgoing_shape = jax.ShapeDtypeStruct((arrived_blocks, *block), jnp.bfloat16)
    squares_shape = jax.ShapeDtypeStruct(block, jnp.float32)
    mapped_shape = jax.ShapeDtypeStruct(start.shape, jnp.float32)
    staging = [pltpu.VMEM(outgoing_shape.shape, jnp.bfloat16), pltpu.SemaphoreType.DMA((PACK_CHUNKS,))]
    kind_count = kernels.shape[0]
    gather_rows = max(NEAR, far_count) // kind_count * blocks_here * tilt_count
    scratch = [
        pltpu.VMEM((blocks_here + 2 * half_span, *block), jnp.bfloat16),
        pltpu.VMEM(outgoing_shape.shape, jnp.bfloat16),
        pltpu.VMEM(kernels.shape, jnp.bfloat16),
        pltpu.VMEM(rates_by_slot.shape, jnp.bfloat16),
        pltpu.VMEM((2, gather_rows, block_size), jnp.bfloat16),
        pltpu.SemaphoreType.DMA((5 + kind_count,)),
    ]
    map_flops = 2 * slot_count * blocks_here * tilt_count * block_size * block_size

    tilted = factor * start.reshape(tilt_count, blocks_here, block_size).transpose(1, 0, 2)
    tilted = tilted.astype(jnp.bfloat16)
    (outgoing,) = call(pack_kernel, [(outgoing_shape, True)], [asked], [(tilted, False)], staging, 0)
    squares = []
    for iteration in range(ITERS):
        arrived = lax.all_to_all(outgoing, "rows", split_axis=0, concat_axis=0, tiled=True)
        before = lax.ppermute(tilted[blocks_here - half_span :], "rows", up)
        after = lax.ppermute(tilted[:half_span], "rows", down)
        pieces = [(a, True) for a in (before, tilted, after, arrived, kernels, rates_by_slot)]
        if iteration < ITERS - 1:
            tilted, outgoing, square = call(
                step_kernel,
                [(tilted_shape, False), (outgoing_shape, True), (squares_shape, False)],
                [near_index, far_index, asked],
                [*pieces, (factor, False)],
                staging + scratch,
                map_flops,
            )
        else:
            mapped, square = call(
                last_kernel,
                [(mapped_shape, False), (squares_shape, False)],
                [near_index, far_index],
                pieces,
                scratch,
                map_flops,
            )
        squares.append(jnp.sum(square, axis=1))

    partial = jnp.concatenate(squares)
    spread = jnp.broadcast_to(partial, (peer_count, partial.shape[0]))
    gathered = lax.all_to_all(spread, "rows", split_axis=0, concat_axis=0, tiled=True)
    totals = jnp.sum(gathered, axis=0).reshape(ITERS, tilt_count)
    states = total_blocks * block_size
    product = jnp.ones((tilt_count,), jnp.float32)
    growth = []
    for j in range(ITERS):
        scale = jnp.sqrt(totals[j] / product / product / states + 1e-06)
        product = product * scale
        growth.append(jnp.log(scale))
    return (mapped / product[:, None], jnp.stack(growth))


def solution(mesh):
    placed = (P("tilt", "rows"), P("rows"), P("tilt"), P(), P("rows", None, None), P("rows", None))
    return jax.shard_map(
        on_device,
        mesh=mesh,
        in_specs=placed,
        out_specs=(P("tilt", "rows"), P(None, "tilt")),
        check_vma=False,
    )
```

```python
import jax
import jax.numpy as jnp
from jax import lax
from jax.experimental import pallas as pl
from jax.experimental.pallas import tpu as pltpu
from jax.sharding import PartitionSpec as P

NEAR = 8
ITERS = 2
PACK_CHUNKS = 8
HALF_WORD = 1 << 16
VMEM_LIMIT = 62 * 1024 * 1024
SMALL_LIMIT = 48 * 1024 * 1024


def request_kernel(blocks_here, pattern, codes):
    peers = codes.shape[0]
    slots, rows = pattern.shape
    base = lax.broadcasted_iota(jnp.int32, (peers, rows), 0) * blocks_here
    low = jnp.full((peers, rows), blocks_here, jnp.int32)
    high = jnp.full((peers, rows), -1, jnp.int32)
    for slot in range(NEAR, slots):
        within = pattern[slot : slot + 1, :] - base
        named = (within >= 0) & (within < blocks_here)
        low = jnp.minimum(low, jnp.where(named, within, blocks_here))
        high = jnp.maximum(high, jnp.where(named, within, -1))
    low = jnp.min(low, axis=1, keepdims=True)
    high = jnp.max(high, axis=1, keepdims=True)
    code = jnp.where(high >= 0, high * HALF_WORD + low, 0)
    codes[...] = jnp.broadcast_to(code, codes.shape)


def start_copy(src, dst, sem):
    copy = pltpu.make_async_copy(src, dst, sem)
    copy.start()
    return copy


def pack_blocks(asked, tilted, staged, outgoing, sems):
    chunk = outgoing.shape[0] // PACK_CHUNKS
    copies = []
    for part in range(PACK_CHUNKS):

        def body(j, carry, part=part):
            code = asked[0, part * (chunk // 2) + j]
            staged[part * chunk + 2 * j] = tilted[lax.rem(code, HALF_WORD)]
            staged[part * chunk + 2 * j + 1] = tilted[lax.div(code, HALF_WORD)]
            return carry

        lax.fori_loop(0, chunk // 2, body, 0, unroll=8)
        span = pl.ds(part * chunk, chunk)
        copies.append(start_copy(staged.at[span], outgoing.at[span], sems.at[part]))
    return copies


def pack_kernel(codes, tilted, asked, outgoing, line, asked_smem, staged, line_sem, sems):
    peers = codes.shape[0]
    same = lax.broadcasted_iota(jnp.int32, (peers, peers), 0) == lax.broadcasted_iota(
        jnp.int32, (peers, peers), 1
    )
    words = jnp.sum(jnp.where(same, codes[:, :peers], 0), axis=0, keepdims=True)
    line[...] = words
    asked[...] = words
    start_copy(line, asked_smem, line_sem).wait()
    for copy in pack_blocks(asked_smem, tilted, staged, outgoing, sems):
        copy.wait()


def weighted(index, stride, slots, source, weights, gathered, rows, tilts):
    span = rows * tilts
    for n, slot in enumerate(slots):

        def gather(pair, carry, slot=slot, n=n):
            low = source[index[2 * pair * stride + slot]]
            high = source[index[(2 * pair + 1) * stride + slot]]
            at = pl.multiple_of(n * span + pair * 2 * tilts, 2 * tilts)
            gathered[pl.ds(at, 2 * tilts), :] = jnp.concatenate([low, high], axis=0)
            return carry

        lax.fori_loop(0, rows // 2, gather, 0, unroll=True)
    taken = gathered[: len(slots) * span, :]
    product = jnp.dot(taken, weights, preferred_element_type=jnp.float32)
    return product.reshape(len(slots), rows, tilts, weights.shape[1])


def map_blocks(operands, scratch):
    near_index, far_index, before, own, after, arrived, kernels, rates = operands
    near_smem, far_smem, extended, far_blocks, weights, rate_buf, gathered, sems = scratch
    kinds = kernels.shape[0]
    (rows, tilts, _), half = own.shape, before.shape[0]
    far_count = rates.shape[0] - NEAR

    first = [
        start_copy(near_index, near_smem, sems.at[0]),
        start_copy(before, extended.at[pl.ds(0, half)], sems.at[1]),
        start_copy(own, extended.at[pl.ds(half, rows)], sems.at[2]),
        start_copy(after, extended.at[pl.ds(half + rows, half)], sems.at[3]),
    ]
    kernel_copies = [start_copy(kernels.at[0], weights.at[0], sems.at[4])]
    rate_copy = start_copy(rates, rate_buf, sems.at[4 + kinds])
    kernel_copies += [
        start_copy(kernels.at[k], weights.at[k], sems.at[4 + k]) for k in range(1, kinds)
    ]
    late = [
        start_copy(far_index, far_smem, sems.at[5 + kinds]),
        start_copy(arrived, far_blocks, sems.at[6 + kinds]),
    ]
    for copy in first:
        copy.wait()

    total = None
    for kind in range(kinds):
        slots = range(kind, NEAR, kinds)
        kernel_copies[kind].wait()
        if kind == 0:
            rate_copy.wait()
        product = weighted(
            near_smem, NEAR, slots, extended, weights[kind], gathered.at[kind % 2], rows, tilts
        )
        for n, slot in enumerate(slots):
            term = product[n] * rate_buf[slot].astype(jnp.float32)[:, None, :]
            total = term if total is None else total + term
    for copy in late:
        copy.wait()
    for kind in range(kinds):
        slots = range(kind, far_count, kinds)
        product = weighted(
            far_smem, far_count, slots, far_blocks, weights[kind], gathered.at[kind % 2], rows, tilts
        )
        for n, slot in enumerate(slots):
            total = total + product[n] * rate_buf[NEAR + slot].astype(jnp.float32)[:, None, :]
    return total


def step_kernel(asked, factor, *refs):
    operands, (tilted, outgoing, squares) = refs[:8], refs[8:11]
    asked_smem, factor_buf, tilted_buf, staged, squares_buf, pack_sems, sems = refs[11:18]
    asked_copy = start_copy(asked, asked_smem, sems.at[0])
    factor_copy = start_copy(factor, factor_buf, sems.at[1])
    total = map_blocks(operands, refs[18:])
    factor_copy.wait()
    tilted_buf[...] = (factor_buf[...] * total).astype(jnp.bfloat16)
    copies = [start_copy(tilted_buf, tilted, sems.at[2])]
    asked_copy.wait()
    copies += pack_blocks(asked_smem, tilted_buf, staged, outgoing, pack_sems)
    squares_buf[...] = jnp.sum(total * total, axis=0)
    copies.append(start_copy(squares_buf, squares, sems.at[3]))
    for copy in copies:
        copy.wait()


def last_kernel(*refs):
    operands, (mapped, squares) = refs[:8], refs[8:10]
    mapped_buf, squares_buf, sems = refs[10:13]
    total = map_blocks(operands, refs[13:])
    for row in range(total.shape[0]):
        mapped_buf[:, row * total.shape[2] : (row + 1) * total.shape[2]] = total[row]
    copies = [start_copy(mapped_buf, mapped, sems.at[0])]
    squares_buf[...] = jnp.sum(total * total, axis=0)
    copies.append(start_copy(squares_buf, squares, sems.at[1]))
    for copy in copies:
        copy.wait()


def call(kernel, outs, arrays, scratch, flops, in_vmem=(), limit=VMEM_LIMIT):
    spec = [pl.BlockSpec(memory_space=pltpu.VMEM), pl.BlockSpec(memory_space=pl.ANY)]
    moved = sum(a.size * a.dtype.itemsize for a in (*arrays, *outs))
    return pl.pallas_call(
        kernel,
        out_shape=outs,
        in_specs=[spec[n not in in_vmem] for n in range(len(arrays))],
        out_specs=[spec[len(arrays) + n not in in_vmem] for n in range(len(outs))],
        scratch_shapes=scratch,
        compiler_params=pltpu.CompilerParams(vmem_limit_bytes=limit),
        cost_estimate=pl.CostEstimate(flops=flops, bytes_accessed=moved, transcendentals=0),
    )(*arrays)


def on_device(start, reward, theta, kernels, rates, pattern):
    tilt_count = start.shape[0]
    blocks_here, slot_count = pattern.shape
    kind_count, block_size = kernels.shape[:2]
    peer_count = lax.axis_size("rows")
    position = lax.axis_index("rows")
    total_blocks = blocks_here * peer_count
    far_count = slot_count - NEAR
    half_span = blocks_here // 2
    capacity = 2
    shape = jax.ShapeDtypeStruct
    sem = pltpu.SemaphoreType.DMA

    pattern_by_slot = pattern.T
    (codes,) = call(
        lambda *refs: request_kernel(blocks_here, *refs),
        [shape((peer_count, 128), jnp.int32)],
        [pattern_by_slot],
        [],
        0,
        in_vmem=(0, 1),
        limit=SMALL_LIMIT,
    )
    codes = lax.all_to_all(codes, "rows", split_axis=0, concat_axis=0, tiled=True)

    far_cols = pattern[:, NEAR:].reshape(-1)
    owners = lax.div(far_cols, blocks_here)
    smaller = (owners[:, None] == owners[None, :]) & (far_cols[None, :] < far_cols[:, None])
    far_index = owners * capacity + jnp.any(smaller, axis=1).astype(jnp.int32)
    local_rows = jnp.arange(blocks_here, dtype=jnp.int32)
    global_rows = position * blocks_here + local_rows
    shifts = (pattern[:, :NEAR] - global_rows[:, None] + half_span) % total_blocks - half_span
    near_index = (local_rows[:, None] + shifts + half_span).reshape(-1)

    up = [(i, (i + 1) % peer_count) for i in range(peer_count)]
    down = [(j, i) for i, j in up]
    rates_by_slot = rates.transpose(1, 0, 2)
    factor = jnp.exp(theta[None, :, None] * reward.reshape(blocks_here, 1, block_size))

    block = (tilt_count, block_size)
    asked_shape = shape((1, peer_count), jnp.int32)
    tilted_shape = shape((blocks_here, *block), jnp.bfloat16)
    outgoing_shape = shape((peer_count * capacity, *block), jnp.bfloat16)
    squares_shape = shape(block, jnp.float32)
    mapped_shape = shape(start.shape, jnp.float32)
    asked_smem = pltpu.SMEM(asked_shape.shape, jnp.int32)
    staged = pltpu.VMEM(outgoing_shape.shape, jnp.bfloat16)
    gather_rows = max(NEAR, far_count) // kind_count * blocks_here * tilt_count
    map_scratch = [
        pltpu.SMEM(near_index.shape, jnp.int32),
        pltpu.SMEM(far_index.shape, jnp.int32),
        pltpu.VMEM((blocks_here + 2 * half_span, *block), jnp.bfloat16),
        pltpu.VMEM(outgoing_shape.shape, jnp.bfloat16),
        pltpu.VMEM(kernels.shape, jnp.bfloat16),
        pltpu.VMEM(rates_by_slot.shape, jnp.bfloat16),
        pltpu.VMEM((2, gather_rows, block_size), jnp.bfloat16),
        sem((7 + kind_count,)),
    ]
    map_flops = 2 * slot_count * blocks_here * tilt_count * block_size * block_size

    tilted = factor * start.reshape(tilt_count, blocks_here, block_size).transpose(1, 0, 2)
    tilted = tilted.astype(jnp.bfloat16)
    asked, outgoing = call(
        pack_kernel,
        [asked_shape, outgoing_shape],
        [codes, tilted],
        [pltpu.VMEM(asked_shape.shape, jnp.int32), asked_smem, staged, sem, sem((PACK_CHUNKS,))],
        0,
        in_vmem=(0, 1, 2),
        limit=SMALL_LIMIT,
    )
    squares = []
    for iteration in range(ITERS):
        arrived = lax.all_to_all(outgoing, "rows", split_axis=0, concat_axis=0, tiled=True)
        before = lax.ppermute(tilted[blocks_here - half_span :], "rows", up)
        after = lax.ppermute(tilted[:half_span], "rows", down)
        operands = [near_index, far_index, before, tilted, after, arrived, kernels, rates_by_slot]
        if iteration < ITERS - 1:
            step_scratch = [
                asked_smem,
                pltpu.VMEM(tilted_shape.shape, jnp.float32),
                pltpu.VMEM(tilted_shape.shape, jnp.bfloat16),
                staged,
                pltpu.VMEM(block, jnp.float32),
                sem((PACK_CHUNKS,)),
                sem((4,)),
            ]
            tilted, outgoing, square = call(
                step_kernel,
                [tilted_shape, outgoing_shape, squares_shape],
                [asked, factor, *operands],
                step_scratch + map_scratch,
                map_flops,
            )
        else:
            last_scratch = [pltpu.VMEM(start.shape, jnp.float32), pltpu.VMEM(block, jnp.float32), sem((2,))]
            mapped, square = call(
                last_kernel,
                [mapped_shape, squares_shape],
                operands,
                last_scratch + map_scratch,
                map_flops,
            )
        squares.append(jnp.sum(square, axis=1))

    partial = jnp.concatenate(squares)
    spread = jnp.broadcast_to(partial, (peer_count, partial.shape[0]))
    gathered = lax.all_to_all(spread, "rows", split_axis=0, concat_axis=0, tiled=True)
    totals = jnp.sum(gathered, axis=0).reshape(ITERS, tilt_count)
    states = total_blocks * block_size
    product = jnp.ones((tilt_count,), jnp.float32)
    growth = []
    for j in range(ITERS):
        scale = jnp.sqrt(totals[j] / product / product / states + 1e-06)
        product = product * scale
        growth.append(jnp.log(scale))
    return (mapped / product[:, None], jnp.stack(growth))


def solution(mesh):
    placed = (P("tilt", "rows"), P("rows"), P("tilt"), P(), P("rows", None, None), P("rows", None))
    return jax.shard_map(
        on_device,
        mesh=mesh,
        in_specs=placed,
        out_specs=(P("tilt", "rows"), P(None, "tilt")),
        check_vma=False,
    )
```

```python
import jax
import jax.numpy as jnp
from jax import lax
from jax.experimental import pallas as pl
from jax.experimental.pallas import tpu as pltpu
from jax.sharding import PartitionSpec as P

NEAR = 8
ITERS = 2
PACK_CHUNKS = 8
HALF_WORD = 1 << 16
VMEM_LIMIT = 62 * 1024 * 1024
SMALL_LIMIT = 48 * 1024 * 1024


def request_kernel(blocks_here, pattern, codes):
    peers = codes.shape[0]
    slots, rows = pattern.shape
    base = lax.broadcasted_iota(jnp.int32, (peers, rows), 0) * blocks_here
    low = jnp.full((peers, rows), blocks_here, jnp.int32)
    high = jnp.full((peers, rows), -1, jnp.int32)
    for slot in range(NEAR, slots):
        within = pattern[slot : slot + 1, :] - base
        named = (within >= 0) & (within < blocks_here)
        low = jnp.minimum(low, jnp.where(named, within, blocks_here))
        high = jnp.maximum(high, jnp.where(named, within, -1))
    low = jnp.min(low, axis=1, keepdims=True)
    high = jnp.max(high, axis=1, keepdims=True)
    codes[...] = jnp.where(high >= 0, high * HALF_WORD + low, 0)


def start_copy(src, dst, sem):
    copy = pltpu.make_async_copy(src, dst, sem)
    copy.start()
    return copy


def read_words(codes, line, words, sem):
    peers = codes.shape[0]
    across = lax.broadcasted_iota(jnp.int32, (peers, peers), 1)
    same = lax.broadcasted_iota(jnp.int32, (peers, peers), 0) == across
    line[...] = jnp.sum(jnp.where(same, codes[...], 0), axis=0, keepdims=True)
    return start_copy(line, words, sem)


def pack_blocks(words, tilted, staged, outgoing, sems):
    chunk = outgoing.shape[0] // PACK_CHUNKS
    copies = []
    for part in range(PACK_CHUNKS):

        def body(j, carry, part=part):
            word = words[0, part * (chunk // 2) + j]
            staged[part * chunk + 2 * j] = tilted[lax.rem(word, HALF_WORD)]
            staged[part * chunk + 2 * j + 1] = tilted[lax.div(word, HALF_WORD)]
            return carry

        lax.fori_loop(0, chunk // 2, body, 0, unroll=8)
        span = pl.ds(part * chunk, chunk)
        copies.append(start_copy(staged.at[span], outgoing.at[span], sems.at[part]))
    return copies


def pack_kernel(codes, tilted, outgoing, line, words, staged, word_sem, sems):
    read_words(codes, line, words, word_sem).wait()
    for copy in pack_blocks(words, tilted, staged, outgoing, sems):
        copy.wait()


def weighted(index, stride, slots, source, weights, gathered, rows, tilts):
    span = rows * tilts
    for n, slot in enumerate(slots):

        def gather(pair, carry, slot=slot, n=n):
            low = source[index[2 * pair * stride + slot]]
            high = source[index[(2 * pair + 1) * stride + slot]]
            at = pl.multiple_of(n * span + pair * 2 * tilts, 2 * tilts)
            gathered[pl.ds(at, 2 * tilts), :] = jnp.concatenate([low, high], axis=0)
            return carry

        lax.fori_loop(0, rows // 2, gather, 0, unroll=True)
    taken = gathered[: len(slots) * span, :]
    product = jnp.dot(taken, weights, preferred_element_type=jnp.float32)
    return product.reshape(len(slots), rows, tilts, weights.shape[1])


def map_blocks(operands, scratch):
    near_index, far_index, before, own, after, arrived, kernels, rates = operands
    near_smem, far_smem, extended, far_blocks, weights, rate_buf, gathered, sems = scratch
    kinds = kernels.shape[0]
    (rows, tilts, _), half = own.shape, before.shape[0]
    far_count = rates.shape[0] - NEAR

    first = [
        start_copy(near_index, near_smem, sems.at[0]),
        start_copy(before, extended.at[pl.ds(0, half)], sems.at[1]),
        start_copy(own, extended.at[pl.ds(half, rows)], sems.at[2]),
        start_copy(after, extended.at[pl.ds(half + rows, half)], sems.at[3]),
    ]
    kernel_copies = [start_copy(kernels.at[0], weights.at[0], sems.at[4])]
    rate_copy = start_copy(rates, rate_buf, sems.at[4 + kinds])
    kernel_copies += [
        start_copy(kernels.at[k], weights.at[k], sems.at[4 + k]) for k in range(1, kinds)
    ]
    late = [
        start_copy(far_index, far_smem, sems.at[5 + kinds]),
        start_copy(arrived, far_blocks, sems.at[6 + kinds]),
    ]
    for copy in first:
        copy.wait()

    total = None
    for kind in range(kinds):
        slots = range(kind, NEAR, kinds)
        kernel_copies[kind].wait()
        if kind == 0:
            rate_copy.wait()
        product = weighted(
            near_smem, NEAR, slots, extended, weights[kind], gathered.at[kind % 2], rows, tilts
        )
        for n, slot in enumerate(slots):
            term = product[n] * rate_buf[slot].astype(jnp.float32)[:, None, :]
            total = term if total is None else total + term
    for copy in late:
        copy.wait()
    for kind in range(kinds):
        slots = range(kind, far_count, kinds)
        product = weighted(
            far_smem, far_count, slots, far_blocks, weights[kind], gathered.at[kind % 2], rows, tilts
        )
        for n, slot in enumerate(slots):
            total = total + product[n] * rate_buf[NEAR + slot].astype(jnp.float32)[:, None, :]
    return total


def sum_of_squares(total):
    return jnp.sum(jnp.sum(total * total, axis=0), axis=1, keepdims=True)


def step_kernel(codes, reward, theta, *refs):
    operands, (tilted, outgoing, squares) = refs[:8], refs[8:11]
    codes_buf, line, words, reward_buf, theta_smem, tilted_buf, staged, pack_sems, sems = refs[11:20]
    codes_copy = start_copy(codes, codes_buf, sems.at[0])
    reward_copy = start_copy(reward, reward_buf, sems.at[1])
    theta_copy = start_copy(theta, theta_smem, sems.at[4])
    total = map_blocks(operands, refs[20:])
    reward_copy.wait()
    theta_copy.wait()
    codes_copy.wait()
    words_copy = read_words(codes_buf, line, words, sems.at[2])
    tilt = lax.broadcasted_iota(jnp.int32, total.shape[1:], 0)
    thetas = jnp.zeros(total.shape[1:], jnp.float32)
    for t in range(total.shape[1]):
        thetas = jnp.where(tilt == t, theta_smem[t], thetas)
    factor = jnp.exp(thetas[None] * reward_buf[...][:, None, :])
    tilted_buf[...] = (factor * total).astype(jnp.bfloat16)
    copies = [start_copy(tilted_buf, tilted, sems.at[3])]
    words_copy.wait()
    copies += pack_blocks(words, tilted_buf, staged, outgoing, pack_sems)
    squares[...] = jnp.broadcast_to(sum_of_squares(total), squares.shape)
    for copy in copies:
        copy.wait()


def last_kernel(first_squares, *refs):
    operands, (mapped, sums) = refs[:8], refs[8:10]
    total = map_blocks(operands, refs[10:])
    for row in range(total.shape[0]):
        mapped[:, row * total.shape[2] : (row + 1) * total.shape[2]] = total[row]
    tilts = total.shape[1]
    across = lax.broadcasted_iota(jnp.int32, (tilts, sums.shape[1]), 1)
    tilt = lax.broadcasted_iota(jnp.int32, (tilts, sums.shape[1]), 0)
    both = jnp.where(across == tilt, first_squares[:, :1], 0.0) + jnp.where(
        across == tilt + tilts, sum_of_squares(total), 0.0
    )
    sums[...] = jnp.broadcast_to(jnp.sum(both, axis=0, keepdims=True), sums.shape)


def call(kernel, outs, arrays, scratch, flops, in_vmem=(), limit=VMEM_LIMIT):
    spec = [pl.BlockSpec(memory_space=pltpu.VMEM), pl.BlockSpec(memory_space=pl.ANY)]
    moved = sum(a.size * a.dtype.itemsize for a in (*arrays, *outs))
    return pl.pallas_call(
        kernel,
        out_shape=outs,
        in_specs=[spec[n not in in_vmem] for n in range(len(arrays))],
        out_specs=[spec[len(arrays) + n not in in_vmem] for n in range(len(outs))],
        scratch_shapes=scratch,
        compiler_params=pltpu.CompilerParams(vmem_limit_bytes=limit),
        cost_estimate=pl.CostEstimate(flops=flops, bytes_accessed=moved, transcendentals=0),
    )(*arrays)


def on_device(start, reward, theta, kernels, rates, pattern):
    tilt_count = start.shape[0]
    blocks_here, slot_count = pattern.shape
    kind_count, block_size = kernels.shape[:2]
    peer_count = lax.axis_size("rows")
    position = lax.axis_index("rows")
    total_blocks = blocks_here * peer_count
    far_count = slot_count - NEAR
    half_span = blocks_here // 2
    capacity = 2
    shape = jax.ShapeDtypeStruct
    sem = pltpu.SemaphoreType.DMA

    pattern_by_slot = pattern.T
    (codes,) = call(
        lambda *refs: request_kernel(blocks_here, *refs),
        [shape((peer_count, 1), jnp.int32)],
        [pattern_by_slot],
        [],
        0,
        in_vmem=(0, 1),
    )
    codes = lax.all_to_all(codes, "rows", split_axis=0, concat_axis=0, tiled=True)

    far_cols = pattern[:, NEAR:].reshape(-1)
    owners = lax.div(far_cols, blocks_here)
    smaller = (owners[:, None] == owners[None, :]) & (far_cols[None, :] < far_cols[:, None])
    far_index = owners * capacity + jnp.any(smaller, axis=1).astype(jnp.int32)
    local_rows = jnp.arange(blocks_here, dtype=jnp.int32)
    global_rows = position * blocks_here + local_rows
    shifts = (pattern[:, :NEAR] - global_rows[:, None] + half_span) % total_blocks - half_span
    near_index = (local_rows[:, None] + shifts + half_span).reshape(-1)

    up = [(i, (i + 1) % peer_count) for i in range(peer_count)]
    down = [(j, i) for i, j in up]
    rates_by_slot = rates.transpose(1, 0, 2)
    reward = reward.reshape(blocks_here, block_size)

    block = (tilt_count, block_size)
    tilted_shape = shape((blocks_here, *block), jnp.bfloat16)
    outgoing_shape = shape((peer_count * capacity, *block), jnp.bfloat16)
    squares_shape = shape((tilt_count, 128), jnp.float32)
    sums_shape = shape((peer_count, ITERS * tilt_count), jnp.float32)
    mapped_shape = shape(start.shape, jnp.float32)
    word_buffers = [pltpu.VMEM((1, peer_count), jnp.int32), pltpu.SMEM((1, peer_count), jnp.int32)]
    staged = pltpu.VMEM(outgoing_shape.shape, jnp.bfloat16)
    gather_rows = max(NEAR, far_count) // kind_count * blocks_here * tilt_count
    map_scratch = [
        pltpu.SMEM(near_index.shape, jnp.int32),
        pltpu.SMEM(far_index.shape, jnp.int32),
        pltpu.VMEM((blocks_here + 2 * half_span, *block), jnp.bfloat16),
        pltpu.VMEM(outgoing_shape.shape, jnp.bfloat16),
        pltpu.VMEM(kernels.shape, jnp.bfloat16),
        pltpu.VMEM(rates_by_slot.shape, jnp.bfloat16),
        pltpu.VMEM((2, gather_rows, block_size), jnp.bfloat16),
        sem((7 + kind_count,)),
    ]
    map_flops = 2 * slot_count * blocks_here * tilt_count * block_size * block_size

    factor = jnp.exp(theta[None, :, None] * reward[:, None, :])
    tilted = factor * start.reshape(tilt_count, blocks_here, block_size).transpose(1, 0, 2)
    tilted = tilted.astype(jnp.bfloat16)
    (outgoing,) = call(
        pack_kernel,
        [outgoing_shape],
        [codes, tilted],
        [*word_buffers, staged, sem, sem((PACK_CHUNKS,))],
        0,
        in_vmem=(0, 1),
        limit=SMALL_LIMIT,
    )
    for iteration in range(ITERS):
        arrived = lax.all_to_all(outgoing, "rows", split_axis=0, concat_axis=0, tiled=True)
        before = lax.ppermute(tilted[blocks_here - half_span :], "rows", up)
        after = lax.ppermute(tilted[:half_span], "rows", down)
        operands = [near_index, far_index, before, tilted, after, arrived, kernels, rates_by_slot]
        if iteration < ITERS - 1:
            step_scratch = [
                pltpu.VMEM(codes.shape, jnp.int32),
                *word_buffers,
                pltpu.VMEM(reward.shape, jnp.float32),
                pltpu.SMEM(theta.shape, jnp.float32),
                pltpu.VMEM(tilted_shape.shape, jnp.bfloat16),
                staged,
                sem((PACK_CHUNKS,)),
                sem((5,)),
            ]
            tilted, outgoing, squares = call(
                step_kernel,
                [tilted_shape, outgoing_shape, squares_shape],
                [codes, reward, theta, *operands],
                step_scratch + map_scratch,
                map_flops,
                in_vmem=(13,),
            )
        else:
            mapped, sums = call(
                last_kernel,
                [mapped_shape, sums_shape],
                [squares, *operands],
                map_scratch,
                map_flops,
                in_vmem=(0, 9, 10),
            )

    gathered = lax.all_to_all(sums, "rows", split_axis=0, concat_axis=0, tiled=True)
    totals = jnp.sum(gathered, axis=0).reshape(ITERS, tilt_count)
    states = total_blocks * block_size
    product = jnp.ones((tilt_count,), jnp.float32)
    growth = []
    for j in range(ITERS):
        scale = jnp.sqrt(totals[j] / product / product / states + 1e-06)
        product = product * scale
        growth.append(jnp.log(scale))
    return (mapped / product[:, None], jnp.stack(growth))


def solution(mesh):
    placed = (P("tilt", "rows"), P("rows"), P("tilt"), P(), P("rows", None, None), P("rows", None))
    return jax.shard_map(
        on_device,
        mesh=mesh,
        in_specs=placed,
        out_specs=(P("tilt", "rows"), P(None, "tilt")),
        check_vma=False,
    )
```

```python
import jax
import jax.numpy as jnp
from jax import lax
from jax.experimental import pallas as pl
from jax.experimental.pallas import tpu as pltpu
from jax.sharding import PartitionSpec as P

NEAR = 8
ITERS = 2
PACK_CHUNKS = 8
HALF_WORD = 1 << 16
VMEM_LIMIT = 62 * 1024 * 1024
SMALL_LIMIT = 48 * 1024 * 1024
STEP_LIMIT = 51 * 1024 * 1024
LAST_LIMIT = 50 * 1024 * 1024


def request_kernel(blocks_here, pattern, codes):
    peers = codes.shape[0]
    slots, rows = pattern.shape
    base = lax.broadcasted_iota(jnp.int32, (peers, rows), 0) * blocks_here
    low = jnp.full((peers, rows), blocks_here, jnp.int32)
    high = jnp.full((peers, rows), -1, jnp.int32)
    for slot in range(NEAR, slots):
        within = pattern[slot : slot + 1, :] - base
        named = (within >= 0) & (within < blocks_here)
        low = jnp.minimum(low, jnp.where(named, within, blocks_here))
        high = jnp.maximum(high, jnp.where(named, within, -1))
    low = jnp.min(low, axis=1, keepdims=True)
    high = jnp.max(high, axis=1, keepdims=True)
    codes[...] = jnp.where(high >= 0, high * HALF_WORD + low, 0)


def start_copy(src, dst, sem):
    copy = pltpu.make_async_copy(src, dst, sem)
    copy.start()
    return copy


def read_words(codes, line, words, sem):
    peers = codes.shape[0]
    across = lax.broadcasted_iota(jnp.int32, (peers, peers), 1)
    same = lax.broadcasted_iota(jnp.int32, (peers, peers), 0) == across
    line[...] = jnp.sum(jnp.where(same, codes[...], 0), axis=0, keepdims=True)
    return start_copy(line, words, sem)


def pack_blocks(words, tilted, staged, outgoing, sems):
    chunk = outgoing.shape[0] // PACK_CHUNKS
    copies = []
    for part in range(PACK_CHUNKS):

        def body(j, carry, part=part):
            word = words[0, part * (chunk // 2) + j]
            staged[part * chunk + 2 * j] = tilted[word & (HALF_WORD - 1)]
            staged[part * chunk + 2 * j + 1] = tilted[lax.shift_right_logical(word, 16)]
            return carry

        lax.fori_loop(0, chunk // 2, body, 0, unroll=8)
        span = pl.ds(part * chunk, chunk)
        copies.append(start_copy(staged.at[span], outgoing.at[span], sems.at[part]))
    return copies


def pack_kernel(codes, tilted, outgoing, line, words, staged, word_sem, sems):
    read_words(codes, line, words, word_sem).wait()
    for copy in pack_blocks(words, tilted, staged, outgoing, sems):
        copy.wait()


def weighted(index, stride, slots, source, weights, gathered, rows, tilts):
    span = rows * tilts
    for n, slot in enumerate(slots):

        def gather(pair, carry, slot=slot, n=n):
            low = source[index[2 * pair * stride + slot]]
            high = source[index[(2 * pair + 1) * stride + slot]]
            at = pl.multiple_of(n * span + pair * 2 * tilts, 2 * tilts)
            gathered[pl.ds(at, 2 * tilts), :] = jnp.concatenate([low, high], axis=0)
            return carry

        lax.fori_loop(0, rows // 2, gather, 0, unroll=True)
    taken = gathered[: len(slots) * span, :]
    product = jnp.dot(taken, weights, preferred_element_type=jnp.float32)
    return product.reshape(len(slots), rows, tilts, weights.shape[1])


def map_blocks(operands, scratch):
    near_index, far_index, before, own, after, arrived, kernels, rates = operands
    near_smem, far_smem, extended, weights, rate_buf, gathered, sems, *far_buf = scratch
    kinds = kernels.shape[0]
    (rows, tilts, _), half = own.shape, before.shape[0]
    far_count = rates.shape[0] - NEAR

    first = [
        start_copy(near_index, near_smem, sems.at[0]),
        start_copy(before, extended.at[pl.ds(0, half)], sems.at[1]),
        start_copy(own, extended.at[pl.ds(half, rows)], sems.at[2]),
        start_copy(after, extended.at[pl.ds(half + rows, half)], sems.at[3]),
    ]
    kernel_copies = [start_copy(kernels.at[0], weights.at[0], sems.at[4])]
    rate_copy = start_copy(rates, rate_buf, sems.at[4 + kinds])
    kernel_copies += [
        start_copy(kernels.at[k], weights.at[k], sems.at[4 + k]) for k in range(1, kinds)
    ]
    late = [start_copy(far_index, far_smem, sems.at[5 + kinds])]
    if far_buf:
        late.append(start_copy(arrived, far_buf[0], sems.at[6 + kinds]))
        arrived = far_buf[0]
    for copy in first:
        copy.wait()

    total = None
    for kind in range(kinds):
        slots = range(kind, NEAR, kinds)
        kernel_copies[kind].wait()
        if kind == 0:
            rate_copy.wait()
        product = weighted(
            near_smem, NEAR, slots, extended, weights[kind], gathered.at[kind % 2], rows, tilts
        )
        for n, slot in enumerate(slots):
            term = product[n] * rate_buf[slot].astype(jnp.float32)[:, None, :]
            total = term if total is None else total + term
    for copy in late:
        copy.wait()
    for kind in range(kinds):
        slots = range(kind, far_count, kinds)
        product = weighted(
            far_smem, far_count, slots, arrived, weights[kind], gathered.at[kind % 2], rows, tilts
        )
        for n, slot in enumerate(slots):
            total = total + product[n] * rate_buf[NEAR + slot].astype(jnp.float32)[:, None, :]
    return total


def sum_of_squares(total):
    return jnp.sum(jnp.sum(total * total, axis=0), axis=1, keepdims=True)


def step_kernel(codes, factor, *refs):
    operands, (tilted, outgoing, squares) = refs[:8], refs[8:11]
    codes_buf, line, words, factor_buf, tilted_buf, staged, pack_sems, sems = refs[11:19]
    codes_copy = start_copy(codes, codes_buf, sems.at[0])
    factor_copy = start_copy(factor, factor_buf, sems.at[1])
    total = map_blocks(operands, refs[19:])
    codes_copy.wait()
    words_copy = read_words(codes_buf, line, words, sems.at[2])
    factor_copy.wait()
    tilted_buf[...] = (factor_buf[...] * total).astype(jnp.bfloat16)
    copies = [start_copy(tilted_buf, tilted, sems.at[3])]
    words_copy.wait()
    copies += pack_blocks(words, tilted_buf, staged, outgoing, pack_sems)
    squares[...] = jnp.sum(total * total, axis=0)
    for copy in copies:
        copy.wait()


def last_kernel(first_squares, *refs):
    operands, (mapped, sums) = refs[:8], refs[8:10]
    total = map_blocks(operands, refs[10:])
    for row in range(total.shape[0]):
        mapped[:, row * total.shape[2] : (row + 1) * total.shape[2]] = total[row]
    tilts = total.shape[1]
    across = lax.broadcasted_iota(jnp.int32, (tilts, sums.shape[1]), 1)
    tilt = lax.broadcasted_iota(jnp.int32, (tilts, sums.shape[1]), 0)
    first = jnp.sum(first_squares[...], axis=1, keepdims=True)
    both = jnp.where(across == tilt, first, 0.0) + jnp.where(
        across == tilt + tilts, sum_of_squares(total), 0.0
    )
    sums[...] = jnp.broadcast_to(jnp.sum(both, axis=0, keepdims=True), sums.shape)


def call(kernel, outs, arrays, scratch, flops, in_vmem=(), limit=VMEM_LIMIT):
    spec = [pl.BlockSpec(memory_space=pltpu.VMEM), pl.BlockSpec(memory_space=pl.ANY)]
    moved = sum(a.size * a.dtype.itemsize for a in (*arrays, *outs))
    return pl.pallas_call(
        kernel,
        out_shape=outs,
        in_specs=[spec[n not in in_vmem] for n in range(len(arrays))],
        out_specs=[spec[len(arrays) + n not in in_vmem] for n in range(len(outs))],
        scratch_shapes=scratch,
        compiler_params=pltpu.CompilerParams(vmem_limit_bytes=limit),
        cost_estimate=pl.CostEstimate(flops=flops, bytes_accessed=moved, transcendentals=0),
    )(*arrays)


def on_device(start, reward, theta, kernels, rates, pattern):
    tilt_count = start.shape[0]
    blocks_here, slot_count = pattern.shape
    kind_count, block_size = kernels.shape[:2]
    peer_count = lax.axis_size("rows")
    position = lax.axis_index("rows")
    total_blocks = blocks_here * peer_count
    far_count = slot_count - NEAR
    half_span = blocks_here // 2
    capacity = 2
    shape = jax.ShapeDtypeStruct
    sem = pltpu.SemaphoreType.DMA

    pattern_by_slot = pattern.T
    (codes,) = call(
        lambda *refs: request_kernel(blocks_here, *refs),
        [shape((peer_count, 1), jnp.int32)],
        [pattern_by_slot],
        [],
        0,
        in_vmem=(0, 1),
    )
    codes = lax.all_to_all(codes, "rows", split_axis=0, concat_axis=0, tiled=True)

    far_cols = pattern[:, NEAR:].reshape(-1)
    owners = lax.div(far_cols, blocks_here)
    smaller = (owners[:, None] == owners[None, :]) & (far_cols[None, :] < far_cols[:, None])
    far_index = owners * capacity + jnp.any(smaller, axis=1).astype(jnp.int32)
    local_rows = jnp.arange(blocks_here, dtype=jnp.int32)
    global_rows = position * blocks_here + local_rows
    shifts = (pattern[:, :NEAR] - global_rows[:, None] + half_span) % total_blocks - half_span
    near_index = (local_rows[:, None] + shifts + half_span).reshape(-1)

    up = [(i, (i + 1) % peer_count) for i in range(peer_count)]
    down = [(j, i) for i, j in up]
    rates_by_slot = rates.transpose(1, 0, 2)
    reward = reward.reshape(blocks_here, block_size)

    block = (tilt_count, block_size)
    tilted_shape = shape((blocks_here, *block), jnp.bfloat16)
    outgoing_shape = shape((peer_count * capacity, *block), jnp.bfloat16)
    squares_shape = shape(block, jnp.float32)
    sums_shape = shape((peer_count, ITERS * tilt_count), jnp.float32)
    mapped_shape = shape(start.shape, jnp.float32)
    word_buffers = [pltpu.VMEM((1, peer_count), jnp.int32), pltpu.SMEM((1, peer_count), jnp.int32)]
    staged = pltpu.VMEM(outgoing_shape.shape, jnp.bfloat16)
    gather_rows = max(NEAR, far_count) // kind_count * blocks_here * tilt_count
    map_scratch = [
        pltpu.SMEM(near_index.shape, jnp.int32),
        pltpu.SMEM(far_index.shape, jnp.int32),
        pltpu.VMEM((blocks_here + 2 * half_span, *block), jnp.bfloat16),
        pltpu.VMEM(kernels.shape, jnp.bfloat16),
        pltpu.VMEM(rates_by_slot.shape, jnp.bfloat16),
        pltpu.VMEM((2, gather_rows, block_size), jnp.bfloat16),
        sem((7 + kind_count,)),
    ]
    map_flops = 2 * slot_count * blocks_here * tilt_count * block_size * block_size

    factor = jnp.exp(theta[None, :, None] * reward[:, None, :])
    tilted = factor * start.reshape(tilt_count, blocks_here, block_size).transpose(1, 0, 2)
    tilted = tilted.astype(jnp.bfloat16)
    (outgoing,) = call(
        pack_kernel,
        [outgoing_shape],
        [codes, tilted],
        [*word_buffers, staged, sem, sem((PACK_CHUNKS,))],
        0,
        in_vmem=(0, 1),
        limit=SMALL_LIMIT,
    )
    for iteration in range(ITERS):
        arrived = lax.all_to_all(outgoing, "rows", split_axis=0, concat_axis=0, tiled=True)
        before = lax.ppermute(tilted[blocks_here - half_span :], "rows", up)
        after = lax.ppermute(tilted[:half_span], "rows", down)
        operands = [near_index, far_index, before, tilted, after, arrived, kernels, rates_by_slot]
        if iteration < ITERS - 1:
            step_scratch = [
                pltpu.VMEM(codes.shape, jnp.int32),
                *word_buffers,
                pltpu.VMEM(tilted_shape.shape, jnp.float32),
                pltpu.VMEM(tilted_shape.shape, jnp.bfloat16),
                staged,
                sem((PACK_CHUNKS,)),
                sem((4,)),
            ]
            tilted, outgoing, squares = call(
                step_kernel,
                [tilted_shape, outgoing_shape, squares_shape],
                [codes, factor, *operands],
                [*step_scratch, *map_scratch, staged],
                map_flops,
                in_vmem=(12,),
                limit=STEP_LIMIT,
            )
        else:
            mapped, sums = call(
                last_kernel,
                [mapped_shape, sums_shape],
                [squares, *operands],
                map_scratch,
                map_flops,
                in_vmem=(0, 6, 9, 10),
                limit=LAST_LIMIT,
            )

    gathered = lax.all_to_all(sums, "rows", split_axis=0, concat_axis=0, tiled=True)
    totals = jnp.sum(gathered, axis=0).reshape(ITERS, tilt_count)
    states = total_blocks * block_size
    product = jnp.ones((tilt_count,), jnp.float32)
    growth = []
    for j in range(ITERS):
        scale = jnp.sqrt(totals[j] / product / product / states + 1e-06)
        product = product * scale
        growth.append(jnp.log(scale))
    return (mapped / product[:, None], jnp.stack(growth))


def solution(mesh):
    placed = (P("tilt", "rows"), P("rows"), P("tilt"), P(), P("rows", None, None), P("rows", None))
    return jax.shard_map(
        on_device,
        mesh=mesh,
        in_specs=placed,
        out_specs=(P("tilt", "rows"), P(None, "tilt")),
        check_vma=False,
    )
```

```python
import jax
import jax.numpy as jnp
from jax import lax
from jax.experimental import pallas as pl
from jax.experimental.pallas import tpu as pltpu
from jax.sharding import PartitionSpec as P

NEAR = 8
ITERS = 2
PACK_CHUNKS = 8
HALF_WORD = 1 << 16
REQUEST_LIMIT = 62 * 1024 * 1024
PACK_LIMIT = 48 * 1024 * 1024
MAP_LIMIT = 51 * 1024 * 1024


def request_kernel(blocks_here, pattern, codes):
    peers = codes.shape[0]
    slots, rows = pattern.shape
    base = lax.broadcasted_iota(jnp.int32, (peers, rows), 0) * blocks_here
    low = jnp.full((peers, rows), blocks_here, jnp.int32)
    high = jnp.full((peers, rows), -1, jnp.int32)
    for slot in range(NEAR, slots):
        within = pattern[slot : slot + 1, :] - base
        named = (within >= 0) & (within < blocks_here)
        low = jnp.minimum(low, jnp.where(named, within, blocks_here))
        high = jnp.maximum(high, jnp.where(named, within, -1))
    low = jnp.min(low, axis=1, keepdims=True)
    high = jnp.max(high, axis=1, keepdims=True)
    codes[...] = jnp.where(high >= 0, high * HALF_WORD + low, 0)


def start_copy(src, dst, sem):
    copy = pltpu.make_async_copy(src, dst, sem)
    copy.start()
    return copy


def read_words(codes, line, words, sem):
    peers = codes.shape[0]
    across = lax.broadcasted_iota(jnp.int32, (peers, peers), 1)
    same = lax.broadcasted_iota(jnp.int32, (peers, peers), 0) == across
    line[...] = jnp.sum(jnp.where(same, codes[...], 0), axis=0, keepdims=True)
    return start_copy(line, words, sem)


def pack_blocks(words, tilted, staged, outgoing, sems):
    chunk = outgoing.shape[0] // PACK_CHUNKS
    copies = []
    for part in range(PACK_CHUNKS):

        def body(j, carry, part=part):
            word = words[0, part * (chunk // 2) + j]
            staged[part * chunk + 2 * j] = tilted[word & (HALF_WORD - 1)]
            staged[part * chunk + 2 * j + 1] = tilted[lax.shift_right_logical(word, 16)]
            return carry

        lax.fori_loop(0, chunk // 2, body, 0, unroll=8)
        span = pl.ds(part * chunk, chunk)
        copies.append(start_copy(staged.at[span], outgoing.at[span], sems.at[part]))
    return copies


def pack_kernel(codes, tilted, outgoing, line, words, staged, word_sem, sems):
    read_words(codes, line, words, word_sem).wait()
    for copy in pack_blocks(words, tilted, staged, outgoing, sems):
        copy.wait()


def weighted(index, stride, slots, source, weights, gathered, rows, tilts):
    span = rows * tilts
    for n, slot in enumerate(slots):

        def gather(pair, carry, slot=slot, n=n):
            low = source[index[2 * pair * stride + slot]]
            high = source[index[(2 * pair + 1) * stride + slot]]
            at = pl.multiple_of(n * span + pair * 2 * tilts, 2 * tilts)
            gathered[pl.ds(at, 2 * tilts), :] = jnp.concatenate([low, high], axis=0)
            return carry

        lax.fori_loop(0, rows // 2, gather, 0, unroll=True)
    taken = gathered[: len(slots) * span, :]
    product = jnp.dot(taken, weights, preferred_element_type=jnp.float32)
    return product.reshape(len(slots), rows, tilts, weights.shape[1])


def map_blocks(operands, scratch, meanwhile=None):
    near_index, far_index, before, own, after, arrived, kernels, rates = operands
    near_smem, far_smem, extended, far_blocks, weights, rate_buf, gathered, sems = scratch
    kinds = kernels.shape[0]
    (rows, tilts, _), half = own.shape, before.shape[0]
    far_count = rates.shape[0] - NEAR

    first = [
        start_copy(near_index, near_smem, sems.at[0]),
        start_copy(before, extended.at[pl.ds(0, half)], sems.at[1]),
        start_copy(own, extended.at[pl.ds(half, rows)], sems.at[2]),
        start_copy(after, extended.at[pl.ds(half + rows, half)], sems.at[3]),
    ]
    kernel_copies = [start_copy(kernels.at[0], weights.at[0], sems.at[4])]
    rate_copy = start_copy(rates, rate_buf, sems.at[4 + kinds])
    kernel_copies += [
        start_copy(kernels.at[k], weights.at[k], sems.at[4 + k]) for k in range(1, kinds)
    ]
    late = [
        start_copy(far_index, far_smem, sems.at[5 + kinds]),
        start_copy(arrived, far_blocks, sems.at[6 + kinds]),
    ]
    if meanwhile is not None:
        meanwhile()
    for copy in first:
        copy.wait()

    total = None
    for kind in range(kinds):
        slots = range(kind, NEAR, kinds)
        kernel_copies[kind].wait()
        if kind == 0:
            rate_copy.wait()
        product = weighted(
            near_smem, NEAR, slots, extended, weights[kind], gathered.at[kind % 2], rows, tilts
        )
        for n, slot in enumerate(slots):
            term = product[n] * rate_buf[slot].astype(jnp.float32)[:, None, :]
            total = term if total is None else total + term
    for copy in late:
        copy.wait()
    for kind in range(kinds):
        slots = range(kind, far_count, kinds)
        product = weighted(
            far_smem, far_count, slots, far_blocks, weights[kind], gathered.at[kind % 2], rows, tilts
        )
        for n, slot in enumerate(slots):
            total = total + product[n] * rate_buf[NEAR + slot].astype(jnp.float32)[:, None, :]
    return total


def sum_of_squares(total):
    return jnp.sum(jnp.sum(total * total, axis=0), axis=1, keepdims=True)


def step_kernel(codes, factor, *refs):
    operands, (tilted, outgoing, squares) = refs[:8], refs[8:11]
    codes_buf, line, words, factor_buf, tilted_buf, staged, pack_sems, sems = refs[11:19]
    codes_copy = start_copy(codes, codes_buf, sems.at[0])
    waits = []

    def decode():
        waits.append(start_copy(factor, factor_buf, sems.at[1]))
        codes_copy.wait()
        waits.append(read_words(codes_buf, line, words, sems.at[2]))

    total = map_blocks(operands, refs[19:], decode)
    factor_copy, words_copy = waits
    factor_copy.wait()
    tilted_buf[...] = (factor_buf[...] * total).astype(jnp.bfloat16)
    copies = [start_copy(tilted_buf, tilted, sems.at[3])]
    words_copy.wait()
    copies += pack_blocks(words, tilted_buf, staged, outgoing, pack_sems)
    squares[...] = jnp.sum(total * total, axis=0)
    for copy in copies:
        copy.wait()


def last_kernel(first_squares, *refs):
    operands, (mapped, sums) = refs[:8], refs[8:10]
    total = map_blocks(operands, refs[10:])
    for row in range(total.shape[0]):
        mapped[:, row * total.shape[2] : (row + 1) * total.shape[2]] = total[row]
    tilts = total.shape[1]
    across = lax.broadcasted_iota(jnp.int32, (tilts, sums.shape[1]), 1)
    tilt = lax.broadcasted_iota(jnp.int32, (tilts, sums.shape[1]), 0)
    first = jnp.sum(first_squares[...], axis=1, keepdims=True)
    both = jnp.where(across == tilt, first, 0.0) + jnp.where(
        across == tilt + tilts, sum_of_squares(total), 0.0
    )
    sums[...] = jnp.broadcast_to(jnp.sum(both, axis=0, keepdims=True), sums.shape)


def call(kernel, outs, arrays, scratch, flops, limit, in_vmem=()):
    spec = [pl.BlockSpec(memory_space=pltpu.VMEM), pl.BlockSpec(memory_space=pl.ANY)]
    moved = sum(a.size * a.dtype.itemsize for a in (*arrays, *outs))
    return pl.pallas_call(
        kernel,
        out_shape=outs,
        in_specs=[spec[n not in in_vmem] for n in range(len(arrays))],
        out_specs=[spec[len(arrays) + n not in in_vmem] for n in range(len(outs))],
        scratch_shapes=scratch,
        compiler_params=pltpu.CompilerParams(vmem_limit_bytes=limit),
        cost_estimate=pl.CostEstimate(flops=flops, bytes_accessed=moved, transcendentals=0),
    )(*arrays)


def on_device(start, reward, theta, kernels, rates, pattern):
    tilt_count = start.shape[0]
    blocks_here, slot_count = pattern.shape
    kind_count, block_size = kernels.shape[:2]
    peer_count = lax.axis_size("rows")
    position = lax.axis_index("rows")
    total_blocks = blocks_here * peer_count
    far_count = slot_count - NEAR
    half_span = blocks_here // 2
    capacity = 2
    shape = jax.ShapeDtypeStruct
    sem = pltpu.SemaphoreType.DMA

    pattern_by_slot = pattern.T
    (codes,) = call(
        lambda *refs: request_kernel(blocks_here, *refs),
        [shape((peer_count, 1), jnp.int32)],
        [pattern_by_slot],
        [],
        0,
        REQUEST_LIMIT,
        in_vmem=(0, 1),
    )
    codes = lax.all_to_all(codes, "rows", split_axis=0, concat_axis=0, tiled=True)

    far_cols = pattern[:, NEAR:].reshape(-1)
    owners = lax.div(far_cols, blocks_here)
    smaller = (owners[:, None] == owners[None, :]) & (far_cols[None, :] < far_cols[:, None])
    far_index = owners * capacity + jnp.any(smaller, axis=1).astype(jnp.int32)
    local_rows = jnp.arange(blocks_here, dtype=jnp.int32)
    global_rows = position * blocks_here + local_rows
    shifts = (pattern[:, :NEAR] - global_rows[:, None] + half_span) % total_blocks - half_span
    near_index = (local_rows[:, None] + shifts + half_span).reshape(-1)

    up = [(i, (i + 1) % peer_count) for i in range(peer_count)]
    down = [(j, i) for i, j in up]
    rates_by_slot = rates.transpose(1, 0, 2)
    reward = reward.reshape(blocks_here, block_size)

    block = (tilt_count, block_size)
    tilted_shape = shape((blocks_here, *block), jnp.bfloat16)
    outgoing_shape = shape((peer_count * capacity, *block), jnp.bfloat16)
    squares_shape = shape(block, jnp.float32)
    sums_shape = shape((peer_count, ITERS * tilt_count), jnp.float32)
    mapped_shape = shape(start.shape, jnp.float32)
    word_buffers = [pltpu.VMEM((1, peer_count), jnp.int32), pltpu.SMEM((1, peer_count), jnp.int32)]
    staged = pltpu.VMEM(outgoing_shape.shape, jnp.bfloat16)
    gather_rows = max(NEAR, far_count) // kind_count * blocks_here * tilt_count
    map_scratch = [
        pltpu.SMEM(near_index.shape, jnp.int32),
        pltpu.SMEM(far_index.shape, jnp.int32),
        pltpu.VMEM((blocks_here + 2 * half_span, *block), jnp.bfloat16),
        staged,
        pltpu.VMEM(kernels.shape, jnp.bfloat16),
        pltpu.VMEM(rates_by_slot.shape, jnp.bfloat16),
        pltpu.VMEM((2, gather_rows, block_size), jnp.bfloat16),
        sem((7 + kind_count,)),
    ]
    map_flops = 2 * slot_count * blocks_here * tilt_count * block_size * block_size

    factor = jnp.exp(theta[None, :, None] * reward[:, None, :])
    tilted = factor * start.reshape(tilt_count, blocks_here, block_size).transpose(1, 0, 2)
    tilted = tilted.astype(jnp.bfloat16)
    (outgoing,) = call(
        pack_kernel,
        [outgoing_shape],
        [codes, tilted],
        [*word_buffers, staged, sem, sem((PACK_CHUNKS,))],
        0,
        PACK_LIMIT,
        in_vmem=(0, 1),
    )
    for iteration in range(ITERS):
        arrived = lax.all_to_all(outgoing, "rows", split_axis=0, concat_axis=0, tiled=True)
        before = lax.ppermute(tilted[blocks_here - half_span :], "rows", up)
        after = lax.ppermute(tilted[:half_span], "rows", down)
        operands = [near_index, far_index, before, tilted, after, arrived, kernels, rates_by_slot]
        if iteration < ITERS - 1:
            step_scratch = [
                pltpu.VMEM(codes.shape, jnp.int32),
                *word_buffers,
                pltpu.VMEM(tilted_shape.shape, jnp.float32),
                pltpu.VMEM(tilted_shape.shape, jnp.bfloat16),
                staged,
                sem((PACK_CHUNKS,)),
                sem((4,)),
            ]
            tilted, outgoing, squares = call(
                step_kernel,
                [tilted_shape, outgoing_shape, squares_shape],
                [codes, factor, *operands],
                step_scratch + map_scratch,
                map_flops,
                MAP_LIMIT,
                in_vmem=(12,),
            )
        else:
            mapped, sums = call(
                last_kernel,
                [mapped_shape, sums_shape],
                [squares, *operands],
                map_scratch,
                map_flops,
                MAP_LIMIT,
                in_vmem=(0, 9, 10),
            )

    gathered = lax.all_to_all(sums, "rows", split_axis=0, concat_axis=0, tiled=True)
    totals = jnp.sum(gathered, axis=0).reshape(ITERS, tilt_count)
    states = total_blocks * block_size
    product = jnp.ones((tilt_count,), jnp.float32)
    growth = []
    for j in range(ITERS):
        scale = jnp.sqrt(totals[j] / product / product / states + 1e-06)
        product = product * scale
        growth.append(jnp.log(scale))
    return (mapped / product[:, None], jnp.stack(growth))


def solution(mesh):
    placed = (P("tilt", "rows"), P("rows"), P("tilt"), P(), P("rows", None, None), P("rows", None))
    return jax.shard_map(
        on_device,
        mesh=mesh,
        in_specs=placed,
        out_specs=(P("tilt", "rows"), P(None, "tilt")),
        check_vma=False,
    )
```

```python
import math

import jax
import jax.numpy as jnp
from jax import lax
from jax.experimental import pallas as pl
from jax.experimental.pallas import tpu as pltpu
from jax.sharding import PartitionSpec as P

NEAR = 8
ITERS = 2
PACK_CHUNKS = 8
HALF_WORD = 1 << 16
REQUEST_LIMIT = 62 * 1024 * 1024
PACK_LIMIT = 48 * 1024 * 1024
MAP_LIMIT = 44 * 1024 * 1024


def request_kernel(blocks_here, pattern, codes):
    peers = codes.shape[0]
    slots, rows = pattern.shape
    base = lax.broadcasted_iota(jnp.int32, (peers, rows), 0) * blocks_here
    low = jnp.full((peers, rows), blocks_here, jnp.int32)
    high = jnp.full((peers, rows), -1, jnp.int32)
    for slot in range(NEAR, slots):
        within = pattern[slot : slot + 1, :] - base
        named = (within >= 0) & (within < blocks_here)
        low = jnp.minimum(low, jnp.where(named, within, blocks_here))
        high = jnp.maximum(high, jnp.where(named, within, -1))
    low = jnp.min(low, axis=1, keepdims=True)
    high = jnp.max(high, axis=1, keepdims=True)
    codes[...] = jnp.where(high >= 0, high * HALF_WORD + low, 0)


def start_copy(src, dst, sem):
    copy = pltpu.make_async_copy(src, dst, sem)
    copy.start()
    return copy


def read_words(codes, line, words, sem):
    peers = codes.shape[0]
    across = lax.broadcasted_iota(jnp.int32, (peers, peers), 1)
    same = lax.broadcasted_iota(jnp.int32, (peers, peers), 0) == across
    line[...] = jnp.sum(jnp.where(same, codes[...], 0), axis=0, keepdims=True)
    return start_copy(line, words, sem)


def pack_blocks(words, tilted, staged, outgoing, sems):
    chunk = outgoing.shape[0] // PACK_CHUNKS
    copies = []
    for part in range(PACK_CHUNKS):

        def body(j, carry, part=part):
            word = words[0, part * (chunk // 2) + j]
            staged[part * chunk + 2 * j] = tilted[word & (HALF_WORD - 1)]
            staged[part * chunk + 2 * j + 1] = tilted[lax.shift_right_logical(word, 16)]
            return carry

        lax.fori_loop(0, chunk // 2, body, 0, unroll=8)
        span = pl.ds(part * chunk, chunk)
        copies.append(start_copy(staged.at[span], outgoing.at[span], sems.at[part]))
    return copies


def pack_kernel(codes, tilted, outgoing, line, words, staged, word_sem, sems):
    read_words(codes, line, words, word_sem).wait()
    for copy in pack_blocks(words, tilted, staged, outgoing, sems):
        copy.wait()


def weighted(index, stride, slots, source, weights, gathered, rows, tilts):
    span = rows * tilts
    for n, slot in enumerate(slots):

        def gather(pair, carry, slot=slot, n=n):
            low = source[index[2 * pair * stride + slot]]
            high = source[index[(2 * pair + 1) * stride + slot]]
            at = pl.multiple_of(n * span + pair * 2 * tilts, 2 * tilts)
            gathered[pl.ds(at, 2 * tilts), :] = jnp.concatenate([low, high], axis=0)
            return carry

        lax.fori_loop(0, rows // 2, gather, 0, unroll=True)
    taken = gathered[: len(slots) * span, :]
    product = jnp.dot(taken, weights, preferred_element_type=jnp.float32)
    return product.reshape(len(slots), rows, tilts, weights.shape[1])


def map_blocks(operands, scratch, meanwhile=None):
    near_index, far_index, before, own, after, arrived, kernels, rates = operands
    near_smem, far_smem, extended, far_blocks, rate_buf, gathered, sems = scratch
    kinds = kernels.shape[0]
    (rows, tilts, _), half = own.shape, before.shape[0]
    far_count = rates.shape[0] - NEAR

    first = [
        start_copy(near_index, near_smem, sems.at[0]),
        start_copy(before, extended.at[pl.ds(0, half)], sems.at[1]),
        start_copy(own, extended.at[pl.ds(half, rows)], sems.at[2]),
        start_copy(after, extended.at[pl.ds(half + rows, half)], sems.at[3]),
    ]
    first.append(start_copy(rates, rate_buf, sems.at[4]))
    late = [
        start_copy(far_index, far_smem, sems.at[5]),
        start_copy(arrived, far_blocks, sems.at[6]),
    ]
    if meanwhile is not None:
        meanwhile()
    for copy in first:
        copy.wait()

    total = None
    for kind in range(kinds):
        slots = range(kind, NEAR, kinds)
        product = weighted(
            near_smem, NEAR, slots, extended, kernels[kind], gathered.at[kind % 2], rows, tilts
        )
        for n, slot in enumerate(slots):
            term = product[n] * rate_buf[slot].astype(jnp.float32)[:, None, :]
            total = term if total is None else total + term
    for copy in late:
        copy.wait()
    for kind in range(kinds):
        slots = range(kind, far_count, kinds)
        product = weighted(
            far_smem, far_count, slots, far_blocks, kernels[kind], gathered.at[kind % 2], rows, tilts
        )
        for n, slot in enumerate(slots):
            total = total + product[n] * rate_buf[NEAR + slot].astype(jnp.float32)[:, None, :]
    return total


def sum_of_squares(total):
    return jnp.sum(jnp.sum(total * total, axis=0), axis=1, keepdims=True)


def step_kernel(codes, factor, *refs):
    operands, (tilted, outgoing, squares) = refs[:8], refs[8:11]
    codes_buf, line, words, tilted_buf, staged, pack_sems, sems = refs[11:18]
    codes_copy = start_copy(codes, codes_buf, sems.at[0])
    decoded = []

    def decode():
        codes_copy.wait()
        decoded.append(read_words(codes_buf, line, words, sems.at[1]))

    total = map_blocks(operands, refs[18:], decode)
    tilted_buf[...] = (factor[...] * total).astype(jnp.bfloat16)
    copies = [start_copy(tilted_buf, tilted, sems.at[2])]
    decoded[0].wait()
    copies += pack_blocks(words, tilted_buf, staged, outgoing, pack_sems)
    squares[...] = jnp.sum(total * total, axis=0)
    for copy in copies:
        copy.wait()


def last_kernel(first_squares, *refs):
    operands, (mapped, sums) = refs[:8], refs[8:10]
    total = map_blocks(operands, refs[10:])
    for row in range(total.shape[0]):
        mapped[:, row * total.shape[2] : (row + 1) * total.shape[2]] = total[row]
    tilts = total.shape[1]
    across = lax.broadcasted_iota(jnp.int32, (tilts, sums.shape[1]), 1)
    tilt = lax.broadcasted_iota(jnp.int32, (tilts, sums.shape[1]), 0)
    first = jnp.sum(first_squares[...], axis=1, keepdims=True)
    both = jnp.where(across == tilt, first, 0.0) + jnp.where(
        across == tilt + tilts, sum_of_squares(total), 0.0
    )
    sums[...] = jnp.broadcast_to(jnp.sum(both, axis=0, keepdims=True), sums.shape)


def call(kernel, outs, arrays, scratch, flops, limit, in_vmem=()):
    spec = [pl.BlockSpec(memory_space=pltpu.VMEM), pl.BlockSpec(memory_space=pl.ANY)]
    moved = sum(math.prod(a.shape) * a.dtype.itemsize for a in (*arrays, *outs))
    return pl.pallas_call(
        kernel,
        out_shape=outs,
        in_specs=[spec[n not in in_vmem] for n in range(len(arrays))],
        out_specs=[spec[len(arrays) + n not in in_vmem] for n in range(len(outs))],
        scratch_shapes=scratch,
        compiler_params=pltpu.CompilerParams(vmem_limit_bytes=limit),
        cost_estimate=pl.CostEstimate(flops=flops, bytes_accessed=moved, transcendentals=0),
    )(*arrays)


def on_device(start, reward, theta, kernels, rates, pattern):
    tilt_count = start.shape[0]
    blocks_here, slot_count = pattern.shape
    kind_count, block_size = kernels.shape[:2]
    peer_count = lax.axis_size("rows")
    position = lax.axis_index("rows")
    total_blocks = blocks_here * peer_count
    far_count = slot_count - NEAR
    half_span = blocks_here // 2
    capacity = 2
    shape = jax.ShapeDtypeStruct
    sem = pltpu.SemaphoreType.DMA

    pattern_by_slot = pattern.T
    (codes,) = call(
        lambda *refs: request_kernel(blocks_here, *refs),
        [shape((peer_count, 1), jnp.int32)],
        [pattern_by_slot],
        [],
        0,
        REQUEST_LIMIT,
        in_vmem=(0, 1),
    )
    codes = lax.all_to_all(codes, "rows", split_axis=0, concat_axis=0, tiled=True)

    far_cols = pattern[:, NEAR:].reshape(-1)
    owners = lax.div(far_cols, blocks_here)
    smaller = (owners[:, None] == owners[None, :]) & (far_cols[None, :] < far_cols[:, None])
    far_index = owners * capacity + jnp.any(smaller, axis=1).astype(jnp.int32)
    local_rows = jnp.arange(blocks_here, dtype=jnp.int32)
    global_rows = position * blocks_here + local_rows
    shifts = (pattern[:, :NEAR] - global_rows[:, None] + half_span) % total_blocks - half_span
    near_index = (local_rows[:, None] + shifts + half_span).reshape(-1)

    up = [(i, (i + 1) % peer_count) for i in range(peer_count)]
    down = [(j, i) for i, j in up]
    rates_by_slot = rates.transpose(1, 0, 2)
    reward = reward.reshape(blocks_here, block_size)

    block = (tilt_count, block_size)
    tilted_shape = shape((blocks_here, *block), jnp.bfloat16)
    outgoing_shape = shape((peer_count * capacity, *block), jnp.bfloat16)
    squares_shape = shape(block, jnp.float32)
    sums_shape = shape((peer_count, ITERS * tilt_count), jnp.float32)
    mapped_shape = shape(start.shape, jnp.float32)
    word_buffers = [pltpu.VMEM((1, peer_count), jnp.int32), pltpu.SMEM((1, peer_count), jnp.int32)]
    staged = pltpu.VMEM(outgoing_shape.shape, jnp.bfloat16)
    gather_rows = max(NEAR, far_count) // kind_count * blocks_here * tilt_count
    map_scratch = [
        pltpu.SMEM(near_index.shape, jnp.int32),
        pltpu.SMEM(far_index.shape, jnp.int32),
        pltpu.VMEM((blocks_here + 2 * half_span, *block), jnp.bfloat16),
        staged,
        pltpu.VMEM(rates_by_slot.shape, jnp.bfloat16),
        pltpu.VMEM((2, gather_rows, block_size), jnp.bfloat16),
        sem((7,)),
    ]
    map_flops = 2 * slot_count * blocks_here * tilt_count * block_size * block_size

    factor = jnp.exp(theta[None, :, None] * reward[:, None, :])
    tilted = factor * start.reshape(tilt_count, blocks_here, block_size).transpose(1, 0, 2)
    tilted = tilted.astype(jnp.bfloat16)
    (outgoing,) = call(
        pack_kernel,
        [pltpu.HBM(outgoing_shape.shape, outgoing_shape.dtype)],
        [codes, tilted],
        [*word_buffers, staged, sem, sem((PACK_CHUNKS,))],
        0,
        PACK_LIMIT,
        in_vmem=(0, 1),
    )
    for iteration in range(ITERS):
        arrived = lax.all_to_all(outgoing, "rows", split_axis=0, concat_axis=0, tiled=True)
        before = lax.ppermute(tilted[blocks_here - half_span :], "rows", up)
        after = lax.ppermute(tilted[:half_span], "rows", down)
        arrived = pltpu.with_memory_space_constraint(arrived, pltpu.HBM)
        rates_hbm = pltpu.with_memory_space_constraint(rates_by_slot, pltpu.HBM)
        if iteration < ITERS - 1:
            before = pltpu.with_memory_space_constraint(before, pltpu.HBM)
            after = pltpu.with_memory_space_constraint(after, pltpu.HBM)
        operands = [near_index, far_index, before, tilted, after, arrived, kernels, rates_hbm]
        if iteration < ITERS - 1:
            step_scratch = [
                pltpu.VMEM(codes.shape, jnp.int32),
                *word_buffers,
                pltpu.VMEM(tilted_shape.shape, jnp.bfloat16),
                staged,
                sem((PACK_CHUNKS,)),
                sem((3,)),
            ]
            tilted, outgoing, squares = call(
                step_kernel,
                [tilted_shape, pltpu.HBM(outgoing_shape.shape, outgoing_shape.dtype), squares_shape],
                [codes, factor, *operands],
                step_scratch + map_scratch,
                map_flops,
                MAP_LIMIT,
                in_vmem=(1, 8, 12),
            )
        else:
            mapped, sums = call(
                last_kernel,
                [mapped_shape, sums_shape],
                [squares, *operands],
                map_scratch,
                map_flops,
                MAP_LIMIT,
                in_vmem=(0, 7, 9, 10),
            )

    gathered = lax.all_to_all(sums, "rows", split_axis=0, concat_axis=0, tiled=True)
    totals = jnp.sum(gathered, axis=0).reshape(ITERS, tilt_count)
    states = total_blocks * block_size
    product = jnp.ones((tilt_count,), jnp.float32)
    growth = []
    for j in range(ITERS):
        scale = jnp.sqrt(totals[j] / product / product / states + 1e-06)
        product = product * scale
        growth.append(jnp.log(scale))
    return (mapped / product[:, None], jnp.stack(growth))


def solution(mesh):
    placed = (P("tilt", "rows"), P("rows"), P("tilt"), P(), P("rows", None, None), P("rows", None))
    return jax.shard_map(
        on_device,
        mesh=mesh,
        in_specs=placed,
        out_specs=(P("tilt", "rows"), P(None, "tilt")),
        check_vma=False,
    )
```

```python
import math

import jax
import jax.numpy as jnp
from jax import lax
from jax.experimental import pallas as pl
from jax.experimental.pallas import tpu as pltpu
from jax.sharding import PartitionSpec as P

NEAR = 8
ITERS = 2
PACK_CHUNKS = 8
END_CHUNKS = 4
HALF_WORD = 1 << 16
REQUEST_LIMIT = 62 * 1024 * 1024
PACK_LIMIT = 48 * 1024 * 1024
MAP_LIMIT = 44 * 1024 * 1024


def request_kernel(blocks_here, pattern, codes):
    peers = codes.shape[0]
    slots, rows = pattern.shape
    base = lax.broadcasted_iota(jnp.int32, (peers, rows), 0) * blocks_here
    low = jnp.full((peers, rows), blocks_here, jnp.int32)
    high = jnp.full((peers, rows), -1, jnp.int32)
    for slot in range(NEAR, slots):
        within = pattern[slot : slot + 1, :] - base
        named = (within >= 0) & (within < blocks_here)
        low = jnp.minimum(low, jnp.where(named, within, blocks_here))
        high = jnp.maximum(high, jnp.where(named, within, -1))
    low = jnp.min(low, axis=1, keepdims=True)
    high = jnp.max(high, axis=1, keepdims=True)
    codes[...] = jnp.where(high >= 0, high * HALF_WORD + low, 0)


def start_copy(src, dst, sem):
    copy = pltpu.make_async_copy(src, dst, sem)
    copy.start()
    return copy


def read_words(codes, line, words, sem):
    peers = codes.shape[0]
    across = lax.broadcasted_iota(jnp.int32, (peers, peers), 1)
    same = lax.broadcasted_iota(jnp.int32, (peers, peers), 0) == across
    line[...] = jnp.sum(jnp.where(same, codes[...], 0), axis=0, keepdims=True)
    return start_copy(line, words, sem)


def pack_blocks(words, tilted, staged, outgoing, sems):
    chunk = outgoing.shape[0] // PACK_CHUNKS
    copies = []
    for part in range(PACK_CHUNKS):

        def body(j, carry, part=part):
            word = words[0, part * (chunk // 2) + j]
            staged[part * chunk + 2 * j] = tilted[word & (HALF_WORD - 1)]
            staged[part * chunk + 2 * j + 1] = tilted[lax.shift_right_logical(word, 16)]
            return carry

        lax.fori_loop(0, chunk // 2, body, 0, unroll=8)
        span = pl.ds(part * chunk, chunk)
        copies.append(start_copy(staged.at[span], outgoing.at[span], sems.at[part]))
    return copies


def pack_kernel(codes, tilted, outgoing, line, words, staged, word_sem, sems):
    read_words(codes, line, words, word_sem).wait()
    for copy in pack_blocks(words, tilted, staged, outgoing, sems):
        copy.wait()


def weighted(index, stride, slots, source, weights, gathered, rows, tilts):
    span = rows * tilts
    for n, slot in enumerate(slots):

        def gather(pair, carry, slot=slot, n=n):
            low = source[index[2 * pair * stride + slot]]
            high = source[index[(2 * pair + 1) * stride + slot]]
            at = pl.multiple_of(n * span + pair * 2 * tilts, 2 * tilts)
            gathered[pl.ds(at, 2 * tilts), :] = jnp.concatenate([low, high], axis=0)
            return carry

        lax.fori_loop(0, rows // 2, gather, 0, unroll=True)
    taken = gathered[: len(slots) * span, :]
    product = jnp.dot(taken, weights, preferred_element_type=jnp.float32)
    return product.reshape(len(slots), rows, tilts, weights.shape[1])


def map_blocks(operands, scratch, meanwhile=None):
    near_index, far_index, before, own, after, arrived, kernels, rates = operands
    near_smem, far_smem, extended, far_blocks, rate_buf, gathered, sems = scratch
    kinds = kernels.shape[0]
    (rows, tilts, _), half = own.shape, before.shape[0]
    far_count = rates.shape[0] - NEAR

    first = [
        start_copy(near_index, near_smem, sems.at[0]),
        start_copy(before, extended.at[pl.ds(0, half)], sems.at[1]),
        start_copy(own, extended.at[pl.ds(half, rows)], sems.at[2]),
        start_copy(after, extended.at[pl.ds(half + rows, half)], sems.at[3]),
    ]
    rate_copy = start_copy(rates, rate_buf, sems.at[4])
    late = [
        start_copy(far_index, far_smem, sems.at[5]),
        start_copy(arrived, far_blocks, sems.at[6]),
    ]
    if meanwhile is not None:
        meanwhile()
    for copy in first:
        copy.wait()

    total = None
    for kind in range(kinds):
        slots = range(kind, NEAR, kinds)
        product = weighted(
            near_smem, NEAR, slots, extended, kernels[kind], gathered.at[kind % 2], rows, tilts
        )
        if kind == 0:
            rate_copy.wait()
        for n, slot in enumerate(slots):
            term = product[n] * rate_buf[slot].astype(jnp.float32)[:, None, :]
            total = term if total is None else total + term
    for copy in late:
        copy.wait()
    for kind in range(kinds):
        slots = range(kind, far_count, kinds)
        product = weighted(
            far_smem, far_count, slots, far_blocks, kernels[kind], gathered.at[kind % 2], rows, tilts
        )
        for n, slot in enumerate(slots):
            total = total + product[n] * rate_buf[NEAR + slot].astype(jnp.float32)[:, None, :]
    return total


def sum_of_squares(total):
    return jnp.sum(jnp.sum(total * total, axis=0), axis=1, keepdims=True)


def step_kernel(codes, factor, *refs):
    operands, (tilted, outgoing, squares) = refs[:8], refs[8:11]
    line, words, tilted_buf, staged, pack_sems, sems = refs[11:17]
    decoded = []

    def decode():
        decoded.append(read_words(codes, line, words, sems.at[0]))

    total = map_blocks(operands, refs[17:], decode)
    tilted_buf[...] = (factor[...] * total).astype(jnp.bfloat16)
    copies = [start_copy(tilted_buf, tilted, sems.at[1])]
    decoded[0].wait()
    copies += pack_blocks(words, tilted_buf, staged, outgoing, pack_sems)
    squares[...] = jnp.sum(total * total, axis=0)
    for copy in copies:
        copy.wait()


def last_kernel(first_squares, *refs):
    operands, (mapped, sums) = refs[:8], refs[8:10]
    total = map_blocks(operands, refs[10:])
    for row in range(total.shape[0]):
        mapped[:, row * total.shape[2] : (row + 1) * total.shape[2]] = total[row]
    tilts = total.shape[1]
    across = lax.broadcasted_iota(jnp.int32, (tilts, sums.shape[1]), 1)
    tilt = lax.broadcasted_iota(jnp.int32, (tilts, sums.shape[1]), 0)
    first = jnp.sum(first_squares[...], axis=1, keepdims=True)
    both = jnp.where(across == tilt, first, 0.0) + jnp.where(
        across == tilt + tilts, sum_of_squares(total), 0.0
    )
    sums[...] = jnp.broadcast_to(jnp.sum(both, axis=0, keepdims=True), sums.shape)


def end_kernel(states, sums, mapped, iterate, growth, scaled, sems):
    tilts = mapped.shape[0]
    totals = jnp.sum(sums[...], axis=0, keepdims=True)
    across = lax.broadcasted_iota(jnp.int32, (tilts, sums.shape[1]), 1)
    tilt = lax.broadcasted_iota(jnp.int32, (tilts, sums.shape[1]), 0)
    diagonal = lax.broadcasted_iota(jnp.int32, (tilts, tilts), 0) == lax.broadcasted_iota(
        jnp.int32, (tilts, tilts), 1
    )
    product = jnp.ones((tilts, 1), jnp.float32)
    for j in range(ITERS):
        total = jnp.sum(jnp.where(across == tilt + j * tilts, totals, 0.0), axis=1, keepdims=True)
        scale = jnp.sqrt(total / product / product / states + 1e-06)
        product = product * scale
        growth[j : j + 1, :] = jnp.sum(
            jnp.where(diagonal, jnp.log(scale), 0.0), axis=0, keepdims=True
        )
    inverse = 1.0 / product
    width = mapped.shape[1] // END_CHUNKS
    copies = []
    for part in range(END_CHUNKS):
        span = pl.ds(part * width, width)
        scaled[:, span] = mapped[:, span] * inverse
        copies.append(start_copy(scaled.at[:, span], iterate.at[:, span], sems.at[part]))
    for copy in copies:
        copy.wait()


def call(kernel, outs, arrays, scratch, flops, limit, in_vmem=()):
    spec = [pl.BlockSpec(memory_space=pltpu.VMEM), pl.BlockSpec(memory_space=pl.ANY)]
    moved = sum(math.prod(a.shape) * a.dtype.itemsize for a in (*arrays, *outs))
    return pl.pallas_call(
        kernel,
        out_shape=outs,
        in_specs=[spec[n not in in_vmem] for n in range(len(arrays))],
        out_specs=[spec[len(arrays) + n not in in_vmem] for n in range(len(outs))],
        scratch_shapes=scratch,
        compiler_params=pltpu.CompilerParams(vmem_limit_bytes=limit),
        cost_estimate=pl.CostEstimate(flops=flops, bytes_accessed=moved, transcendentals=0),
    )(*arrays)


def on_device(start, reward, theta, kernels, rates, pattern):
    tilt_count = start.shape[0]
    blocks_here, slot_count = pattern.shape
    kind_count, block_size = kernels.shape[:2]
    peer_count = lax.axis_size("rows")
    position = lax.axis_index("rows")
    total_blocks = blocks_here * peer_count
    far_count = slot_count - NEAR
    half_span = blocks_here // 2
    capacity = 2
    shape = jax.ShapeDtypeStruct
    sem = pltpu.SemaphoreType.DMA

    pattern_by_slot = pattern.T
    (codes,) = call(
        lambda *refs: request_kernel(blocks_here, *refs),
        [shape((peer_count, 1), jnp.int32)],
        [pattern_by_slot],
        [],
        0,
        REQUEST_LIMIT,
        in_vmem=(0, 1),
    )
    codes = lax.all_to_all(codes, "rows", split_axis=0, concat_axis=0, tiled=True)

    far_cols = pattern[:, NEAR:].reshape(-1)
    owners = lax.div(far_cols, blocks_here)
    smaller = (owners[:, None] == owners[None, :]) & (far_cols[None, :] < far_cols[:, None])
    far_index = owners * capacity + jnp.any(smaller, axis=1).astype(jnp.int32)
    local_rows = jnp.arange(blocks_here, dtype=jnp.int32)
    global_rows = position * blocks_here + local_rows
    shifts = (pattern[:, :NEAR] - global_rows[:, None] + half_span) % total_blocks - half_span
    near_index = (local_rows[:, None] + shifts + half_span).reshape(-1)

    up = [(i, (i + 1) % peer_count) for i in range(peer_count)]
    down = [(j, i) for i, j in up]
    rates_by_slot = rates.transpose(1, 0, 2)
    reward = reward.reshape(blocks_here, block_size)

    block = (tilt_count, block_size)
    tilted_shape = shape((blocks_here, *block), jnp.bfloat16)
    outgoing_shape = shape((peer_count * capacity, *block), jnp.bfloat16)
    squares_shape = shape(block, jnp.float32)
    sums_shape = shape((peer_count, ITERS * tilt_count), jnp.float32)
    mapped_shape = shape(start.shape, jnp.float32)
    word_buffers = [pltpu.VMEM((1, peer_count), jnp.int32), pltpu.SMEM((1, peer_count), jnp.int32)]
    staged = pltpu.VMEM(outgoing_shape.shape, jnp.bfloat16)
    gather_rows = max(NEAR, far_count) // kind_count * blocks_here * tilt_count
    map_scratch = [
        pltpu.SMEM(near_index.shape, jnp.int32),
        pltpu.SMEM(far_index.shape, jnp.int32),
        pltpu.VMEM((blocks_here + 2 * half_span, *block), jnp.bfloat16),
        staged,
        pltpu.VMEM(rates_by_slot.shape, jnp.bfloat16),
        pltpu.VMEM((2, gather_rows, block_size), jnp.bfloat16),
        sem((7,)),
    ]
    map_flops = 2 * slot_count * blocks_here * tilt_count * block_size * block_size

    factor = jnp.exp(theta[None, :, None] * reward[:, None, :])
    tilted = factor * start.reshape(tilt_count, blocks_here, block_size).transpose(1, 0, 2)
    tilted = tilted.astype(jnp.bfloat16)
    (outgoing,) = call(
        pack_kernel,
        [pltpu.HBM(outgoing_shape.shape, outgoing_shape.dtype)],
        [codes, tilted],
        [*word_buffers, staged, sem, sem((PACK_CHUNKS,))],
        0,
        PACK_LIMIT,
        in_vmem=(0, 1),
    )
    for iteration in range(ITERS):
        arrived = lax.all_to_all(outgoing, "rows", split_axis=0, concat_axis=0, tiled=True)
        before = lax.ppermute(tilted[blocks_here - half_span :], "rows", up)
        after = lax.ppermute(tilted[:half_span], "rows", down)
        arrived = pltpu.with_memory_space_constraint(arrived, pltpu.HBM)
        rates_hbm = pltpu.with_memory_space_constraint(rates_by_slot, pltpu.HBM)
        if iteration < ITERS - 1:
            before = pltpu.with_memory_space_constraint(before, pltpu.HBM)
            after = pltpu.with_memory_space_constraint(after, pltpu.HBM)
        operands = [near_index, far_index, before, tilted, after, arrived, kernels, rates_hbm]
        if iteration < ITERS - 1:
            step_scratch = [
                *word_buffers,
                pltpu.VMEM(tilted_shape.shape, jnp.bfloat16),
                staged,
                sem((PACK_CHUNKS,)),
                sem((2,)),
            ]
            tilted, outgoing, squares = call(
                step_kernel,
                [tilted_shape, pltpu.HBM(outgoing_shape.shape, outgoing_shape.dtype), squares_shape],
                [codes, factor, *operands],
                step_scratch + map_scratch,
                map_flops,
                MAP_LIMIT,
                in_vmem=(0, 1, 8, 12),
            )
        else:
            mapped, sums = call(
                last_kernel,
                [mapped_shape, sums_shape],
                [squares, *operands],
                map_scratch,
                map_flops,
                MAP_LIMIT,
                in_vmem=(0, 7, 9, 10),
            )

    gathered = lax.all_to_all(sums, "rows", split_axis=0, concat_axis=0, tiled=True)
    states = total_blocks * block_size
    return call(
        lambda *refs: end_kernel(states, *refs),
        [mapped_shape, shape((ITERS, tilt_count), jnp.float32)],
        [gathered, mapped],
        [pltpu.VMEM(start.shape, jnp.float32), sem((END_CHUNKS,))],
        0,
        MAP_LIMIT,
        in_vmem=(0, 1, 3),
    )


def solution(mesh):
    placed = (P("tilt", "rows"), P("rows"), P("tilt"), P(), P("rows", None, None), P("rows", None))
    return jax.shard_map(
        on_device,
        mesh=mesh,
        in_specs=placed,
        out_specs=(P("tilt", "rows"), P(None, "tilt")),
        check_vma=False,
    )
```

```python
import math

import jax
import jax.numpy as jnp
from jax import lax
from jax.experimental import pallas as pl
from jax.experimental.pallas import tpu as pltpu
from jax.sharding import PartitionSpec as P

NEAR = 8
ITERS = 2
PACK_CHUNKS = 8
END_CHUNKS = 4
HALF_WORD = 1 << 16
REQUEST_LIMIT = 62 * 1024 * 1024
PACK_LIMIT = 48 * 1024 * 1024
MAP_LIMIT = 44 * 1024 * 1024


def request_kernel(blocks_here, pattern, codes):
    peers = codes.shape[0]
    slots, rows = pattern.shape
    base = lax.broadcasted_iota(jnp.int32, (peers, rows), 0) * blocks_here
    low = jnp.full((peers, rows), blocks_here, jnp.int32)
    high = jnp.full((peers, rows), -1, jnp.int32)
    for slot in range(NEAR, slots):
        within = pattern[slot : slot + 1, :] - base
        named = (within >= 0) & (within < blocks_here)
        low = jnp.minimum(low, jnp.where(named, within, blocks_here))
        high = jnp.maximum(high, jnp.where(named, within, -1))
    low = jnp.min(low, axis=1, keepdims=True)
    high = jnp.max(high, axis=1, keepdims=True)
    codes[...] = jnp.where(high >= 0, high * HALF_WORD + low, 0)


def start_copy(src, dst, sem):
    copy = pltpu.make_async_copy(src, dst, sem)
    copy.start()
    return copy


def read_words(codes, line, words, sem):
    peers = codes.shape[0]
    across = lax.broadcasted_iota(jnp.int32, (peers, peers), 1)
    same = lax.broadcasted_iota(jnp.int32, (peers, peers), 0) == across
    line[...] = jnp.sum(jnp.where(same, codes[...], 0), axis=0, keepdims=True)
    return start_copy(line, words, sem)


def pack_blocks(words, tilted, staged, outgoing, sems):
    chunk = outgoing.shape[0] // PACK_CHUNKS
    copies = []
    for part in range(PACK_CHUNKS):

        def body(j, carry, part=part):
            word = words[0, part * (chunk // 2) + j]
            staged[part * chunk + 2 * j] = tilted[word & (HALF_WORD - 1)]
            staged[part * chunk + 2 * j + 1] = tilted[lax.shift_right_logical(word, 16)]
            return carry

        lax.fori_loop(0, chunk // 2, body, 0, unroll=8)
        span = pl.ds(part * chunk, chunk)
        copies.append(start_copy(staged.at[span], outgoing.at[span], sems.at[part]))
    return copies


def pack_kernel(codes, tilted, outgoing, line, words, staged, word_sem, sems):
    read_words(codes, line, words, word_sem).wait()
    for copy in pack_blocks(words, tilted, staged, outgoing, sems):
        copy.wait()


def weighted(index, stride, slots, source, weights, gathered, rows, tilts):
    span = rows * tilts
    for n, slot in enumerate(slots):

        def gather(pair, carry, slot=slot, n=n):
            low = source[index[2 * pair * stride + slot]]
            high = source[index[(2 * pair + 1) * stride + slot]]
            at = pl.multiple_of(n * span + pair * 2 * tilts, 2 * tilts)
            gathered[pl.ds(at, 2 * tilts), :] = jnp.concatenate([low, high], axis=0)
            return carry

        lax.fori_loop(0, rows // 2, gather, 0, unroll=True)
    taken = gathered[: len(slots) * span, :]
    product = jnp.dot(taken, weights, preferred_element_type=jnp.float32)
    return product.reshape(len(slots), rows, tilts, weights.shape[1])


def near_sum(index, first_row, source, kernels, rates, gathered, rows, before_first_use=None):
    kinds, tilts = kernels.shape[0], source.shape[1]
    total = None
    for kind in range(kinds):
        slots = range(kind, NEAR, kinds)
        product = weighted(
            index, NEAR, slots, source, kernels[kind], gathered.at[kind % 2], rows, tilts
        )
        if kind == 0 and before_first_use is not None:
            before_first_use.wait()
        for n, slot in enumerate(slots):
            rate = rates[slot, first_row : first_row + rows, :].astype(jnp.float32)
            term = product[n] * rate[:, None, :]
            total = term if total is None else total + term
    return total


def upper_kernel(index, own, after, kernels, rates, out, *scratch):
    index_smem, extended, rate_buf, out_buf, gathered, sems = scratch
    rows, half = own.shape[0], after.shape[0]
    copies = [
        start_copy(index, index_smem, sems.at[0]),
        start_copy(own, extended.at[pl.ds(0, rows)], sems.at[1]),
        start_copy(after, extended.at[pl.ds(rows, half)], sems.at[2]),
    ]
    rate_copy = start_copy(rates.at[pl.ds(0, NEAR)], rate_buf, sems.at[3])
    for copy in copies:
        copy.wait()
    out_buf[...] = near_sum(
        index_smem, rows - half, extended, kernels, rate_buf, gathered, half, rate_copy
    )
    start_copy(out_buf, out, sems.at[4]).wait()


def map_blocks(operands, scratch, meanwhile=None):
    near_index, far_index, before, own, upper, arrived, kernels, rates = operands
    near_smem, far_smem, extended, far_blocks, rate_buf, upper_buf, gathered, sems = scratch
    kinds = kernels.shape[0]
    (rows, tilts, _), half = own.shape, before.shape[0]
    far_count = rates.shape[0] - NEAR

    first = [
        start_copy(near_index, near_smem, sems.at[0]),
        start_copy(before, extended.at[pl.ds(0, half)], sems.at[1]),
        start_copy(own, extended.at[pl.ds(half, rows)], sems.at[2]),
    ]
    rate_copy = start_copy(rates, rate_buf, sems.at[3])
    late = [
        start_copy(far_index, far_smem, sems.at[4]),
        start_copy(upper, upper_buf, sems.at[5]),
        start_copy(arrived, far_blocks, sems.at[6]),
    ]
    if meanwhile is not None:
        meanwhile()
    for copy in first:
        copy.wait()

    lower = near_sum(near_smem, 0, extended, kernels, rate_buf, gathered, half, rate_copy)
    for copy in late:
        copy.wait()
    total = jnp.concatenate([lower, upper_buf[...]], axis=0)
    for kind in range(kinds):
        slots = range(kind, far_count, kinds)
        product = weighted(
            far_smem, far_count, slots, far_blocks, kernels[kind], gathered.at[kind % 2], rows, tilts
        )
        for n, slot in enumerate(slots):
            total = total + product[n] * rate_buf[NEAR + slot].astype(jnp.float32)[:, None, :]
    return total


def sum_of_squares(total):
    return jnp.sum(jnp.sum(total * total, axis=0), axis=1, keepdims=True)


def step_kernel(codes, factor, *refs):
    operands, (tilted, outgoing, squares) = refs[:8], refs[8:11]
    line, words, tilted_buf, staged, pack_sems, sems = refs[11:17]
    decoded = []

    def decode():
        decoded.append(read_words(codes, line, words, sems.at[0]))

    total = map_blocks(operands, refs[17:], decode)
    tilted_buf[...] = (factor[...] * total).astype(jnp.bfloat16)
    copies = [start_copy(tilted_buf, tilted, sems.at[1])]
    decoded[0].wait()
    copies += pack_blocks(words, tilted_buf, staged, outgoing, pack_sems)
    squares[...] = jnp.sum(total * total, axis=0)
    for copy in copies:
        copy.wait()


def last_kernel(first_squares, *refs):
    operands, (mapped, sums) = refs[:8], refs[8:10]
    total = map_blocks(operands, refs[10:])
    for row in range(total.shape[0]):
        mapped[:, row * total.shape[2] : (row + 1) * total.shape[2]] = total[row]
    tilts = total.shape[1]
    across = lax.broadcasted_iota(jnp.int32, (tilts, sums.shape[1]), 1)
    tilt = lax.broadcasted_iota(jnp.int32, (tilts, sums.shape[1]), 0)
    first = jnp.sum(first_squares[...], axis=1, keepdims=True)
    both = jnp.where(across == tilt, first, 0.0) + jnp.where(
        across == tilt + tilts, sum_of_squares(total), 0.0
    )
    sums[...] = jnp.broadcast_to(jnp.sum(both, axis=0, keepdims=True), sums.shape)


def end_kernel(states, sums, mapped, iterate, growth, scaled, sems):
    tilts = mapped.shape[0]
    totals = jnp.sum(sums[...], axis=0, keepdims=True)
    across = lax.broadcasted_iota(jnp.int32, (tilts, sums.shape[1]), 1)
    tilt = lax.broadcasted_iota(jnp.int32, (tilts, sums.shape[1]), 0)
    diagonal = lax.broadcasted_iota(jnp.int32, (tilts, tilts), 0) == lax.broadcasted_iota(
        jnp.int32, (tilts, tilts), 1
    )
    product = jnp.ones((tilts, 1), jnp.float32)
    for j in range(ITERS):
        total = jnp.sum(jnp.where(across == tilt + j * tilts, totals, 0.0), axis=1, keepdims=True)
        scale = jnp.sqrt(total / product / product / states + 1e-06)
        product = product * scale
        growth[j : j + 1, :] = jnp.sum(
            jnp.where(diagonal, jnp.log(scale), 0.0), axis=0, keepdims=True
        )
    inverse = 1.0 / product
    width = mapped.shape[1] // END_CHUNKS
    copies = []
    for part in range(END_CHUNKS):
        span = pl.ds(part * width, width)
        scaled[:, span] = mapped[:, span] * inverse
        copies.append(start_copy(scaled.at[:, span], iterate.at[:, span], sems.at[part]))
    for copy in copies:
        copy.wait()


def call(kernel, outs, arrays, scratch, flops, limit, in_vmem=()):
    spec = [pl.BlockSpec(memory_space=pltpu.VMEM), pl.BlockSpec(memory_space=pl.ANY)]
    moved = sum(math.prod(a.shape) * a.dtype.itemsize for a in (*arrays, *outs))
    return pl.pallas_call(
        kernel,
        out_shape=outs,
        in_specs=[spec[n not in in_vmem] for n in range(len(arrays))],
        out_specs=[spec[len(arrays) + n not in in_vmem] for n in range(len(outs))],
        scratch_shapes=scratch,
        compiler_params=pltpu.CompilerParams(vmem_limit_bytes=limit),
        cost_estimate=pl.CostEstimate(flops=flops, bytes_accessed=moved, transcendentals=0),
    )(*arrays)


def on_device(start, reward, theta, kernels, rates, pattern):
    tilt_count = start.shape[0]
    blocks_here, slot_count = pattern.shape
    kind_count, block_size = kernels.shape[:2]
    peer_count = lax.axis_size("rows")
    position = lax.axis_index("rows")
    total_blocks = blocks_here * peer_count
    far_count = slot_count - NEAR
    half_span = blocks_here // 2
    capacity = 2
    shape = jax.ShapeDtypeStruct
    sem = pltpu.SemaphoreType.DMA

    pattern_by_slot = pattern.T
    (codes,) = call(
        lambda *refs: request_kernel(blocks_here, *refs),
        [shape((peer_count, 1), jnp.int32)],
        [pattern_by_slot],
        [],
        0,
        REQUEST_LIMIT,
        in_vmem=(0, 1),
    )
    codes = lax.all_to_all(codes, "rows", split_axis=0, concat_axis=0, tiled=True)

    far_cols = pattern[:, NEAR:].reshape(-1)
    owners = lax.div(far_cols, blocks_here)
    smaller = (owners[:, None] == owners[None, :]) & (far_cols[None, :] < far_cols[:, None])
    far_index = owners * capacity + jnp.any(smaller, axis=1).astype(jnp.int32)
    local_rows = jnp.arange(blocks_here, dtype=jnp.int32)
    global_rows = position * blocks_here + local_rows
    shifts = (pattern[:, :NEAR] - global_rows[:, None] + half_span) % total_blocks - half_span
    near_index = local_rows[:, None] + shifts + half_span
    lower_index = near_index[:half_span].reshape(-1)
    upper_index = near_index[half_span:].reshape(-1) - half_span

    up = [(i, (i + 1) % peer_count) for i in range(peer_count)]
    down = [(j, i) for i, j in up]
    rates_by_slot = rates.transpose(1, 0, 2)
    reward = reward.reshape(blocks_here, block_size)

    block = (tilt_count, block_size)
    tilted_shape = shape((blocks_here, *block), jnp.bfloat16)
    outgoing_shape = shape((peer_count * capacity, *block), jnp.bfloat16)
    squares_shape = shape(block, jnp.float32)
    sums_shape = shape((peer_count, ITERS * tilt_count), jnp.float32)
    mapped_shape = shape(start.shape, jnp.float32)
    word_buffers = [pltpu.VMEM((1, peer_count), jnp.int32), pltpu.SMEM((1, peer_count), jnp.int32)]
    staged = pltpu.VMEM(outgoing_shape.shape, jnp.bfloat16)
    upper_shape = shape((half_span, *block), jnp.float32)
    reach = pltpu.VMEM((blocks_here + half_span, *block), jnp.bfloat16)
    near_rows = NEAR // kind_count * half_span * tilt_count
    far_rows = far_count // kind_count * blocks_here * tilt_count
    gathered = pltpu.VMEM((2, max(near_rows, far_rows), block_size), jnp.bfloat16)
    upper_scratch = [
        pltpu.SMEM(upper_index.shape, jnp.int32),
        reach,
        pltpu.VMEM((NEAR, blocks_here, block_size), jnp.bfloat16),
        pltpu.VMEM(upper_shape.shape, jnp.float32),
        gathered,
        sem((5,)),
    ]
    map_scratch = [
        pltpu.SMEM(lower_index.shape, jnp.int32),
        pltpu.SMEM(far_index.shape, jnp.int32),
        reach,
        staged,
        pltpu.VMEM(rates_by_slot.shape, jnp.bfloat16),
        pltpu.VMEM(upper_shape.shape, jnp.float32),
        gathered,
        sem((7,)),
    ]
    slot_flops = 2 * blocks_here * tilt_count * block_size * block_size
    upper_flops = NEAR * slot_flops // 2
    map_flops = slot_count * slot_flops - upper_flops

    factor = jnp.exp(theta[None, :, None] * reward[:, None, :])
    tilted = factor * start.reshape(tilt_count, blocks_here, block_size).transpose(1, 0, 2)
    tilted = tilted.astype(jnp.bfloat16)
    (outgoing,) = call(
        pack_kernel,
        [pltpu.HBM(outgoing_shape.shape, outgoing_shape.dtype)],
        [codes, tilted],
        [*word_buffers, staged, sem, sem((PACK_CHUNKS,))],
        0,
        PACK_LIMIT,
        in_vmem=(0, 1),
    )
    for iteration in range(ITERS):
        arrived = lax.all_to_all(outgoing, "rows", split_axis=0, concat_axis=0, tiled=True)
        before = lax.ppermute(tilted[blocks_here - half_span :], "rows", up)
        after = lax.ppermute(tilted[:half_span], "rows", down)
        arrived = pltpu.with_memory_space_constraint(arrived, pltpu.HBM)
        rates_hbm = pltpu.with_memory_space_constraint(rates_by_slot, pltpu.HBM)
        if iteration < ITERS - 1:
            before = pltpu.with_memory_space_constraint(before, pltpu.HBM)
        (upper,) = call(
            upper_kernel,
            [pltpu.HBM(upper_shape.shape, upper_shape.dtype)],
            [upper_index, tilted, after, kernels, rates_hbm],
            upper_scratch,
            upper_flops,
            MAP_LIMIT,
            in_vmem=(3,),
        )
        upper = pltpu.with_memory_space_constraint(upper, pltpu.HBM)
        operands = [lower_index, far_index, before, tilted, upper, arrived, kernels, rates_hbm]
        if iteration < ITERS - 1:
            step_scratch = [
                *word_buffers,
                pltpu.VMEM(tilted_shape.shape, jnp.bfloat16),
                staged,
                sem((PACK_CHUNKS,)),
                sem((2,)),
            ]
            tilted, outgoing, squares = call(
                step_kernel,
                [tilted_shape, pltpu.HBM(outgoing_shape.shape, outgoing_shape.dtype), squares_shape],
                [codes, factor, *operands],
                step_scratch + map_scratch,
                map_flops,
                MAP_LIMIT,
                in_vmem=(0, 1, 8, 12),
            )
        else:
            mapped, sums = call(
                last_kernel,
                [mapped_shape, sums_shape],
                [squares, *operands],
                map_scratch,
                map_flops,
                MAP_LIMIT,
                in_vmem=(0, 7, 9, 10),
            )

    gathered = lax.all_to_all(sums, "rows", split_axis=0, concat_axis=0, tiled=True)
    states = total_blocks * block_size
    return call(
        lambda *refs: end_kernel(states, *refs),
        [mapped_shape, shape((ITERS, tilt_count), jnp.float32)],
        [gathered, mapped],
        [pltpu.VMEM(start.shape, jnp.float32), sem((END_CHUNKS,))],
        0,
        MAP_LIMIT,
        in_vmem=(0, 1, 3),
    )


def solution(mesh):
    placed = (P("tilt", "rows"), P("rows"), P("tilt"), P(), P("rows", None, None), P("rows", None))
    return jax.shard_map(
        on_device,
        mesh=mesh,
        in_specs=placed,
        out_specs=(P("tilt", "rows"), P(None, "tilt")),
        check_vma=False,
    )
```

```python
import math

import jax
import jax.numpy as jnp
from jax import lax
from jax.experimental import pallas as pl
from jax.experimental.pallas import tpu as pltpu
from jax.sharding import PartitionSpec as P

NEAR = 8
ITERS = 2
PACK_CHUNKS = 8
END_CHUNKS = 4
HALF_WORD = 1 << 16
REQUEST_LIMIT = 62 * 1024 * 1024
PACK_LIMIT = 48 * 1024 * 1024
MAP_LIMIT = 44 * 1024 * 1024


def request_kernel(blocks_here, pattern, codes):
    peers = codes.shape[0]
    slots, rows = pattern.shape
    base = lax.broadcasted_iota(jnp.int32, (peers, rows), 0) * blocks_here
    low = jnp.full((peers, rows), blocks_here, jnp.int32)
    high = jnp.full((peers, rows), -1, jnp.int32)
    for slot in range(NEAR, slots):
        within = pattern[slot : slot + 1, :] - base
        named = (within >= 0) & (within < blocks_here)
        low = jnp.minimum(low, jnp.where(named, within, blocks_here))
        high = jnp.maximum(high, jnp.where(named, within, -1))
    low = jnp.min(low, axis=1, keepdims=True)
    high = jnp.max(high, axis=1, keepdims=True)
    codes[...] = jnp.where(high >= 0, high * HALF_WORD + low, 0)


def start_copy(src, dst, sem):
    copy = pltpu.make_async_copy(src, dst, sem)
    copy.start()
    return copy


def read_words(codes, line, words, sem):
    peers = codes.shape[0]
    across = lax.broadcasted_iota(jnp.int32, (peers, peers), 1)
    same = lax.broadcasted_iota(jnp.int32, (peers, peers), 0) == across
    line[...] = jnp.sum(jnp.where(same, codes[...], 0), axis=0, keepdims=True)
    return start_copy(line, words, sem)


def pack_blocks(words, tilted, staged, outgoing, sems):
    chunk = outgoing.shape[0] // PACK_CHUNKS
    copies = []
    for part in range(PACK_CHUNKS):

        def body(j, carry, part=part):
            word = words[0, part * (chunk // 2) + j]
            staged[part * chunk + 2 * j] = tilted[word & (HALF_WORD - 1)]
            staged[part * chunk + 2 * j + 1] = tilted[lax.shift_right_logical(word, 16)]
            return carry

        lax.fori_loop(0, chunk // 2, body, 0, unroll=8)
        span = pl.ds(part * chunk, chunk)
        copies.append(start_copy(staged.at[span], outgoing.at[span], sems.at[part]))
    return copies


def pack_kernel(codes, tilted, outgoing, line, words, staged, word_sem, sems):
    read_words(codes, line, words, word_sem).wait()
    for copy in pack_blocks(words, tilted, staged, outgoing, sems):
        copy.wait()


def weighted(index, stride, slots, source, weights, gathered, rows, tilts):
    span = rows * tilts
    for n, slot in enumerate(slots):

        def gather(pair, carry, slot=slot, n=n):
            low = source[index[2 * pair * stride + slot]]
            high = source[index[(2 * pair + 1) * stride + slot]]
            at = pl.multiple_of(n * span + pair * 2 * tilts, 2 * tilts)
            gathered[pl.ds(at, 2 * tilts), :] = jnp.concatenate([low, high], axis=0)
            return carry

        lax.fori_loop(0, rows // 2, gather, 0, unroll=True)
    taken = gathered[: len(slots) * span, :]
    product = jnp.dot(taken, weights, preferred_element_type=jnp.float32)
    return product.reshape(len(slots), rows, tilts, weights.shape[1])


def near_sum(index, source, kernels, rates, gathered, rows, before_first_use=None):
    kinds, tilts, size = kernels.shape[0], source.shape[1], source.shape[2]
    upper = jnp.full((rows, size), index[rows * NEAR]) > 0
    total = None
    for kind in range(kinds):
        slots = range(kind, NEAR, kinds)
        product = weighted(
            index, NEAR, slots, source, kernels[kind], gathered.at[kind % 2], rows, tilts
        )
        if kind == 0 and before_first_use is not None:
            before_first_use.wait()
        for n, slot in enumerate(slots):
            rate = rates[slot].astype(jnp.float32)
            rate = jnp.where(upper, rate[rows:], rate[:rows])
            term = product[n] * rate[:, None, :]
            total = term if total is None else total + term
    return total


def early_kernel(index, own, halo, kernels, rates, out, *scratch):
    index_smem, extended, rate_buf, out_buf, gathered, sems = scratch
    rows, half = own.shape[0], halo.shape[0]
    copies = [
        start_copy(index, index_smem, sems.at[0]),
        start_copy(own, extended.at[pl.ds(0, rows)], sems.at[1]),
        start_copy(halo, extended.at[pl.ds(rows, half)], sems.at[2]),
    ]
    rate_copy = start_copy(rates.at[pl.ds(0, NEAR)], rate_buf, sems.at[3])
    for copy in copies:
        copy.wait()
    out_buf[...] = near_sum(index_smem, extended, kernels, rate_buf, gathered, half, rate_copy)
    start_copy(out_buf, out, sems.at[4]).wait()


def map_blocks(operands, scratch, meanwhile=None):
    near_index, far_index, halo, own, early, arrived, kernels, rates = operands
    near_smem, far_smem, extended, far_blocks, rate_buf, early_buf, gathered, sems = scratch
    kinds = kernels.shape[0]
    (rows, tilts, size), half = own.shape, halo.shape[0]
    far_count = rates.shape[0] - NEAR

    first = [
        start_copy(near_index, near_smem, sems.at[0]),
        start_copy(own, extended.at[pl.ds(0, rows)], sems.at[1]),
        start_copy(halo, extended.at[pl.ds(rows, half)], sems.at[2]),
    ]
    rate_copy = start_copy(rates, rate_buf, sems.at[3])
    late = [
        start_copy(far_index, far_smem, sems.at[4]),
        start_copy(early, early_buf, sems.at[5]),
        start_copy(arrived, far_blocks, sems.at[6]),
    ]
    if meanwhile is not None:
        meanwhile()
    for copy in first:
        copy.wait()

    here = near_sum(near_smem, extended, kernels, rate_buf, gathered, half, rate_copy)
    for copy in late:
        copy.wait()
    upper = jnp.full((half, tilts, size), near_smem[half * NEAR]) > 0
    other = early_buf[...]
    total = jnp.concatenate([jnp.where(upper, other, here), jnp.where(upper, here, other)], axis=0)
    for kind in range(kinds):
        slots = range(kind, far_count, kinds)
        product = weighted(
            far_smem, far_count, slots, far_blocks, kernels[kind], gathered.at[kind % 2], rows, tilts
        )
        for n, slot in enumerate(slots):
            total = total + product[n] * rate_buf[NEAR + slot].astype(jnp.float32)[:, None, :]
    return total


def sum_of_squares(total):
    return jnp.sum(jnp.sum(total * total, axis=0), axis=1, keepdims=True)


def step_kernel(codes, factor, *refs):
    operands, (tilted, outgoing, squares) = refs[:8], refs[8:11]
    line, words, tilted_buf, staged, pack_sems, sems = refs[11:17]
    decoded = []

    def decode():
        decoded.append(read_words(codes, line, words, sems.at[0]))

    total = map_blocks(operands, refs[17:], decode)
    tilted_buf[...] = (factor[...] * total).astype(jnp.bfloat16)
    copies = [start_copy(tilted_buf, tilted, sems.at[1])]
    decoded[0].wait()
    copies += pack_blocks(words, tilted_buf, staged, outgoing, pack_sems)
    squares[...] = jnp.sum(total * total, axis=0)
    for copy in copies:
        copy.wait()


def last_kernel(first_squares, *refs):
    operands, (mapped, sums) = refs[:8], refs[8:10]
    total = map_blocks(operands, refs[10:])
    for row in range(total.shape[0]):
        mapped[:, row * total.shape[2] : (row + 1) * total.shape[2]] = total[row]
    tilts = total.shape[1]
    across = lax.broadcasted_iota(jnp.int32, (tilts, sums.shape[1]), 1)
    tilt = lax.broadcasted_iota(jnp.int32, (tilts, sums.shape[1]), 0)
    first = jnp.sum(first_squares[...], axis=1, keepdims=True)
    both = jnp.where(across == tilt, first, 0.0) + jnp.where(
        across == tilt + tilts, sum_of_squares(total), 0.0
    )
    sums[...] = jnp.broadcast_to(jnp.sum(both, axis=0, keepdims=True), sums.shape)


def end_kernel(states, sums, mapped, iterate, growth, scaled, sems):
    tilts = mapped.shape[0]
    totals = jnp.sum(sums[...], axis=0, keepdims=True)
    across = lax.broadcasted_iota(jnp.int32, (tilts, sums.shape[1]), 1)
    tilt = lax.broadcasted_iota(jnp.int32, (tilts, sums.shape[1]), 0)
    diagonal = lax.broadcasted_iota(jnp.int32, (tilts, tilts), 0) == lax.broadcasted_iota(
        jnp.int32, (tilts, tilts), 1
    )
    product = jnp.ones((tilts, 1), jnp.float32)
    for j in range(ITERS):
        total = jnp.sum(jnp.where(across == tilt + j * tilts, totals, 0.0), axis=1, keepdims=True)
        scale = jnp.sqrt(total / product / product / states + 1e-06)
        product = product * scale
        growth[j : j + 1, :] = jnp.sum(
            jnp.where(diagonal, jnp.log(scale), 0.0), axis=0, keepdims=True
        )
    inverse = 1.0 / product
    width = mapped.shape[1] // END_CHUNKS
    copies = []
    for part in range(END_CHUNKS):
        span = pl.ds(part * width, width)
        scaled[:, span] = mapped[:, span] * inverse
        copies.append(start_copy(scaled.at[:, span], iterate.at[:, span], sems.at[part]))
    for copy in copies:
        copy.wait()


def call(kernel, outs, arrays, scratch, flops, limit, in_vmem=()):
    spec = [pl.BlockSpec(memory_space=pltpu.VMEM), pl.BlockSpec(memory_space=pl.ANY)]
    moved = sum(math.prod(a.shape) * a.dtype.itemsize for a in (*arrays, *outs))
    return pl.pallas_call(
        kernel,
        out_shape=outs,
        in_specs=[spec[n not in in_vmem] for n in range(len(arrays))],
        out_specs=[spec[len(arrays) + n not in in_vmem] for n in range(len(outs))],
        scratch_shapes=scratch,
        compiler_params=pltpu.CompilerParams(vmem_limit_bytes=limit),
        cost_estimate=pl.CostEstimate(flops=flops, bytes_accessed=moved, transcendentals=0),
    )(*arrays)


def on_device(start, reward, theta, kernels, rates, pattern):
    tilt_count = start.shape[0]
    blocks_here, slot_count = pattern.shape
    kind_count, block_size = kernels.shape[:2]
    peer_count = lax.axis_size("rows")
    position = lax.axis_index("rows")
    total_blocks = blocks_here * peer_count
    far_count = slot_count - NEAR
    half_span = blocks_here // 2
    capacity = 2
    shape = jax.ShapeDtypeStruct
    sem = pltpu.SemaphoreType.DMA

    pattern_by_slot = pattern.T
    (codes,) = call(
        lambda *refs: request_kernel(blocks_here, *refs),
        [shape((peer_count, 1), jnp.int32)],
        [pattern_by_slot],
        [],
        0,
        REQUEST_LIMIT,
        in_vmem=(0, 1),
    )
    codes = lax.all_to_all(codes, "rows", split_axis=0, concat_axis=0, tiled=True)

    far_cols = pattern[:, NEAR:].reshape(-1)
    owners = lax.div(far_cols, blocks_here)
    smaller = (owners[:, None] == owners[None, :]) & (far_cols[None, :] < far_cols[:, None])
    far_index = owners * capacity + jnp.any(smaller, axis=1).astype(jnp.int32)
    local_rows = jnp.arange(blocks_here, dtype=jnp.int32)
    global_rows = position * blocks_here + local_rows
    shifts = (pattern[:, :NEAR] - global_rows[:, None] + half_span) % total_blocks - half_span
    reached = local_rows[:, None] + shifts
    reached = jnp.where(reached < 0, reached + blocks_here + half_span, reached)

    odd = position % 2
    early_first = half_span * (1 - odd)

    def half_index(start_row):
        entries = lax.dynamic_slice(reached, (start_row, 0), (half_span, NEAR)).reshape(-1)
        return jnp.concatenate([entries, start_row[None]])

    early_index = half_index(early_first)
    late_index = half_index(half_span - early_first)
    on_chip = [(i, i + 1 - 2 * (i % 2)) for i in range(peer_count)]
    off_chip = [(i, (i - 1 + 2 * (i % 2)) % peer_count) for i in range(peer_count)]
    rates_by_slot = rates.transpose(1, 0, 2)
    reward = reward.reshape(blocks_here, block_size)

    block = (tilt_count, block_size)
    tilted_shape = shape((blocks_here, *block), jnp.bfloat16)
    outgoing_shape = shape((peer_count * capacity, *block), jnp.bfloat16)
    squares_shape = shape(block, jnp.float32)
    sums_shape = shape((peer_count, ITERS * tilt_count), jnp.float32)
    mapped_shape = shape(start.shape, jnp.float32)
    word_buffers = [pltpu.VMEM((1, peer_count), jnp.int32), pltpu.SMEM((1, peer_count), jnp.int32)]
    staged = pltpu.VMEM(outgoing_shape.shape, jnp.bfloat16)
    early_shape = shape((half_span, *block), jnp.float32)
    reach = pltpu.VMEM((blocks_here + half_span, *block), jnp.bfloat16)
    near_rows = NEAR // kind_count * half_span * tilt_count
    far_rows = far_count // kind_count * blocks_here * tilt_count
    gathered = pltpu.VMEM((2, max(near_rows, far_rows), block_size), jnp.bfloat16)
    early_scratch = [
        pltpu.SMEM(early_index.shape, jnp.int32),
        reach,
        pltpu.VMEM((NEAR, blocks_here, block_size), jnp.bfloat16),
        pltpu.VMEM(early_shape.shape, jnp.float32),
        gathered,
        sem((5,)),
    ]
    map_scratch = [
        pltpu.SMEM(late_index.shape, jnp.int32),
        pltpu.SMEM(far_index.shape, jnp.int32),
        reach,
        staged,
        pltpu.VMEM(rates_by_slot.shape, jnp.bfloat16),
        pltpu.VMEM(early_shape.shape, jnp.float32),
        gathered,
        sem((7,)),
    ]
    slot_flops = 2 * blocks_here * tilt_count * block_size * block_size
    early_flops = NEAR * slot_flops // 2
    map_flops = slot_count * slot_flops - early_flops

    factor = jnp.exp(theta[None, :, None] * reward[:, None, :])
    tilted = factor * start.reshape(tilt_count, blocks_here, block_size).transpose(1, 0, 2)
    tilted = tilted.astype(jnp.bfloat16)
    (outgoing,) = call(
        pack_kernel,
        [pltpu.HBM(outgoing_shape.shape, outgoing_shape.dtype)],
        [codes, tilted],
        [*word_buffers, staged, sem, sem((PACK_CHUNKS,))],
        0,
        PACK_LIMIT,
        in_vmem=(0, 1),
    )
    for iteration in range(ITERS):
        arrived = lax.all_to_all(outgoing, "rows", split_axis=0, concat_axis=0, tiled=True)
        head, tail = tilted[:half_span], tilted[blocks_here - half_span :]
        near_halo = lax.ppermute(jnp.where(odd, head, tail), "rows", on_chip)
        far_halo = lax.ppermute(jnp.where(odd, tail, head), "rows", off_chip)
        arrived = pltpu.with_memory_space_constraint(arrived, pltpu.HBM)
        rates_hbm = pltpu.with_memory_space_constraint(rates_by_slot, pltpu.HBM)
        if iteration < ITERS - 1:
            far_halo = pltpu.with_memory_space_constraint(far_halo, pltpu.HBM)
        (early,) = call(
            early_kernel,
            [pltpu.HBM(early_shape.shape, early_shape.dtype)],
            [early_index, tilted, near_halo, kernels, rates_hbm],
            early_scratch,
            early_flops,
            MAP_LIMIT,
            in_vmem=(3,),
        )
        early = pltpu.with_memory_space_constraint(early, pltpu.HBM)
        operands = [late_index, far_index, far_halo, tilted, early, arrived, kernels, rates_hbm]
        if iteration < ITERS - 1:
            step_scratch = [
                *word_buffers,
                pltpu.VMEM(tilted_shape.shape, jnp.bfloat16),
                staged,
                sem((PACK_CHUNKS,)),
                sem((2,)),
            ]
            tilted, outgoing, squares = call(
                step_kernel,
                [tilted_shape, pltpu.HBM(outgoing_shape.shape, outgoing_shape.dtype), squares_shape],
                [codes, factor, *operands],
                step_scratch + map_scratch,
                map_flops,
                MAP_LIMIT,
                in_vmem=(0, 1, 8, 12),
            )
        else:
            mapped, sums = call(
                last_kernel,
                [mapped_shape, sums_shape],
                [squares, *operands],
                map_scratch,
                map_flops,
                MAP_LIMIT,
                in_vmem=(0, 7, 9, 10),
            )

    gathered = lax.all_to_all(sums, "rows", split_axis=0, concat_axis=0, tiled=True)
    states = total_blocks * block_size
    return call(
        lambda *refs: end_kernel(states, *refs),
        [mapped_shape, shape((ITERS, tilt_count), jnp.float32)],
        [gathered, mapped],
        [pltpu.VMEM(start.shape, jnp.float32), sem((END_CHUNKS,))],
        0,
        MAP_LIMIT,
        in_vmem=(0, 1, 3),
    )


def solution(mesh):
    placed = (P("tilt", "rows"), P("rows"), P("tilt"), P(), P("rows", None, None), P("rows", None))
    return jax.shard_map(
        on_device,
        mesh=mesh,
        in_specs=placed,
        out_specs=(P("tilt", "rows"), P(None, "tilt")),
        check_vma=False,
    )
```

```python
import math

import jax
import jax.numpy as jnp
from jax import lax
from jax.experimental import pallas as pl
from jax.experimental.pallas import tpu as pltpu
from jax.sharding import PartitionSpec as P

NEAR = 8
ITERS = 2
PACK_CHUNKS = 8
END_CHUNKS = 4
HALF_WORD = 1 << 16
REQUEST_LIMIT = 62 * 1024 * 1024
PACK_LIMIT = 48 * 1024 * 1024
MAP_LIMIT = 44 * 1024 * 1024


def request_kernel(blocks_here, pattern, codes):
    peers = codes.shape[0]
    slots, rows = pattern.shape
    base = lax.broadcasted_iota(jnp.int32, (peers, rows), 0) * blocks_here
    low = jnp.full((peers, rows), blocks_here, jnp.int32)
    high = jnp.full((peers, rows), -1, jnp.int32)
    for slot in range(NEAR, slots):
        within = pattern[slot : slot + 1, :] - base
        named = (within >= 0) & (within < blocks_here)
        low = jnp.minimum(low, jnp.where(named, within, blocks_here))
        high = jnp.maximum(high, jnp.where(named, within, -1))
    low = jnp.min(low, axis=1, keepdims=True)
    high = jnp.max(high, axis=1, keepdims=True)
    codes[...] = jnp.where(high >= 0, high * HALF_WORD + low, 0)


def start_copy(src, dst, sem):
    copy = pltpu.make_async_copy(src, dst, sem)
    copy.start()
    return copy


def read_words(codes, line, words, sem):
    peers = codes.shape[0]
    across = lax.broadcasted_iota(jnp.int32, (peers, peers), 1)
    same = lax.broadcasted_iota(jnp.int32, (peers, peers), 0) == across
    line[...] = jnp.sum(jnp.where(same, codes[...], 0), axis=0, keepdims=True)
    return start_copy(line, words, sem)


def pack_blocks(words, tilted, staged, outgoing, sems):
    chunk = outgoing.shape[0] // PACK_CHUNKS
    copies = []
    for part in range(PACK_CHUNKS):

        def body(j, carry, part=part):
            word = words[0, part * (chunk // 2) + j]
            staged[part * chunk + 2 * j] = tilted[word & (HALF_WORD - 1)]
            staged[part * chunk + 2 * j + 1] = tilted[lax.shift_right_logical(word, 16)]
            return carry

        lax.fori_loop(0, chunk // 2, body, 0, unroll=8)
        span = pl.ds(part * chunk, chunk)
        copies.append(start_copy(staged.at[span], outgoing.at[span], sems.at[part]))
    return copies


def pack_kernel(codes, tilted, outgoing, line, words, staged, word_sem, sems):
    read_words(codes, line, words, word_sem).wait()
    for copy in pack_blocks(words, tilted, staged, outgoing, sems):
        copy.wait()


def weighted(index, stride, slots, source, weights, gathered, rows, tilts):
    span = rows * tilts
    for n, slot in enumerate(slots):

        def gather(pair, carry, slot=slot, n=n):
            low = source[index[2 * pair * stride + slot]]
            high = source[index[(2 * pair + 1) * stride + slot]]
            at = pl.multiple_of(n * span + pair * 2 * tilts, 2 * tilts)
            gathered[pl.ds(at, 2 * tilts), :] = jnp.concatenate([low, high], axis=0)
            return carry

        lax.fori_loop(0, rows // 2, gather, 0, unroll=True)
    taken = gathered[: len(slots) * span, :]
    product = jnp.dot(taken, weights, preferred_element_type=jnp.float32)
    return product.reshape(len(slots), rows, tilts, weights.shape[1])


def near_sum(index, source, kernels, rates, gathered, rows, before_first_use=None):
    kinds, tilts, size = kernels.shape[0], source.shape[1], source.shape[2]
    upper = jnp.full((rows, size), index[rows * NEAR]) > 0
    total = None
    for kind in range(kinds):
        slots = range(kind, NEAR, kinds)
        product = weighted(
            index, NEAR, slots, source, kernels[kind], gathered.at[kind % 2], rows, tilts
        )
        if kind == 0 and before_first_use is not None:
            before_first_use.wait()
        for n, slot in enumerate(slots):
            rate = rates[slot].astype(jnp.float32)
            rate = jnp.where(upper, rate[rows:], rate[:rows])
            term = product[n] * rate[:, None, :]
            total = term if total is None else total + term
    return total


def early_kernel(index, own, halo, kernels, rates, out, *scratch):
    index_smem, extended, rate_buf, out_buf, gathered, sems = scratch
    rows, half = own.shape[0], halo.shape[0]
    copies = [
        start_copy(index, index_smem, sems.at[0]),
        start_copy(own, extended.at[pl.ds(0, rows)], sems.at[1]),
        start_copy(halo, extended.at[pl.ds(rows, half)], sems.at[2]),
    ]
    rate_copy = start_copy(rates.at[pl.ds(0, NEAR)], rate_buf, sems.at[3])
    for copy in copies:
        copy.wait()
    out_buf[...] = near_sum(index_smem, extended, kernels, rate_buf, gathered, half, rate_copy)
    start_copy(out_buf, out, sems.at[4]).wait()


def map_blocks(operands, scratch, meanwhile=None):
    near_index, far_index, halo, own, early, arrived, kernels, rates = operands
    near_smem, far_smem, extended, far_blocks, rate_buf, early_buf, gathered, sems = scratch
    kinds = kernels.shape[0]
    (rows, tilts, size), half = own.shape, halo.shape[0]
    far_count = rates.shape[0] - NEAR

    first = [
        start_copy(near_index, near_smem, sems.at[0]),
        start_copy(own, extended.at[pl.ds(0, rows)], sems.at[1]),
        start_copy(halo, extended.at[pl.ds(rows, half)], sems.at[2]),
    ]
    rate_copy = start_copy(rates, rate_buf, sems.at[3])
    late = [
        start_copy(far_index, far_smem, sems.at[4]),
        start_copy(early, early_buf, sems.at[5]),
        start_copy(arrived, far_blocks, sems.at[6]),
    ]
    if meanwhile is not None:
        meanwhile()
    for copy in first:
        copy.wait()

    here = near_sum(near_smem, extended, kernels, rate_buf, gathered, half, rate_copy)
    for copy in late:
        copy.wait()
    upper = jnp.full((half, tilts, size), near_smem[half * NEAR]) > 0
    other = early_buf[...]
    total = jnp.concatenate([jnp.where(upper, other, here), jnp.where(upper, here, other)], axis=0)
    for kind in range(kinds):
        slots = range(kind, far_count, kinds)
        product = weighted(
            far_smem, far_count, slots, far_blocks, kernels[kind], gathered.at[kind % 2], rows, tilts
        )
        for n, slot in enumerate(slots):
            total = total + product[n] * rate_buf[NEAR + slot].astype(jnp.float32)[:, None, :]
    return total


def sum_of_squares(total):
    return jnp.sum(jnp.sum(total * total, axis=0), axis=1, keepdims=True)


def step_kernel(codes, factor, *refs):
    operands, (tilted, outgoing, squares) = refs[:8], refs[8:11]
    line, words, factor_buf, tilted_buf, staged, pack_sems, sems = refs[11:18]
    started = []

    def meanwhile():
        started.append(read_words(codes, line, words, sems.at[0]))
        started.append(start_copy(factor, factor_buf, sems.at[2]))

    total = map_blocks(operands, refs[18:], meanwhile)
    words_copy, factor_copy = started
    factor_copy.wait()
    tilted_buf[...] = (factor_buf[...] * total).astype(jnp.bfloat16)
    copies = [start_copy(tilted_buf, tilted, sems.at[1])]
    words_copy.wait()
    copies += pack_blocks(words, tilted_buf, staged, outgoing, pack_sems)
    squares[...] = jnp.sum(total * total, axis=0)
    for copy in copies:
        copy.wait()


def last_kernel(first_squares, *refs):
    operands, (mapped, sums) = refs[:8], refs[8:10]
    total = map_blocks(operands, refs[10:])
    for row in range(total.shape[0]):
        mapped[:, row * total.shape[2] : (row + 1) * total.shape[2]] = total[row]
    tilts = total.shape[1]
    across = lax.broadcasted_iota(jnp.int32, (tilts, sums.shape[1]), 1)
    tilt = lax.broadcasted_iota(jnp.int32, (tilts, sums.shape[1]), 0)
    first = jnp.sum(first_squares[...], axis=1, keepdims=True)
    both = jnp.where(across == tilt, first, 0.0) + jnp.where(
        across == tilt + tilts, sum_of_squares(total), 0.0
    )
    sums[...] = jnp.broadcast_to(jnp.sum(both, axis=0, keepdims=True), sums.shape)


def end_kernel(states, sums, mapped, iterate, growth, scaled, sems):
    tilts = mapped.shape[0]
    totals = jnp.sum(sums[...], axis=0, keepdims=True)
    across = lax.broadcasted_iota(jnp.int32, (tilts, sums.shape[1]), 1)
    tilt = lax.broadcasted_iota(jnp.int32, (tilts, sums.shape[1]), 0)
    diagonal = lax.broadcasted_iota(jnp.int32, (tilts, tilts), 0) == lax.broadcasted_iota(
        jnp.int32, (tilts, tilts), 1
    )
    product = jnp.ones((tilts, 1), jnp.float32)
    for j in range(ITERS):
        total = jnp.sum(jnp.where(across == tilt + j * tilts, totals, 0.0), axis=1, keepdims=True)
        scale = jnp.sqrt(total / product / product / states + 1e-06)
        product = product * scale
        growth[j : j + 1, :] = jnp.sum(
            jnp.where(diagonal, jnp.log(scale), 0.0), axis=0, keepdims=True
        )
    inverse = 1.0 / product
    width = mapped.shape[1] // END_CHUNKS
    copies = []
    for part in range(END_CHUNKS):
        span = pl.ds(part * width, width)
        scaled[:, span] = mapped[:, span] * inverse
        copies.append(start_copy(scaled.at[:, span], iterate.at[:, span], sems.at[part]))
    for copy in copies:
        copy.wait()


def call(kernel, outs, arrays, scratch, flops, limit, in_vmem=()):
    spec = [pl.BlockSpec(memory_space=pltpu.VMEM), pl.BlockSpec(memory_space=pl.ANY)]
    moved = sum(math.prod(a.shape) * a.dtype.itemsize for a in (*arrays, *outs))
    return pl.pallas_call(
        kernel,
        out_shape=outs,
        in_specs=[spec[n not in in_vmem] for n in range(len(arrays))],
        out_specs=[spec[len(arrays) + n not in in_vmem] for n in range(len(outs))],
        scratch_shapes=scratch,
        compiler_params=pltpu.CompilerParams(vmem_limit_bytes=limit),
        cost_estimate=pl.CostEstimate(flops=flops, bytes_accessed=moved, transcendentals=0),
    )(*arrays)


def on_device(start, reward, theta, kernels, rates, pattern):
    tilt_count = start.shape[0]
    blocks_here, slot_count = pattern.shape
    kind_count, block_size = kernels.shape[:2]
    peer_count = lax.axis_size("rows")
    position = lax.axis_index("rows")
    total_blocks = blocks_here * peer_count
    far_count = slot_count - NEAR
    half_span = blocks_here // 2
    capacity = 2
    shape = jax.ShapeDtypeStruct
    sem = pltpu.SemaphoreType.DMA

    pattern_by_slot = pattern.T
    (codes,) = call(
        lambda *refs: request_kernel(blocks_here, *refs),
        [shape((peer_count, 1), jnp.int32)],
        [pattern_by_slot],
        [],
        0,
        REQUEST_LIMIT,
        in_vmem=(0, 1),
    )
    codes = lax.all_to_all(codes, "rows", split_axis=0, concat_axis=0, tiled=True)

    far_cols = pattern[:, NEAR:].reshape(-1)
    owners = lax.div(far_cols, blocks_here)
    smaller = (owners[:, None] == owners[None, :]) & (far_cols[None, :] < far_cols[:, None])
    far_index = owners * capacity + jnp.any(smaller, axis=1).astype(jnp.int32)
    local_rows = jnp.arange(blocks_here, dtype=jnp.int32)
    global_rows = position * blocks_here + local_rows
    shifts = (pattern[:, :NEAR] - global_rows[:, None] + half_span) % total_blocks - half_span
    reached = local_rows[:, None] + shifts
    reached = jnp.where(reached < 0, reached + blocks_here + half_span, reached)

    odd = position % 2
    early_first = half_span * (1 - odd)

    def half_index(start_row):
        entries = lax.dynamic_slice(reached, (start_row, 0), (half_span, NEAR)).reshape(-1)
        return jnp.concatenate([entries, start_row[None]])

    early_index = half_index(early_first)
    late_index = half_index(half_span - early_first)
    on_chip = [(i, i + 1 - 2 * (i % 2)) for i in range(peer_count)]
    off_chip = [(i, (i - 1 + 2 * (i % 2)) % peer_count) for i in range(peer_count)]
    rates_by_slot = rates.transpose(1, 0, 2)
    reward = reward.reshape(blocks_here, block_size)

    block = (tilt_count, block_size)
    tilted_shape = shape((blocks_here, *block), jnp.bfloat16)
    outgoing_shape = shape((peer_count * capacity, *block), jnp.bfloat16)
    squares_shape = shape(block, jnp.float32)
    sums_shape = shape((peer_count, ITERS * tilt_count), jnp.float32)
    mapped_shape = shape(start.shape, jnp.float32)
    word_buffers = [pltpu.VMEM((1, peer_count), jnp.int32), pltpu.SMEM((1, peer_count), jnp.int32)]
    staged = pltpu.VMEM(outgoing_shape.shape, jnp.bfloat16)
    early_shape = shape((half_span, *block), jnp.float32)
    reach = pltpu.VMEM((blocks_here + half_span, *block), jnp.bfloat16)
    near_rows = NEAR // kind_count * half_span * tilt_count
    far_rows = far_count // kind_count * blocks_here * tilt_count
    gathered = pltpu.VMEM((2, max(near_rows, far_rows), block_size), jnp.bfloat16)
    early_scratch = [
        pltpu.SMEM(early_index.shape, jnp.int32),
        reach,
        pltpu.VMEM((NEAR, blocks_here, block_size), jnp.bfloat16),
        pltpu.VMEM(early_shape.shape, jnp.float32),
        gathered,
        sem((5,)),
    ]
    map_scratch = [
        pltpu.SMEM(late_index.shape, jnp.int32),
        pltpu.SMEM(far_index.shape, jnp.int32),
        reach,
        staged,
        pltpu.VMEM(rates_by_slot.shape, jnp.bfloat16),
        pltpu.VMEM(early_shape.shape, jnp.float32),
        gathered,
        sem((7,)),
    ]
    slot_flops = 2 * blocks_here * tilt_count * block_size * block_size
    early_flops = NEAR * slot_flops // 2
    map_flops = slot_count * slot_flops - early_flops

    factor = jnp.exp(theta[None, :, None] * reward[:, None, :])
    tilted = factor * start.reshape(tilt_count, blocks_here, block_size).transpose(1, 0, 2)
    tilted = tilted.astype(jnp.bfloat16)
    (outgoing,) = call(
        pack_kernel,
        [pltpu.HBM(outgoing_shape.shape, outgoing_shape.dtype)],
        [codes, tilted],
        [*word_buffers, staged, sem, sem((PACK_CHUNKS,))],
        0,
        PACK_LIMIT,
        in_vmem=(0, 1),
    )
    for iteration in range(ITERS):
        arrived = lax.all_to_all(outgoing, "rows", split_axis=0, concat_axis=0, tiled=True)
        head, tail = tilted[:half_span], tilted[blocks_here - half_span :]
        near_halo = lax.ppermute(jnp.where(odd, head, tail), "rows", on_chip)
        far_halo = lax.ppermute(jnp.where(odd, tail, head), "rows", off_chip)
        arrived = pltpu.with_memory_space_constraint(arrived, pltpu.HBM)
        rates_hbm = pltpu.with_memory_space_constraint(rates_by_slot, pltpu.HBM)
        if iteration < ITERS - 1:
            factor_hbm = pltpu.with_memory_space_constraint(factor, pltpu.HBM)
        (early,) = call(
            early_kernel,
            [pltpu.HBM(early_shape.shape, early_shape.dtype)],
            [early_index, tilted, near_halo, kernels, rates_hbm],
            early_scratch,
            early_flops,
            MAP_LIMIT,
            in_vmem=(3,),
        )
        early = pltpu.with_memory_space_constraint(early, pltpu.HBM)
        operands = [late_index, far_index, far_halo, tilted, early, arrived, kernels, rates_hbm]
        if iteration < ITERS - 1:
            step_scratch = [
                *word_buffers,
                pltpu.VMEM(tilted_shape.shape, jnp.float32),
                pltpu.VMEM(tilted_shape.shape, jnp.bfloat16),
                staged,
                sem((PACK_CHUNKS,)),
                sem((3,)),
            ]
            tilted, outgoing, squares = call(
                step_kernel,
                [tilted_shape, pltpu.HBM(outgoing_shape.shape, outgoing_shape.dtype), squares_shape],
                [codes, factor_hbm, *operands],
                step_scratch + map_scratch,
                map_flops,
                MAP_LIMIT,
                in_vmem=(0, 8, 12),
            )
        else:
            mapped, sums = call(
                last_kernel,
                [mapped_shape, sums_shape],
                [squares, *operands],
                map_scratch,
                map_flops,
                MAP_LIMIT,
                in_vmem=(0, 7, 9, 10),
            )

    gathered = lax.all_to_all(sums, "rows", split_axis=0, concat_axis=0, tiled=True)
    states = total_blocks * block_size
    return call(
        lambda *refs: end_kernel(states, *refs),
        [mapped_shape, shape((ITERS, tilt_count), jnp.float32)],
        [gathered, mapped],
        [pltpu.VMEM(start.shape, jnp.float32), sem((END_CHUNKS,))],
        0,
        MAP_LIMIT,
        in_vmem=(0, 1, 3),
    )


def solution(mesh):
    placed = (P("tilt", "rows"), P("rows"), P("tilt"), P(), P("rows", None, None), P("rows", None))
    return jax.shard_map(
        on_device,
        mesh=mesh,
        in_specs=placed,
        out_specs=(P("tilt", "rows"), P(None, "tilt")),
        check_vma=False,
    )
```

```python
import math

import jax
import jax.numpy as jnp
from jax import lax
from jax.experimental import pallas as pl
from jax.experimental.pallas import tpu as pltpu
from jax.sharding import PartitionSpec as P

NEAR = 8
ITERS = 2
PACK_CHUNKS = 8
END_CHUNKS = 4
HALF_WORD = 1 << 16
REQUEST_LIMIT = 62 * 1024 * 1024
PACK_LIMIT = 48 * 1024 * 1024
MAP_LIMIT = 44 * 1024 * 1024


def request_kernel(blocks_here, pattern, codes):
    peers = codes.shape[0]
    slots, rows = pattern.shape
    base = lax.broadcasted_iota(jnp.int32, (peers, rows), 0) * blocks_here
    low = jnp.full((peers, rows), blocks_here, jnp.int32)
    high = jnp.full((peers, rows), -1, jnp.int32)
    for slot in range(NEAR, slots):
        within = pattern[slot : slot + 1, :] - base
        named = (within >= 0) & (within < blocks_here)
        low = jnp.minimum(low, jnp.where(named, within, blocks_here))
        high = jnp.maximum(high, jnp.where(named, within, -1))
    low = jnp.min(low, axis=1, keepdims=True)
    high = jnp.max(high, axis=1, keepdims=True)
    codes[...] = jnp.where(high >= 0, high * HALF_WORD + low, 0)


def start_copy(src, dst, sem):
    copy = pltpu.make_async_copy(src, dst, sem)
    copy.start()
    return copy


def read_words(codes, line, words, sem):
    peers = codes.shape[0]
    across = lax.broadcasted_iota(jnp.int32, (peers, peers), 1)
    same = lax.broadcasted_iota(jnp.int32, (peers, peers), 0) == across
    line[...] = jnp.sum(jnp.where(same, codes[...], 0), axis=0, keepdims=True)
    return start_copy(line, words, sem)


def pack_blocks(words, tilted, staged, outgoing, sems):
    chunk = outgoing.shape[0] // PACK_CHUNKS
    copies = []
    for part in range(PACK_CHUNKS):

        def body(j, carry, part=part):
            word = words[0, part * (chunk // 2) + j]
            staged[part * chunk + 2 * j] = tilted[word & (HALF_WORD - 1)]
            staged[part * chunk + 2 * j + 1] = tilted[lax.shift_right_logical(word, 16)]
            return carry

        lax.fori_loop(0, chunk // 2, body, 0, unroll=8)
        span = pl.ds(part * chunk, chunk)
        copies.append(start_copy(staged.at[span], outgoing.at[span], sems.at[part]))
    return copies


def pack_kernel(codes, tilted, outgoing, line, words, staged, word_sem, sems):
    read_words(codes, line, words, word_sem).wait()
    for copy in pack_blocks(words, tilted, staged, outgoing, sems):
        copy.wait()


def weighted(index, stride, slots, source, weights, gathered, rows, tilts):
    span = rows * tilts
    for n, slot in enumerate(slots):

        def gather(pair, carry, slot=slot, n=n):
            low = source[index[2 * pair * stride + slot]]
            high = source[index[(2 * pair + 1) * stride + slot]]
            at = pl.multiple_of(n * span + pair * 2 * tilts, 2 * tilts)
            gathered[pl.ds(at, 2 * tilts), :] = jnp.concatenate([low, high], axis=0)
            return carry

        lax.fori_loop(0, rows // 2, gather, 0, unroll=True)
    taken = gathered[: len(slots) * span, :]
    product = jnp.dot(taken, weights, preferred_element_type=jnp.float32)
    return product.reshape(len(slots), rows, tilts, weights.shape[1])


def near_sum(index, source, kernels, rates, gathered, rows):
    kinds, tilts, size = kernels.shape[0], source.shape[1], source.shape[2]
    upper = jnp.full((rows, size), index[rows * NEAR]) > 0
    total = None
    for kind in range(kinds):
        slots = range(kind, NEAR, kinds)
        product = weighted(
            index, NEAR, slots, source, kernels[kind], gathered.at[kind % 2], rows, tilts
        )
        for n, slot in enumerate(slots):
            rate = rates[slot].astype(jnp.float32)
            rate = jnp.where(upper, rate[rows:], rate[:rows])
            term = product[n] * rate[:, None, :]
            total = term if total is None else total + term
    return total


def early_kernel(index, own, halo, kernels, rates, out, *scratch):
    index_smem, extended, out_buf, gathered, sems = scratch
    rows, half = own.shape[0], halo.shape[0]
    copies = [
        start_copy(index, index_smem, sems.at[0]),
        start_copy(own, extended.at[pl.ds(0, rows)], sems.at[1]),
        start_copy(halo, extended.at[pl.ds(rows, half)], sems.at[2]),
    ]
    for copy in copies:
        copy.wait()
    out_buf[...] = near_sum(index_smem, extended, kernels, rates, gathered, half)
    start_copy(out_buf, out, sems.at[3]).wait()


def map_blocks(operands, scratch, meanwhile=None):
    near_index, far_index, halo, own, early, arrived, kernels, rates = operands
    near_smem, far_smem, extended, far_blocks, early_buf, gathered, sems = scratch
    kinds = kernels.shape[0]
    (rows, tilts, size), half = own.shape, halo.shape[0]
    far_count = rates.shape[0] - NEAR

    first = [
        start_copy(near_index, near_smem, sems.at[0]),
        start_copy(own, extended.at[pl.ds(0, rows)], sems.at[1]),
        start_copy(halo, extended.at[pl.ds(rows, half)], sems.at[2]),
    ]
    late = [
        start_copy(far_index, far_smem, sems.at[3]),
        start_copy(early, early_buf, sems.at[4]),
        start_copy(arrived, far_blocks, sems.at[5]),
    ]
    if meanwhile is not None:
        meanwhile()
    for copy in first:
        copy.wait()

    here = near_sum(near_smem, extended, kernels, rates, gathered, half)
    for copy in late:
        copy.wait()
    upper = jnp.full((half, tilts, size), near_smem[half * NEAR]) > 0
    other = early_buf[...]
    total = jnp.concatenate([jnp.where(upper, other, here), jnp.where(upper, here, other)], axis=0)
    for kind in range(kinds):
        slots = range(kind, far_count, kinds)
        product = weighted(
            far_smem, far_count, slots, far_blocks, kernels[kind], gathered.at[kind % 2], rows, tilts
        )
        for n, slot in enumerate(slots):
            total = total + product[n] * rates[NEAR + slot].astype(jnp.float32)[:, None, :]
    return total


def sum_of_squares(total):
    return jnp.sum(jnp.sum(total * total, axis=0), axis=1, keepdims=True)


def step_kernel(codes, factor, *refs):
    operands, (tilted, outgoing, squares) = refs[:8], refs[8:11]
    line, words, factor_buf, tilted_buf, staged, pack_sems, sems = refs[11:18]
    started = []

    def meanwhile():
        started.append(read_words(codes, line, words, sems.at[0]))
        started.append(start_copy(factor, factor_buf, sems.at[2]))

    total = map_blocks(operands, refs[18:], meanwhile)
    words_copy, factor_copy = started
    factor_copy.wait()
    tilted_buf[...] = (factor_buf[...] * total).astype(jnp.bfloat16)
    copies = [start_copy(tilted_buf, tilted, sems.at[1])]
    words_copy.wait()
    copies += pack_blocks(words, tilted_buf, staged, outgoing, pack_sems)
    squares[...] = jnp.sum(total * total, axis=0)
    for copy in copies:
        copy.wait()


def last_kernel(first_squares, *refs):
    operands, (mapped, sums) = refs[:8], refs[8:10]
    total = map_blocks(operands, refs[10:])
    for row in range(total.shape[0]):
        mapped[:, row * total.shape[2] : (row + 1) * total.shape[2]] = total[row]
    tilts = total.shape[1]
    across = lax.broadcasted_iota(jnp.int32, (tilts, sums.shape[1]), 1)
    tilt = lax.broadcasted_iota(jnp.int32, (tilts, sums.shape[1]), 0)
    first = jnp.sum(first_squares[...], axis=1, keepdims=True)
    both = jnp.where(across == tilt, first, 0.0) + jnp.where(
        across == tilt + tilts, sum_of_squares(total), 0.0
    )
    sums[...] = jnp.broadcast_to(jnp.sum(both, axis=0, keepdims=True), sums.shape)


def end_kernel(states, sums, mapped, iterate, growth, scaled, sems):
    tilts = mapped.shape[0]
    totals = jnp.sum(sums[...], axis=0, keepdims=True)
    across = lax.broadcasted_iota(jnp.int32, (tilts, sums.shape[1]), 1)
    tilt = lax.broadcasted_iota(jnp.int32, (tilts, sums.shape[1]), 0)
    diagonal = lax.broadcasted_iota(jnp.int32, (tilts, tilts), 0) == lax.broadcasted_iota(
        jnp.int32, (tilts, tilts), 1
    )
    product = jnp.ones((tilts, 1), jnp.float32)
    for j in range(ITERS):
        total = jnp.sum(jnp.where(across == tilt + j * tilts, totals, 0.0), axis=1, keepdims=True)
        scale = jnp.sqrt(total / product / product / states + 1e-06)
        product = product * scale
        growth[j : j + 1, :] = jnp.sum(
            jnp.where(diagonal, jnp.log(scale), 0.0), axis=0, keepdims=True
        )
    inverse = 1.0 / product
    width = mapped.shape[1] // END_CHUNKS
    copies = []
    for part in range(END_CHUNKS):
        span = pl.ds(part * width, width)
        scaled[:, span] = mapped[:, span] * inverse
        copies.append(start_copy(scaled.at[:, span], iterate.at[:, span], sems.at[part]))
    for copy in copies:
        copy.wait()


def call(kernel, outs, arrays, scratch, flops, limit, in_vmem=()):
    spec = [pl.BlockSpec(memory_space=pltpu.VMEM), pl.BlockSpec(memory_space=pl.ANY)]
    moved = sum(math.prod(a.shape) * a.dtype.itemsize for a in (*arrays, *outs))
    return pl.pallas_call(
        kernel,
        out_shape=outs,
        in_specs=[spec[n not in in_vmem] for n in range(len(arrays))],
        out_specs=[spec[len(arrays) + n not in in_vmem] for n in range(len(outs))],
        scratch_shapes=scratch,
        compiler_params=pltpu.CompilerParams(vmem_limit_bytes=limit),
        cost_estimate=pl.CostEstimate(flops=flops, bytes_accessed=moved, transcendentals=0),
    )(*arrays)


def on_device(start, reward, theta, kernels, rates, pattern):
    tilt_count = start.shape[0]
    blocks_here, slot_count = pattern.shape
    kind_count, block_size = kernels.shape[:2]
    peer_count = lax.axis_size("rows")
    position = lax.axis_index("rows")
    total_blocks = blocks_here * peer_count
    far_count = slot_count - NEAR
    half_span = blocks_here // 2
    capacity = 2
    shape = jax.ShapeDtypeStruct
    sem = pltpu.SemaphoreType.DMA

    pattern_by_slot = pattern.T
    (codes,) = call(
        lambda *refs: request_kernel(blocks_here, *refs),
        [shape((peer_count, 1), jnp.int32)],
        [pattern_by_slot],
        [],
        0,
        REQUEST_LIMIT,
        in_vmem=(0, 1),
    )
    codes = lax.all_to_all(codes, "rows", split_axis=0, concat_axis=0, tiled=True)

    far_cols = pattern[:, NEAR:].reshape(-1)
    owners = lax.div(far_cols, blocks_here)
    smaller = (owners[:, None] == owners[None, :]) & (far_cols[None, :] < far_cols[:, None])
    far_index = owners * capacity + jnp.any(smaller, axis=1).astype(jnp.int32)
    local_rows = jnp.arange(blocks_here, dtype=jnp.int32)
    global_rows = position * blocks_here + local_rows
    shifts = (pattern[:, :NEAR] - global_rows[:, None] + half_span) % total_blocks - half_span
    reached = local_rows[:, None] + shifts
    reached = jnp.where(reached < 0, reached + blocks_here + half_span, reached)

    odd = position % 2
    early_first = half_span * (1 - odd)

    def half_index(start_row):
        entries = lax.dynamic_slice(reached, (start_row, 0), (half_span, NEAR)).reshape(-1)
        return jnp.concatenate([entries, start_row[None]])

    early_index = half_index(early_first)
    late_index = half_index(half_span - early_first)
    on_chip = [(i, i + 1 - 2 * (i % 2)) for i in range(peer_count)]
    off_chip = [(i, (i - 1 + 2 * (i % 2)) % peer_count) for i in range(peer_count)]
    rates_by_slot = rates.transpose(1, 0, 2)
    reward = reward.reshape(blocks_here, block_size)

    block = (tilt_count, block_size)
    tilted_shape = shape((blocks_here, *block), jnp.bfloat16)
    outgoing_shape = shape((peer_count * capacity, *block), jnp.bfloat16)
    squares_shape = shape(block, jnp.float32)
    sums_shape = shape((peer_count, ITERS * tilt_count), jnp.float32)
    mapped_shape = shape(start.shape, jnp.float32)
    word_buffers = [pltpu.VMEM((1, peer_count), jnp.int32), pltpu.SMEM((1, peer_count), jnp.int32)]
    staged = pltpu.VMEM(outgoing_shape.shape, jnp.bfloat16)
    early_shape = shape((half_span, *block), jnp.float32)
    reach = pltpu.VMEM((blocks_here + half_span, *block), jnp.bfloat16)
    near_rows = NEAR // kind_count * half_span * tilt_count
    far_rows = far_count // kind_count * blocks_here * tilt_count
    gathered = pltpu.VMEM((2, max(near_rows, far_rows), block_size), jnp.bfloat16)
    early_scratch = [
        pltpu.SMEM(early_index.shape, jnp.int32),
        reach,
        pltpu.VMEM(early_shape.shape, jnp.float32),
        gathered,
        sem((4,)),
    ]
    map_scratch = [
        pltpu.SMEM(late_index.shape, jnp.int32),
        pltpu.SMEM(far_index.shape, jnp.int32),
        reach,
        staged,
        pltpu.VMEM(early_shape.shape, jnp.float32),
        gathered,
        sem((6,)),
    ]
    slot_flops = 2 * blocks_here * tilt_count * block_size * block_size
    early_flops = NEAR * slot_flops // 2
    map_flops = slot_count * slot_flops - early_flops

    factor = jnp.exp(theta[None, :, None] * reward[:, None, :])
    tilted = factor * start.reshape(tilt_count, blocks_here, block_size).transpose(1, 0, 2)
    tilted = tilted.astype(jnp.bfloat16)
    (outgoing,) = call(
        pack_kernel,
        [pltpu.HBM(outgoing_shape.shape, outgoing_shape.dtype)],
        [codes, tilted],
        [*word_buffers, staged, sem, sem((PACK_CHUNKS,))],
        0,
        PACK_LIMIT,
        in_vmem=(0, 1),
    )
    for iteration in range(ITERS):
        arrived = lax.all_to_all(outgoing, "rows", split_axis=0, concat_axis=0, tiled=True)
        head, tail = tilted[:half_span], tilted[blocks_here - half_span :]
        near_halo = lax.ppermute(jnp.where(odd, head, tail), "rows", on_chip)
        far_halo = lax.ppermute(jnp.where(odd, tail, head), "rows", off_chip)
        arrived = pltpu.with_memory_space_constraint(arrived, pltpu.HBM)
        if iteration < ITERS - 1:
            factor_hbm = pltpu.with_memory_space_constraint(factor, pltpu.HBM)
        (early,) = call(
            early_kernel,
            [pltpu.HBM(early_shape.shape, early_shape.dtype)],
            [early_index, tilted, near_halo, kernels, rates_by_slot],
            early_scratch,
            early_flops,
            MAP_LIMIT,
            in_vmem=(3, 4),
        )
        early = pltpu.with_memory_space_constraint(early, pltpu.HBM)
        operands = [late_index, far_index, far_halo, tilted, early, arrived, kernels, rates_by_slot]
        if iteration < ITERS - 1:
            step_scratch = [
                *word_buffers,
                pltpu.VMEM(tilted_shape.shape, jnp.float32),
                pltpu.VMEM(tilted_shape.shape, jnp.bfloat16),
                staged,
                sem((PACK_CHUNKS,)),
                sem((3,)),
            ]
            tilted, outgoing, squares = call(
                step_kernel,
                [tilted_shape, pltpu.HBM(outgoing_shape.shape, outgoing_shape.dtype), squares_shape],
                [codes, factor_hbm, *operands],
                step_scratch + map_scratch,
                map_flops,
                MAP_LIMIT,
                in_vmem=(0, 8, 9, 12),
            )
        else:
            mapped, sums = call(
                last_kernel,
                [mapped_shape, sums_shape],
                [squares, *operands],
                map_scratch,
                map_flops,
                MAP_LIMIT,
                in_vmem=(0, 7, 8, 9, 10),
            )

    gathered = lax.all_to_all(sums, "rows", split_axis=0, concat_axis=0, tiled=True)
    states = total_blocks * block_size
    return call(
        lambda *refs: end_kernel(states, *refs),
        [mapped_shape, shape((ITERS, tilt_count), jnp.float32)],
        [gathered, mapped],
        [pltpu.VMEM(start.shape, jnp.float32), sem((END_CHUNKS,))],
        0,
        MAP_LIMIT,
        in_vmem=(0, 1, 3),
    )


def solution(mesh):
    placed = (P("tilt", "rows"), P("rows"), P("tilt"), P(), P("rows", None, None), P("rows", None))
    return jax.shard_map(
        on_device,
        mesh=mesh,
        in_specs=placed,
        out_specs=(P("tilt", "rows"), P(None, "tilt")),
        check_vma=False,
    )
```

```python
import math

import jax
import jax.numpy as jnp
from jax import lax
from jax.experimental import pallas as pl
from jax.experimental.pallas import tpu as pltpu
from jax.sharding import PartitionSpec as P

NEAR = 8
ITERS = 2
PACK_CHUNKS = 8
END_CHUNKS = 4
HALF_WORD = 1 << 16
REQUEST_LIMIT = 62 * 1024 * 1024
PACK_LIMIT = 48 * 1024 * 1024
MAP_LIMIT = 44 * 1024 * 1024


def request_kernel(blocks_here, pattern, codes):
    peers = codes.shape[0]
    slots, rows = pattern.shape
    base = lax.broadcasted_iota(jnp.int32, (peers, rows), 0) * blocks_here
    low = jnp.full((peers, rows), blocks_here, jnp.int32)
    high = jnp.full((peers, rows), -1, jnp.int32)
    for slot in range(NEAR, slots):
        within = pattern[slot : slot + 1, :] - base
        named = (within >= 0) & (within < blocks_here)
        low = jnp.minimum(low, jnp.where(named, within, blocks_here))
        high = jnp.maximum(high, jnp.where(named, within, -1))
    low = jnp.min(low, axis=1, keepdims=True)
    high = jnp.max(high, axis=1, keepdims=True)
    codes[...] = jnp.where(high >= 0, high * HALF_WORD + low, 0)


def start_copy(src, dst, sem):
    copy = pltpu.make_async_copy(src, dst, sem)
    copy.start()
    return copy


def read_words(codes, line, words, sem):
    peers = codes.shape[0]
    across = lax.broadcasted_iota(jnp.int32, (peers, peers), 1)
    same = lax.broadcasted_iota(jnp.int32, (peers, peers), 0) == across
    line[...] = jnp.sum(jnp.where(same, codes[...], 0), axis=0, keepdims=True)
    return start_copy(line, words, sem)


def pack_blocks(words, tilted, staged, outgoing, sems):
    chunk = outgoing.shape[0] // PACK_CHUNKS
    copies = []
    for part in range(PACK_CHUNKS):

        def body(j, carry, part=part):
            word = words[0, part * (chunk // 2) + j]
            staged[part * chunk + 2 * j] = tilted[word & (HALF_WORD - 1)]
            staged[part * chunk + 2 * j + 1] = tilted[lax.shift_right_logical(word, 16)]
            return carry

        lax.fori_loop(0, chunk // 2, body, 0, unroll=8)
        span = pl.ds(part * chunk, chunk)
        copies.append(start_copy(staged.at[span], outgoing.at[span], sems.at[part]))
    return copies


def pack_kernel(codes, tilted, outgoing, line, words, staged, word_sem, sems):
    read_words(codes, line, words, word_sem).wait()
    for copy in pack_blocks(words, tilted, staged, outgoing, sems):
        copy.wait()


def weighted(index, stride, slots, source, weights, gathered, rows, tilts):
    span = rows * tilts
    for n, slot in enumerate(slots):

        def gather(pair, carry, slot=slot, n=n):
            low = source[index[2 * pair * stride + slot]]
            high = source[index[(2 * pair + 1) * stride + slot]]
            at = pl.multiple_of(n * span + pair * 2 * tilts, 2 * tilts)
            gathered[pl.ds(at, 2 * tilts), :] = jnp.concatenate([low, high], axis=0)
            return carry

        lax.fori_loop(0, rows // 2, gather, 0, unroll=True)
    taken = gathered[: len(slots) * span, :]
    product = jnp.dot(taken, weights, preferred_element_type=jnp.float32)
    return product.reshape(len(slots), rows, tilts, weights.shape[1])


def near_sum(index, source, kernels, rates, gathered, rows):
    kinds, tilts, size = kernels.shape[0], source.shape[1], source.shape[2]
    upper = jnp.full((rows, size), index[rows * NEAR]) > 0
    total = None
    for kind in range(kinds):
        slots = range(kind, NEAR, kinds)
        product = weighted(
            index, NEAR, slots, source, kernels[kind], gathered.at[kind % 2], rows, tilts
        )
        for n, slot in enumerate(slots):
            rate = rates[slot].astype(jnp.float32)
            rate = jnp.where(upper, rate[rows:], rate[:rows])
            term = product[n] * rate[:, None, :]
            total = term if total is None else total + term
    return total


def early_kernel(index, own, halo, kernels, rates, out, *scratch):
    index_smem, extended, out_buf, gathered, sems = scratch
    rows, half = own.shape[0], halo.shape[0]
    copies = [
        start_copy(index, index_smem, sems.at[0]),
        start_copy(own, extended.at[pl.ds(0, rows)], sems.at[1]),
        start_copy(halo, extended.at[pl.ds(rows, half)], sems.at[2]),
    ]
    for copy in copies:
        copy.wait()
    out_buf[...] = near_sum(index_smem, extended, kernels, rates, gathered, half)
    start_copy(out_buf, out, sems.at[3]).wait()


def map_blocks(operands, scratch, meanwhile=None):
    near_index, far_index, halo, own, early, arrived, kernels, rates = operands
    near_smem, far_smem, extended, far_blocks, early_buf, gathered, sems = scratch
    kinds = kernels.shape[0]
    (rows, tilts, size), half = own.shape, halo.shape[0]
    far_count = rates.shape[0] - NEAR

    first = [
        start_copy(near_index, near_smem, sems.at[0]),
        start_copy(own, extended.at[pl.ds(0, rows)], sems.at[1]),
        start_copy(halo, extended.at[pl.ds(rows, half)], sems.at[2]),
    ]
    late = [
        start_copy(far_index, far_smem, sems.at[3]),
        start_copy(early, early_buf, sems.at[4]),
        start_copy(arrived, far_blocks, sems.at[5]),
    ]
    if meanwhile is not None:
        meanwhile()
    for copy in first:
        copy.wait()

    here = near_sum(near_smem, extended, kernels, rates, gathered, half)
    for copy in late:
        copy.wait()
    upper = jnp.full((half, tilts, size), near_smem[half * NEAR]) > 0
    other = early_buf[...]
    total = jnp.concatenate([jnp.where(upper, other, here), jnp.where(upper, here, other)], axis=0)
    for kind in range(kinds):
        slots = range(kind, far_count, kinds)
        product = weighted(
            far_smem, far_count, slots, far_blocks, kernels[kind], gathered.at[kind % 2], rows, tilts
        )
        for n, slot in enumerate(slots):
            total = total + product[n] * rates[NEAR + slot].astype(jnp.float32)[:, None, :]
    return total


def sum_of_squares(total):
    return jnp.sum(jnp.sum(total * total, axis=0), axis=1, keepdims=True)


def step_kernel(codes, factor, *refs):
    operands, (tilted, outgoing, squares) = refs[:8], refs[8:11]
    line, words, factor_buf, tilted_buf, staged, pack_sems, sems = refs[11:18]
    started = []

    def meanwhile():
        started.append(read_words(codes, line, words, sems.at[0]))
        started.append(start_copy(factor, factor_buf, sems.at[2]))

    total = map_blocks(operands, refs[18:], meanwhile)
    words_copy, factor_copy = started
    factor_copy.wait()
    tilted_buf[...] = (factor_buf[...] * total).astype(jnp.bfloat16)
    copies = [start_copy(tilted_buf, tilted, sems.at[1])]
    words_copy.wait()
    copies += pack_blocks(words, tilted_buf, staged, outgoing, pack_sems)
    squares[...] = jnp.sum(total * total, axis=0)
    for copy in copies:
        copy.wait()


def last_kernel(first_squares, *refs):
    operands, (mapped, sums) = refs[:8], refs[8:10]
    total = map_blocks(operands, refs[10:])
    for row in range(total.shape[0]):
        mapped[:, row * total.shape[2] : (row + 1) * total.shape[2]] = total[row]
    tilts = total.shape[1]
    across = lax.broadcasted_iota(jnp.int32, (tilts, sums.shape[1]), 1)
    tilt = lax.broadcasted_iota(jnp.int32, (tilts, sums.shape[1]), 0)
    first = jnp.sum(first_squares[...], axis=1, keepdims=True)
    both = jnp.where(across == tilt, first, 0.0) + jnp.where(
        across == tilt + tilts, sum_of_squares(total), 0.0
    )
    sums[...] = jnp.broadcast_to(jnp.sum(both, axis=0, keepdims=True), sums.shape)


def end_kernel(states, sums, mapped, iterate, growth, scaled, sems):
    tilts = mapped.shape[0]
    totals = jnp.sum(sums[...], axis=0, keepdims=True)
    across = lax.broadcasted_iota(jnp.int32, (tilts, sums.shape[1]), 1)
    tilt = lax.broadcasted_iota(jnp.int32, (tilts, sums.shape[1]), 0)
    diagonal = lax.broadcasted_iota(jnp.int32, (tilts, tilts), 0) == lax.broadcasted_iota(
        jnp.int32, (tilts, tilts), 1
    )
    product = jnp.ones((tilts, 1), jnp.float32)
    scales = []
    for j in range(ITERS):
        total = jnp.sum(jnp.where(across == tilt + j * tilts, totals, 0.0), axis=1, keepdims=True)
        scales.append(jnp.sqrt(total / product / product / states + 1e-06))
        product = product * scales[-1]
    inverse = 1.0 / product
    width = mapped.shape[1] // END_CHUNKS
    copies = []
    for part in range(END_CHUNKS):
        span = pl.ds(part * width, width)
        scaled[:, span] = mapped[:, span] * inverse
        copies.append(start_copy(scaled.at[:, span], iterate.at[:, span], sems.at[part]))
    for j, scale in enumerate(scales):
        growth[j : j + 1, :] = jnp.sum(
            jnp.where(diagonal, jnp.log(scale), 0.0), axis=0, keepdims=True
        )
    for copy in copies:
        copy.wait()


def call(kernel, outs, arrays, scratch, flops, limit, in_vmem=()):
    spec = [pl.BlockSpec(memory_space=pltpu.VMEM), pl.BlockSpec(memory_space=pl.ANY)]
    moved = sum(math.prod(a.shape) * a.dtype.itemsize for a in (*arrays, *outs))
    return pl.pallas_call(
        kernel,
        out_shape=outs,
        in_specs=[spec[n not in in_vmem] for n in range(len(arrays))],
        out_specs=[spec[len(arrays) + n not in in_vmem] for n in range(len(outs))],
        scratch_shapes=scratch,
        compiler_params=pltpu.CompilerParams(vmem_limit_bytes=limit),
        cost_estimate=pl.CostEstimate(flops=flops, bytes_accessed=moved, transcendentals=0),
    )(*arrays)


def on_device(start, reward, theta, kernels, rates, pattern):
    tilt_count = start.shape[0]
    blocks_here, slot_count = pattern.shape
    kind_count, block_size = kernels.shape[:2]
    peer_count = lax.axis_size("rows")
    position = lax.axis_index("rows")
    total_blocks = blocks_here * peer_count
    far_count = slot_count - NEAR
    half_span = blocks_here // 2
    capacity = 2
    shape = jax.ShapeDtypeStruct
    sem = pltpu.SemaphoreType.DMA

    pattern_by_slot = pattern.T
    (codes,) = call(
        lambda *refs: request_kernel(blocks_here, *refs),
        [shape((peer_count, 1), jnp.int32)],
        [pattern_by_slot],
        [],
        0,
        REQUEST_LIMIT,
        in_vmem=(0, 1),
    )
    codes = lax.all_to_all(codes, "rows", split_axis=0, concat_axis=0, tiled=True)

    far_cols = pattern[:, NEAR:].reshape(-1)
    owners = lax.div(far_cols, blocks_here)
    smaller = (owners[:, None] == owners[None, :]) & (far_cols[None, :] < far_cols[:, None])
    far_index = owners * capacity + jnp.any(smaller, axis=1).astype(jnp.int32)
    local_rows = jnp.arange(blocks_here, dtype=jnp.int32)
    global_rows = position * blocks_here + local_rows
    shifts = (pattern[:, :NEAR] - global_rows[:, None] + half_span) % total_blocks - half_span
    reached = local_rows[:, None] + shifts
    reached = jnp.where(reached < 0, reached + blocks_here + half_span, reached)

    odd = position % 2
    early_first = half_span * (1 - odd)

    def half_index(start_row):
        entries = lax.dynamic_slice(reached, (start_row, 0), (half_span, NEAR)).reshape(-1)
        return jnp.concatenate([entries, start_row[None]])

    early_index = half_index(early_first)
    late_index = half_index(half_span - early_first)
    on_chip = [(i, i + 1 - 2 * (i % 2)) for i in range(peer_count)]
    off_chip = [(i, (i - 1 + 2 * (i % 2)) % peer_count) for i in range(peer_count)]
    rates_by_slot = rates.transpose(1, 0, 2)
    reward = reward.reshape(blocks_here, block_size)

    block = (tilt_count, block_size)
    tilted_shape = shape((blocks_here, *block), jnp.bfloat16)
    outgoing_shape = shape((peer_count * capacity, *block), jnp.bfloat16)
    squares_shape = shape(block, jnp.float32)
    sums_shape = shape((peer_count, ITERS * tilt_count), jnp.float32)
    mapped_shape = shape(start.shape, jnp.float32)
    word_buffers = [pltpu.VMEM((1, peer_count), jnp.int32), pltpu.SMEM((1, peer_count), jnp.int32)]
    staged = pltpu.VMEM(outgoing_shape.shape, jnp.bfloat16)
    early_shape = shape((half_span, *block), jnp.float32)
    reach = pltpu.VMEM((blocks_here + half_span, *block), jnp.bfloat16)
    near_rows = NEAR // kind_count * half_span * tilt_count
    far_rows = far_count // kind_count * blocks_here * tilt_count
    gathered = pltpu.VMEM((2, max(near_rows, far_rows), block_size), jnp.bfloat16)
    early_scratch = [
        pltpu.SMEM(early_index.shape, jnp.int32),
        reach,
        pltpu.VMEM(early_shape.shape, jnp.float32),
        gathered,
        sem((4,)),
    ]
    map_scratch = [
        pltpu.SMEM(late_index.shape, jnp.int32),
        pltpu.SMEM(far_index.shape, jnp.int32),
        reach,
        staged,
        pltpu.VMEM(early_shape.shape, jnp.float32),
        gathered,
        sem((6,)),
    ]
    slot_flops = 2 * blocks_here * tilt_count * block_size * block_size
    early_flops = NEAR * slot_flops // 2
    map_flops = slot_count * slot_flops - early_flops

    factor = jnp.exp(theta[None, :, None] * reward[:, None, :])
    tilted = factor * start.reshape(tilt_count, blocks_here, block_size).transpose(1, 0, 2)
    tilted = tilted.astype(jnp.bfloat16)
    (outgoing,) = call(
        pack_kernel,
        [pltpu.HBM(outgoing_shape.shape, outgoing_shape.dtype)],
        [codes, tilted],
        [*word_buffers, staged, sem, sem((PACK_CHUNKS,))],
        0,
        PACK_LIMIT,
        in_vmem=(0, 1),
    )
    for iteration in range(ITERS):
        arrived = lax.all_to_all(outgoing, "rows", split_axis=0, concat_axis=0, tiled=True)
        head, tail = tilted[:half_span], tilted[blocks_here - half_span :]
        near_halo = lax.ppermute(jnp.where(odd, head, tail), "rows", on_chip)
        far_halo = lax.ppermute(jnp.where(odd, tail, head), "rows", off_chip)
        arrived = pltpu.with_memory_space_constraint(arrived, pltpu.HBM)
        if iteration < ITERS - 1:
            factor_hbm = pltpu.with_memory_space_constraint(factor, pltpu.HBM)
        (early,) = call(
            early_kernel,
            [pltpu.HBM(early_shape.shape, early_shape.dtype)],
            [early_index, tilted, near_halo, kernels, rates_by_slot],
            early_scratch,
            early_flops,
            MAP_LIMIT,
            in_vmem=(3, 4),
        )
        early = pltpu.with_memory_space_constraint(early, pltpu.HBM)
        operands = [late_index, far_index, far_halo, tilted, early, arrived, kernels, rates_by_slot]
        if iteration < ITERS - 1:
            step_scratch = [
                *word_buffers,
                pltpu.VMEM(tilted_shape.shape, jnp.float32),
                pltpu.VMEM(tilted_shape.shape, jnp.bfloat16),
                staged,
                sem((PACK_CHUNKS,)),
                sem((3,)),
            ]
            tilted, outgoing, squares = call(
                step_kernel,
                [tilted_shape, pltpu.HBM(outgoing_shape.shape, outgoing_shape.dtype), squares_shape],
                [codes, factor_hbm, *operands],
                step_scratch + map_scratch,
                map_flops,
                MAP_LIMIT,
                in_vmem=(0, 8, 9, 12),
            )
        else:
            mapped, sums = call(
                last_kernel,
                [mapped_shape, sums_shape],
                [squares, *operands],
                map_scratch,
                map_flops,
                MAP_LIMIT,
                in_vmem=(0, 7, 8, 9, 10),
            )

    gathered = lax.all_to_all(sums, "rows", split_axis=0, concat_axis=0, tiled=True)
    states = total_blocks * block_size
    return call(
        lambda *refs: end_kernel(states, *refs),
        [mapped_shape, shape((ITERS, tilt_count), jnp.float32)],
        [gathered, mapped],
        [pltpu.VMEM(start.shape, jnp.float32), sem((END_CHUNKS,))],
        0,
        MAP_LIMIT,
        in_vmem=(0, 1, 3),
    )


def solution(mesh):
    placed = (P("tilt", "rows"), P("rows"), P("tilt"), P(), P("rows", None, None), P("rows", None))
    return jax.shard_map(
        on_device,
        mesh=mesh,
        in_specs=placed,
        out_specs=(P("tilt", "rows"), P(None, "tilt")),
        check_vma=False,
    )
```

```python
import math

import jax
import jax.numpy as jnp
from jax import lax
from jax.experimental import pallas as pl
from jax.experimental.pallas import tpu as pltpu
from jax.sharding import PartitionSpec as P

NEAR = 8
ITERS = 2
PACK_CHUNKS = 4
END_CHUNKS = 4
HALF_WORD = 1 << 16
REQUEST_LIMIT = 62 * 1024 * 1024
PACK_LIMIT = 48 * 1024 * 1024
MAP_LIMIT = 44 * 1024 * 1024


def request_kernel(blocks_here, pattern, codes):
    peers = codes.shape[0]
    slots, rows = pattern.shape
    base = lax.broadcasted_iota(jnp.int32, (peers, rows), 0) * blocks_here
    low = jnp.full((peers, rows), blocks_here, jnp.int32)
    high = jnp.full((peers, rows), -1, jnp.int32)
    for slot in range(NEAR, slots):
        within = pattern[slot : slot + 1, :] - base
        named = (within >= 0) & (within < blocks_here)
        low = jnp.minimum(low, jnp.where(named, within, blocks_here))
        high = jnp.maximum(high, jnp.where(named, within, -1))
    low = jnp.min(low, axis=1, keepdims=True)
    high = jnp.max(high, axis=1, keepdims=True)
    codes[...] = jnp.where(high >= 0, high * HALF_WORD + low, 0)


def start_copy(src, dst, sem):
    copy = pltpu.make_async_copy(src, dst, sem)
    copy.start()
    return copy


def read_words(codes, line, words, sem):
    peers = codes.shape[0]
    across = lax.broadcasted_iota(jnp.int32, (peers, peers), 1)
    same = lax.broadcasted_iota(jnp.int32, (peers, peers), 0) == across
    line[...] = jnp.sum(jnp.where(same, codes[...], 0), axis=0, keepdims=True)
    return start_copy(line, words, sem)


def pack_blocks(words, tilted, staged, outgoing, sems):
    chunk = outgoing.shape[0] // PACK_CHUNKS
    copies = []
    for part in range(PACK_CHUNKS):

        def body(j, carry, part=part):
            word = words[0, part * (chunk // 2) + j]
            staged[part * chunk + 2 * j] = tilted[word & (HALF_WORD - 1)]
            staged[part * chunk + 2 * j + 1] = tilted[lax.shift_right_logical(word, 16)]
            return carry

        lax.fori_loop(0, chunk // 2, body, 0, unroll=8)
        span = pl.ds(part * chunk, chunk)
        copies.append(start_copy(staged.at[span], outgoing.at[span], sems.at[part]))
    return copies


def pack_kernel(codes, tilted, outgoing, line, words, staged, word_sem, sems):
    read_words(codes, line, words, word_sem).wait()
    for copy in pack_blocks(words, tilted, staged, outgoing, sems):
        copy.wait()


def weighted(index, stride, slots, source, weights, gathered, rows, tilts):
    span = rows * tilts
    for n, slot in enumerate(slots):

        def gather(pair, carry, slot=slot, n=n):
            low = source[index[2 * pair * stride + slot]]
            high = source[index[(2 * pair + 1) * stride + slot]]
            at = pl.multiple_of(n * span + pair * 2 * tilts, 2 * tilts)
            gathered[pl.ds(at, 2 * tilts), :] = jnp.concatenate([low, high], axis=0)
            return carry

        lax.fori_loop(0, rows // 2, gather, 0, unroll=True)
    taken = gathered[: len(slots) * span, :]
    product = jnp.dot(taken, weights, preferred_element_type=jnp.float32)
    return product.reshape(len(slots), rows, tilts, weights.shape[1])


def near_sum(index, source, kernels, rates, gathered, rows):
    kinds, tilts, size = kernels.shape[0], source.shape[1], source.shape[2]
    upper = jnp.full((rows, size), index[rows * NEAR]) > 0
    total = None
    for kind in range(kinds):
        slots = range(kind, NEAR, kinds)
        product = weighted(
            index, NEAR, slots, source, kernels[kind], gathered.at[kind % 2], rows, tilts
        )
        for n, slot in enumerate(slots):
            rate = rates[slot].astype(jnp.float32)
            rate = jnp.where(upper, rate[rows:], rate[:rows])
            term = product[n] * rate[:, None, :]
            total = term if total is None else total + term
    return total


def early_kernel(index, own, halo, kernels, rates, out, *scratch):
    index_smem, extended, out_buf, gathered, sems = scratch
    rows, half = own.shape[0], halo.shape[0]
    copies = [
        start_copy(index, index_smem, sems.at[0]),
        start_copy(own, extended.at[pl.ds(0, rows)], sems.at[1]),
        start_copy(halo, extended.at[pl.ds(rows, half)], sems.at[2]),
    ]
    for copy in copies:
        copy.wait()
    out_buf[...] = near_sum(index_smem, extended, kernels, rates, gathered, half)
    start_copy(out_buf, out, sems.at[3]).wait()


def map_blocks(operands, scratch, meanwhile=None):
    near_index, far_index, halo, own, early, arrived, kernels, rates = operands
    near_smem, far_smem, extended, far_blocks, early_buf, gathered, sems = scratch
    kinds = kernels.shape[0]
    (rows, tilts, size), half = own.shape, halo.shape[0]
    far_count = rates.shape[0] - NEAR

    first = [
        start_copy(near_index, near_smem, sems.at[0]),
        start_copy(own, extended.at[pl.ds(0, rows)], sems.at[1]),
        start_copy(halo, extended.at[pl.ds(rows, half)], sems.at[2]),
    ]
    late = [
        start_copy(far_index, far_smem, sems.at[3]),
        start_copy(early, early_buf, sems.at[4]),
        start_copy(arrived, far_blocks, sems.at[5]),
    ]
    if meanwhile is not None:
        meanwhile()
    for copy in first:
        copy.wait()

    here = near_sum(near_smem, extended, kernels, rates, gathered, half)
    for copy in late:
        copy.wait()
    upper = jnp.full((half, tilts, size), near_smem[half * NEAR]) > 0
    other = early_buf[...]
    total = jnp.concatenate([jnp.where(upper, other, here), jnp.where(upper, here, other)], axis=0)
    for kind in range(kinds):
        slots = range(kind, far_count, kinds)
        product = weighted(
            far_smem, far_count, slots, far_blocks, kernels[kind], gathered.at[kind % 2], rows, tilts
        )
        for n, slot in enumerate(slots):
            total = total + product[n] * rates[NEAR + slot].astype(jnp.float32)[:, None, :]
    return total


def sum_of_squares(total):
    return jnp.sum(jnp.sum(total * total, axis=0), axis=1, keepdims=True)


def step_kernel(codes, factor, *refs):
    operands, (tilted, outgoing, squares) = refs[:8], refs[8:11]
    line, words, factor_buf, tilted_buf, staged, pack_sems, sems = refs[11:18]
    started = []

    def meanwhile():
        started.append(read_words(codes, line, words, sems.at[0]))
        started.append(start_copy(factor, factor_buf, sems.at[2]))

    total = map_blocks(operands, refs[18:], meanwhile)
    words_copy, factor_copy = started
    factor_copy.wait()
    tilted_buf[...] = (factor_buf[...] * total).astype(jnp.bfloat16)
    copies = [start_copy(tilted_buf, tilted, sems.at[1])]
    words_copy.wait()
    copies += pack_blocks(words, tilted_buf, staged, outgoing, pack_sems)
    squares[...] = jnp.sum(total * total, axis=0)
    for copy in copies:
        copy.wait()


def last_kernel(first_squares, *refs):
    operands, (mapped, sums) = refs[:8], refs[8:10]
    total = map_blocks(operands, refs[10:])
    for row in range(total.shape[0]):
        mapped[:, row * total.shape[2] : (row + 1) * total.shape[2]] = total[row]
    tilts = total.shape[1]
    across = lax.broadcasted_iota(jnp.int32, (tilts, sums.shape[1]), 1)
    tilt = lax.broadcasted_iota(jnp.int32, (tilts, sums.shape[1]), 0)
    first = jnp.sum(first_squares[...], axis=1, keepdims=True)
    both = jnp.where(across == tilt, first, 0.0) + jnp.where(
        across == tilt + tilts, sum_of_squares(total), 0.0
    )
    sums[...] = jnp.broadcast_to(jnp.sum(both, axis=0, keepdims=True), sums.shape)


def end_kernel(states, sums, mapped, iterate, growth, scaled, sems):
    tilts = mapped.shape[0]
    totals = jnp.sum(sums[...], axis=0, keepdims=True)
    across = lax.broadcasted_iota(jnp.int32, (tilts, sums.shape[1]), 1)
    tilt = lax.broadcasted_iota(jnp.int32, (tilts, sums.shape[1]), 0)
    diagonal = lax.broadcasted_iota(jnp.int32, (tilts, tilts), 0) == lax.broadcasted_iota(
        jnp.int32, (tilts, tilts), 1
    )
    product = jnp.ones((tilts, 1), jnp.float32)
    scales = []
    for j in range(ITERS):
        total = jnp.sum(jnp.where(across == tilt + j * tilts, totals, 0.0), axis=1, keepdims=True)
        scales.append(jnp.sqrt(total / product / product / states + 1e-06))
        product = product * scales[-1]
    inverse = 1.0 / product
    width = mapped.shape[1] // END_CHUNKS
    copies = []
    for part in range(END_CHUNKS):
        span = pl.ds(part * width, width)
        scaled[:, span] = mapped[:, span] * inverse
        copies.append(start_copy(scaled.at[:, span], iterate.at[:, span], sems.at[part]))
    for j, scale in enumerate(scales):
        growth[j : j + 1, :] = jnp.sum(
            jnp.where(diagonal, jnp.log(scale), 0.0), axis=0, keepdims=True
        )
    for copy in copies:
        copy.wait()


def call(kernel, outs, arrays, scratch, flops, limit, in_vmem=()):
    spec = [pl.BlockSpec(memory_space=pltpu.VMEM), pl.BlockSpec(memory_space=pl.ANY)]
    moved = sum(math.prod(a.shape) * a.dtype.itemsize for a in (*arrays, *outs))
    return pl.pallas_call(
        kernel,
        out_shape=outs,
        in_specs=[spec[n not in in_vmem] for n in range(len(arrays))],
        out_specs=[spec[len(arrays) + n not in in_vmem] for n in range(len(outs))],
        scratch_shapes=scratch,
        compiler_params=pltpu.CompilerParams(vmem_limit_bytes=limit),
        cost_estimate=pl.CostEstimate(flops=flops, bytes_accessed=moved, transcendentals=0),
    )(*arrays)


def on_device(start, reward, theta, kernels, rates, pattern):
    tilt_count = start.shape[0]
    blocks_here, slot_count = pattern.shape
    kind_count, block_size = kernels.shape[:2]
    peer_count = lax.axis_size("rows")
    position = lax.axis_index("rows")
    total_blocks = blocks_here * peer_count
    far_count = slot_count - NEAR
    half_span = blocks_here // 2
    capacity = 2
    shape = jax.ShapeDtypeStruct
    sem = pltpu.SemaphoreType.DMA

    pattern_by_slot = pattern.T
    (codes,) = call(
        lambda *refs: request_kernel(blocks_here, *refs),
        [shape((peer_count, 1), jnp.int32)],
        [pattern_by_slot],
        [],
        0,
        REQUEST_LIMIT,
        in_vmem=(0, 1),
    )
    codes = lax.all_to_all(codes, "rows", split_axis=0, concat_axis=0, tiled=True)

    far_cols = pattern[:, NEAR:].reshape(-1)
    owners = lax.div(far_cols, blocks_here)
    smaller = (owners[:, None] == owners[None, :]) & (far_cols[None, :] < far_cols[:, None])
    far_index = owners * capacity + jnp.any(smaller, axis=1).astype(jnp.int32)
    local_rows = jnp.arange(blocks_here, dtype=jnp.int32)
    global_rows = position * blocks_here + local_rows
    shifts = (pattern[:, :NEAR] - global_rows[:, None] + half_span) % total_blocks - half_span
    reached = local_rows[:, None] + shifts
    reached = jnp.where(reached < 0, reached + blocks_here + half_span, reached)

    odd = position % 2
    early_first = half_span * (1 - odd)

    def half_index(start_row):
        entries = lax.dynamic_slice(reached, (start_row, 0), (half_span, NEAR)).reshape(-1)
        return jnp.concatenate([entries, start_row[None]])

    early_index = half_index(early_first)
    late_index = half_index(half_span - early_first)
    on_chip = [(i, i + 1 - 2 * (i % 2)) for i in range(peer_count)]
    off_chip = [(i, (i - 1 + 2 * (i % 2)) % peer_count) for i in range(peer_count)]
    rates_by_slot = rates.transpose(1, 0, 2)
    reward = reward.reshape(blocks_here, block_size)

    block = (tilt_count, block_size)
    tilted_shape = shape((blocks_here, *block), jnp.bfloat16)
    outgoing_shape = shape((peer_count * capacity, *block), jnp.bfloat16)
    squares_shape = shape(block, jnp.float32)
    sums_shape = shape((peer_count, ITERS * tilt_count), jnp.float32)
    mapped_shape = shape(start.shape, jnp.float32)
    word_buffers = [pltpu.VMEM((1, peer_count), jnp.int32), pltpu.SMEM((1, peer_count), jnp.int32)]
    staged = pltpu.VMEM(outgoing_shape.shape, jnp.bfloat16)
    early_shape = shape((half_span, *block), jnp.float32)
    reach = pltpu.VMEM((blocks_here + half_span, *block), jnp.bfloat16)
    near_rows = NEAR // kind_count * half_span * tilt_count
    far_rows = far_count // kind_count * blocks_here * tilt_count
    gathered = pltpu.VMEM((2, max(near_rows, far_rows), block_size), jnp.bfloat16)
    early_scratch = [
        pltpu.SMEM(early_index.shape, jnp.int32),
        reach,
        pltpu.VMEM(early_shape.shape, jnp.float32),
        gathered,
        sem((4,)),
    ]
    map_scratch = [
        pltpu.SMEM(late_index.shape, jnp.int32),
        pltpu.SMEM(far_index.shape, jnp.int32),
        reach,
        staged,
        pltpu.VMEM(early_shape.shape, jnp.float32),
        gathered,
        sem((6,)),
    ]
    slot_flops = 2 * blocks_here * tilt_count * block_size * block_size
    early_flops = NEAR * slot_flops // 2
    map_flops = slot_count * slot_flops - early_flops

    factor = jnp.exp(theta[None, :, None] * reward[:, None, :])
    tilted = factor * start.reshape(tilt_count, blocks_here, block_size).transpose(1, 0, 2)
    tilted = tilted.astype(jnp.bfloat16)
    (outgoing,) = call(
        pack_kernel,
        [pltpu.HBM(outgoing_shape.shape, outgoing_shape.dtype)],
        [codes, tilted],
        [*word_buffers, staged, sem, sem((PACK_CHUNKS,))],
        0,
        PACK_LIMIT,
        in_vmem=(0, 1),
    )
    for iteration in range(ITERS):
        arrived = lax.all_to_all(outgoing, "rows", split_axis=0, concat_axis=0, tiled=True)
        head, tail = tilted[:half_span], tilted[blocks_here - half_span :]
        near_halo = lax.ppermute(jnp.where(odd, head, tail), "rows", on_chip)
        far_halo = lax.ppermute(jnp.where(odd, tail, head), "rows", off_chip)
        arrived = pltpu.with_memory_space_constraint(arrived, pltpu.HBM)
        if iteration < ITERS - 1:
            factor_hbm = pltpu.with_memory_space_constraint(factor, pltpu.HBM)
        (early,) = call(
            early_kernel,
            [pltpu.HBM(early_shape.shape, early_shape.dtype)],
            [early_index, tilted, near_halo, kernels, rates_by_slot],
            early_scratch,
            early_flops,
            MAP_LIMIT,
            in_vmem=(3, 4),
        )
        early = pltpu.with_memory_space_constraint(early, pltpu.HBM)
        operands = [late_index, far_index, far_halo, tilted, early, arrived, kernels, rates_by_slot]
        if iteration < ITERS - 1:
            step_scratch = [
                *word_buffers,
                pltpu.VMEM(tilted_shape.shape, jnp.float32),
                pltpu.VMEM(tilted_shape.shape, jnp.bfloat16),
                staged,
                sem((PACK_CHUNKS,)),
                sem((3,)),
            ]
            tilted, outgoing, squares = call(
                step_kernel,
                [tilted_shape, pltpu.HBM(outgoing_shape.shape, outgoing_shape.dtype), squares_shape],
                [codes, factor_hbm, *operands],
                step_scratch + map_scratch,
                map_flops,
                MAP_LIMIT,
                in_vmem=(0, 8, 9, 12),
            )
        else:
            mapped, sums = call(
                last_kernel,
                [mapped_shape, sums_shape],
                [squares, *operands],
                map_scratch,
                map_flops,
                MAP_LIMIT,
                in_vmem=(0, 7, 8, 9, 10),
            )

    gathered = lax.all_to_all(sums, "rows", split_axis=0, concat_axis=0, tiled=True)
    states = total_blocks * block_size
    return call(
        lambda *refs: end_kernel(states, *refs),
        [mapped_shape, shape((ITERS, tilt_count), jnp.float32)],
        [gathered, mapped],
        [pltpu.VMEM(start.shape, jnp.float32), sem((END_CHUNKS,))],
        0,
        MAP_LIMIT,
        in_vmem=(0, 1, 3),
    )


def solution(mesh):
    placed = (P("tilt", "rows"), P("rows"), P("tilt"), P(), P("rows", None, None), P("rows", None))
    return jax.shard_map(
        on_device,
        mesh=mesh,
        in_specs=placed,
        out_specs=(P("tilt", "rows"), P(None, "tilt")),
        check_vma=False,
    )
```
